32 devices in a mesh: dp: 16 (over z, y, core), fsdp: 2 (over x).
Axes of the slice: x: 2, y: 2, z: 4, core: 2. Of those that a mesh axis runs over, the one named last changes fastest.
Arguments:
- states: float32 [2, 4096, 1536], P('fsdp', 'dp'), may hold values from -50 to 50
- cotangent: float32 [2, 4096, 1536], P('fsdp', 'dp'), may hold values from -6 to 6
- segment_ids: int32 [2, 4096], P('fsdp'), may hold values from -1 to 1, as said below
- frame_ids: int32 [2, 4096], P('fsdp', 'dp'), may hold values from 0 to 15, as said below
- condition: float32 [2, 2, 1536], P('fsdp'), may hold values from -6 to 6
- context: bfloat16 [2, 512, 4096], P('fsdp', 'dp'), may hold values from -6 to 6
- w_modulate: bfloat16 [1536, 6144], P('fsdp'), may hold values from -0.15625 to 0.15625
- w_qkv: bfloat16 [1536, 4608], P('fsdp'), may hold values from -0.15625 to 0.15625
- w_text_kv: bfloat16 [4096, 3072], P('fsdp'), may hold values from -0.09375 to 0.09375
- w_out: bfloat16 [1536, 1536], P('fsdp'), may hold values from -0.15625 to 0.15625
- w_gate_up: bfloat16 [2, 1536, 4096], P(None, None, 'fsdp'), may hold values from -0.15625 to 0.15625
- w_down: bfloat16 [4096, 1536], P('fsdp'), may hold values from -0.09375 to 0.09375
- gain_attn_in: float32 [1536], replicated, may hold values from 0.1 to 1.9
- gain_attn_out: float32 [1536], replicated, may hold values from 0.1 to 1.9
- gain_ffn_in: float32 [1536], replicated, may hold values from 0.1 to 1.9
- gain_ffn_out: float32 [1536], replicated, may hold values from 0.1 to 1.9
- gain_query: float32 [64], replicated, may hold values from 0.1 to 1.9
- gain_key: float32 [64], replicated, may hold values from 0.1 to 1.9
- gain_text_key: float32 [64], replicated, may hold values from 0.1 to 1.9
- cross_gate: float32 [24], replicated, may hold values from -1.5 to 1.5
Outputs:
- output: float32 [2, 4096, 1536], P('fsdp', 'dp')
- grad_states: float32 [2, 4096, 1536], P('fsdp', 'dp')
- grad_w_modulate: float32 [1536, 6144], P('fsdp', 'dp')
- grad_w_qkv: float32 [1536, 4608], P('fsdp', 'dp')
- grad_w_text_kv: float32 [4096, 3072], P('fsdp', 'dp')
- grad_w_out: float32 [1536, 1536], P('fsdp', 'dp')
- grad_w_gate_up: float32 [2, 1536, 4096], P(None, 'dp', 'fsdp')
- grad_w_down: float32 [4096, 1536], P('fsdp', 'dp')
- grad_gain_attn_in: float32 [1536], replicated
- grad_gain_attn_out: float32 [1536], replicated
- grad_gain_ffn_in: float32 [1536], replicated
- grad_gain_ffn_out: float32 [1536], replicated
- grad_gain_query: float32 [64], replicated
- grad_gain_key: float32 [64], replicated
- grad_gain_text_key: float32 [64], replicated
- grad_cross_gate: float32 [24], replicated
The draws below stay inside these ranges and needn't reach their ends.
Inputs may be any that keep to these rules, and one draw needn't show every extreme that they name: `segment_ids`: each stream has 2 clips; clip c covers between 4 and 16 whole frames of 128 tokens that start at multiples of 128, clip 0 exactly 16, with one of its frames first and one last in the stream; -1 marks padding frames. `frame_ids`: the frames of a clip carry the numbers 0 up to its frame count minus one, one frame each, in any order along the stream; padding carries 0.
All inputs are finite; a program needn't handle non-finite values.
Results may differ from the reference program's by a relative error of at most 0.025.
Values may be sent and summed in bfloat16 or wider, within the bound.
No kernel may reach another device: no remote copies, remote signals or barrier semaphores. Data moves between devices by JAX's collectives and lax.ppermute only.
A program may use at most 448 MiB of HBM per device.

```python
import math
import jax
import jax.numpy as jnp
from jax import lax

D = 1536
HEADS = 24
HD = 64
FF = 4096
CDIM = 4096
CTX = 256
FRAME_TOK = 128
PW = 16
MAXF = 16
MINF = 4
STREAMS = 2
LEN = 4096
CLIPS = 2
TEXT_ROWS = 512


def stream_layout(key):
    unit_count = LEN // FRAME_TOK
    frames = jax.random.randint(jax.random.fold_in(key, 1), (CLIPS,), MINF, MAXF + 1).astype(jnp.int32)
    frames = frames.at[0].set(MAXF)
    clip_ends = jnp.cumsum(frames).astype(jnp.int32)
    clip_starts = clip_ends - frames
    canonical = jnp.arange(unit_count).astype(jnp.int32)
    clip_number = jnp.sum((canonical[:, None] >= clip_ends[None, :]).astype(jnp.int32), axis=1)
    live = clip_number < CLIPS
    safe_clip = jnp.minimum(clip_number, CLIPS - 1)
    frame_number = canonical - clip_starts[safe_clip]
    unit_seg = jnp.where(live, clip_number, -1).astype(jnp.int32)
    unit_frame = jnp.where(live, frame_number, 0).astype(jnp.int32)
    others = jnp.concatenate([jnp.arange(1, MAXF - 1), jnp.arange(MAXF, unit_count)]).astype(jnp.int32)
    shuffled = jax.random.permutation(jax.random.fold_in(key, 2), others)
    order = jnp.concatenate([jnp.zeros((1,), jnp.int32), shuffled.astype(jnp.int32), jnp.full((1,), MAXF - 1, jnp.int32)])
    seg_tokens = jnp.repeat(unit_seg[order], FRAME_TOK)
    frame_tokens = jnp.repeat(unit_frame[order], FRAME_TOK)
    return (seg_tokens.astype(jnp.int32), frame_tokens.astype(jnp.int32))


def all_layouts(key):
    base = jax.random.fold_in(key, 77)

    def one_stream(stream_index):
        return stream_layout(jax.random.fold_in(base, stream_index))
    return jax.vmap(one_stream)(jnp.arange(STREAMS))


def draw_segment_ids(key, part):
    return all_layouts(key)[0]


def draw_frame_ids(key, part):
    return all_layouts(key)[1]


def draw_states(key, part):
    shape = (STREAMS, LEN, D)
    row_level = jax.random.uniform(jax.random.fold_in(key, 12), (STREAMS, LEN, 1), jnp.float32, 0.0, 1.0)
    col_level = jax.random.uniform(jax.random.fold_in(key, 13), (1, 1, D), jnp.float32, -0.4, 0.4)
    base = jnp.clip(jax.random.normal(jax.random.fold_in(key, 11), shape, jnp.float32), -6.0, 6.0)
    return base * 0.5 * jnp.exp(row_level * math.log(10.0)) * jnp.exp(col_level)


def shard_levels(stream_key, extent, shards, low, top_value):
    level = 1.0
    for position, blocks in shards:
        heights = jax.random.uniform(jax.random.fold_in(jax.random.fold_in(stream_key, 6), position), (blocks,), jnp.float32, low / len(shards), top_value / len(shards))
        level = level * jnp.repeat(jnp.exp(heights), extent[position] // blocks).reshape((-1,) + (1,) * (len(extent) - 1 - position))
    return level


def scatter_about(stream_key, shape, width, limit, shards=(), held_as=jnp.bfloat16):
    level = shard_levels(stream_key, shape, shards, -0.22, 0.18) if shards else 1.0
    entries = jax.random.normal(stream_key, shape, jnp.float32) * width * level
    return jnp.minimum(jnp.maximum(entries, -limit), limit).astype(held_as)


def setup_inputs(seed: int = 0) -> dict:
    seeds = jax.random.split(jax.random.key(seed), 21)
    states = draw_states(jax.random.fold_in(seeds[20], 71), 0)
    cotangent = scatter_about(seeds[1], (STREAMS, LEN, D), 1.0, 6.0, ((0, 2), (1, 16)), jnp.float32)
    segment_ids = draw_segment_ids(jax.random.fold_in(seeds[20], 71), 0)
    frame_ids = draw_frame_ids(jax.random.fold_in(seeds[20], 71), 0)
    condition = scatter_about(seeds[4], (STREAMS, CLIPS, D), 1.0, 6.0, ((0, 2),), jnp.float32)
    context = scatter_about(seeds[5], (STREAMS, TEXT_ROWS, CDIM), 1.0, 6.0, ((0, 2), (1, 16)))
    w_modulate = scatter_about(seeds[6], (D, 4 * D), D ** -0.5, 0.15625, ((0, 2),))
    w_qkv = scatter_about(seeds[7], (D, 3 * D), D ** -0.5, 0.15625, ((0, 2),))
    w_text_kv = scatter_about(seeds[8], (CDIM, 2 * D), CDIM ** -0.5, 0.09375, ((0, 2),))
    w_out = scatter_about(seeds[9], (D, D), D ** -0.5, 0.15625, ((0, 2),))
    w_gate_up = scatter_about(seeds[10], (2, D, FF), D ** -0.5, 0.15625, ((2, 2),))
    w_down = scatter_about(seeds[11], (FF, D), FF ** -0.5, 0.09375, ((0, 2),))
    gain_attn_in = jnp.clip(1.0 + 0.18 * jax.random.normal(seeds[12], (D,), jnp.float32), 0.1, 1.9)
    gain_attn_out = jnp.clip(1.0 + 0.18 * jax.random.normal(seeds[13], (D,), jnp.float32), 0.1, 1.9)
    gain_ffn_in = jnp.clip(1.0 + 0.18 * jax.random.normal(seeds[14], (D,), jnp.float32), 0.1, 1.9)
    gain_ffn_out = jnp.clip(1.0 + 0.18 * jax.random.normal(seeds[15], (D,), jnp.float32), 0.1, 1.9)
    gain_query = jnp.clip(1.0 + 0.18 * jax.random.normal(seeds[16], (HD,), jnp.float32), 0.1, 1.9)
    gain_key = jnp.clip(1.0 + 0.18 * jax.random.normal(seeds[17], (HD,), jnp.float32), 0.1, 1.9)
    gain_text_key = jnp.clip(1.0 + 0.18 * jax.random.normal(seeds[18], (HD,), jnp.float32), 0.1, 1.9)
    cross_gate = jnp.clip(jax.random.uniform(seeds[19], (HEADS,), jnp.float32, -1.5, 1.5), -1.5, 1.5)
    return dict(states=states, cotangent=cotangent, segment_ids=segment_ids, frame_ids=frame_ids, condition=condition, context=context, w_modulate=w_modulate, w_qkv=w_qkv, w_text_kv=w_text_kv, w_out=w_out, w_gate_up=w_gate_up, w_down=w_down, gain_attn_in=gain_attn_in, gain_attn_out=gain_attn_out, gain_ffn_in=gain_ffn_in, gain_ffn_out=gain_ffn_out, gain_query=gain_query, gain_key=gain_key, gain_text_key=gain_text_key, cross_gate=cross_gate)


EPSILON = 1e-06
HIGHEST = lax.Precision.HIGHEST
NEG_LARGE = -1e+30

@jax.custom_vjp
def low(v):
    return lax.optimization_barrier(v.astype(jnp.bfloat16)).astype(jnp.float32)

@jax.custom_vjp
def low_back(v):
    return v

def low_keep(v):
    return (low(v), None)

def low_pass(kept, grad):
    return (grad,)

def back_keep(v):
    return (v, None)

def back_low(kept, grad):
    return (low(grad),)
low.defvjp(low_keep, low_pass)
low_back.defvjp(back_keep, back_low)

def rms_norm(values, gain):
    return values * lax.rsqrt(lax.optimization_barrier(jnp.mean(values * values, axis=-1, keepdims=True)) + EPSILON) * gain

def frequencies(count):
    return 10000.0 ** (-jnp.arange(count, dtype=jnp.float32) / count)

def rope_tables(frames_row, first_row, row_count):
    place = first_row + jnp.arange(row_count)
    inner = place % FRAME_TOK
    row_pos = (inner // PW).astype(jnp.float32)
    col_pos = (inner % PW).astype(jnp.float32)
    frame_pos = frames_row.astype(jnp.float32)
    half_pairs = HD // 2
    frame_pairs = HD // 8
    row_pairs = (half_pairs - frame_pairs) // 2
    col_pairs = half_pairs - frame_pairs - row_pairs
    angles = jnp.concatenate([frame_pos[:, None] * frequencies(frame_pairs)[None, :], row_pos[:, None] * frequencies(row_pairs)[None, :], col_pos[:, None] * frequencies(col_pairs)[None, :]], axis=1)
    return (jnp.cos(angles), jnp.sin(angles))

def rotate(values, cosine, sine):
    pairs = values.reshape(values.shape[0], values.shape[1], -1, 2)
    first_part = pairs[..., 0]
    second_part = pairs[..., 1]
    cos_heads = cosine[:, None, :]
    sin_heads = sine[:, None, :]
    turned = jnp.stack([first_part * cos_heads - second_part * sin_heads, first_part * sin_heads + second_part * cos_heads], axis=-1)
    return turned.reshape(values.shape)

def stream_forward(params, states, segments, frames, condition, context):
    w_modulate, w_qkv, w_text_kv, w_out, w_gate_up, w_down, gain_attn_in, gain_attn_out, gain_ffn_in, gain_ffn_out, gain_query, gain_key, gain_text_key, cross_gate = params
    length = states.shape[0]
    clip_count = condition.shape[0]
    head_count = cross_gate.shape[0]
    text_count = context.shape[0]
    score_scale = HD ** (-0.5)
    silu_cond = low(jax.nn.silu(condition))
    modulation = jnp.dot(silu_cond, w_modulate, precision=HIGHEST)
    onehot = (segments[:, None] == jnp.arange(clip_count)[None, :]).astype(jnp.float32)
    per_token = jnp.dot(onehot, modulation, precision=HIGHEST)
    scale_attn, gate_attn, scale_ffn, gate_ffn = jnp.split(per_token, 4, axis=1)
    normed = low(rms_norm(states, gain_attn_in) * (1.0 + scale_attn))
    projected = low_back(jnp.dot(normed, w_qkv, precision=HIGHEST))
    query_raw, key_raw, value_raw = jnp.split(projected, 3, axis=1)
    cosine, sine = rope_tables(frames, 0, length)
    query = low(rotate(rms_norm(query_raw.reshape(length, head_count, HD), gain_query), cosine, sine))
    key = low(rotate(rms_norm(key_raw.reshape(length, head_count, HD), gain_key), cosine, sine))
    value = low(value_raw.reshape(length, head_count, HD))
    text_proj = low_back(jnp.dot(context, w_text_kv, precision=HIGHEST))
    text_key = low(rms_norm(text_proj[:, :D].reshape(text_count, head_count, HD), gain_text_key))
    text_value = low(text_proj[:, D:].reshape(text_count, head_count, HD))
    clip_of = jnp.maximum(segments, 0)
    text_clip = jnp.arange(text_count) // CTX
    block_rows = math.gcd(length, 512)
    gate_heads = jnp.tanh(cross_gate)[None, :, None]

    def attend_block(block_index):
        rows_query = lax.dynamic_slice_in_dim(query, block_index * block_rows, block_rows)
        rows_seg = lax.dynamic_slice_in_dim(segments, block_index * block_rows, block_rows)
        rows_clip = lax.dynamic_slice_in_dim(clip_of, block_index * block_rows, block_rows)
        scores = low_back(jnp.einsum('qhd,khd->hqk', rows_query, key, precision=HIGHEST) * score_scale)
        scores = jnp.where((rows_seg[:, None] == segments[None, :])[None], scores, NEG_LARGE)
        attn = jax.nn.softmax(scores, axis=-1)
        self_out = low_back(jnp.einsum('hqk,khd->qhd', attn, value, precision=HIGHEST))
        text_scores = low_back(jnp.einsum('qhd,khd->hqk', rows_query, text_key, precision=HIGHEST) * score_scale)
        text_scores = jnp.where((rows_clip[:, None] == text_clip[None, :])[None], text_scores, NEG_LARGE)
        text_attn = jax.nn.softmax(text_scores, axis=-1)
        text_out = low_back(jnp.einsum('hqk,khd->qhd', text_attn, text_value, precision=HIGHEST))
        return self_out + gate_heads * text_out
    mixed = lax.map(jax.checkpoint(attend_block), jnp.arange(length // block_rows))
    mixed = low(mixed.reshape(length, D))
    mixed_out = low_back(jnp.dot(mixed, w_out, precision=HIGHEST))
    after_attn = states + jnp.tanh(gate_attn) * rms_norm(mixed_out, gain_attn_out)
    ffn_in = low(rms_norm(after_attn, gain_ffn_in) * (1.0 + scale_ffn))
    gate_up = low_back(jnp.einsum('ld,cdf->clf', ffn_in, w_gate_up, precision=HIGHEST))
    hidden = low(jax.nn.silu(gate_up[0]) * gate_up[1])
    ffn_out = low_back(jnp.dot(hidden, w_down, precision=HIGHEST))
    return after_attn + jnp.tanh(gate_ffn) * rms_norm(ffn_out, gain_ffn_out)

def reference(states, cotangent, segment_ids, frame_ids, condition, context, w_modulate, w_qkv, w_text_kv, w_out, w_gate_up, w_down, gain_attn_in, gain_attn_out, gain_ffn_in, gain_ffn_out, gain_query, gain_key, gain_text_key, cross_gate):
    params = (w_modulate.astype(jnp.float32), w_qkv.astype(jnp.float32), w_text_kv.astype(jnp.float32), w_out.astype(jnp.float32), w_gate_up.astype(jnp.float32), w_down.astype(jnp.float32), gain_attn_in, gain_attn_out, gain_ffn_in, gain_ffn_out, gain_query, gain_key, gain_text_key, cross_gate)
    context_wide = context.astype(jnp.float32)

    def forward(inputs, weights):

        def one_stream(packed):
            return stream_forward(weights, packed[0], packed[1], packed[2], packed[3], packed[4])
        return lax.map(one_stream, (inputs, segment_ids, frame_ids, condition, context_wide))
    output, pullback = jax.vjp(forward, states, params)
    grad_states, grads = pullback(cotangent)
    return (output, grad_states, grads[0], grads[1], grads[2], grads[3], grads[4], grads[5], grads[6], grads[7], grads[8], grads[9], grads[10], grads[11], grads[12], grads[13])
```

```python
import functools
import math

import jax
import jax.numpy as jnp
import numpy as np
from jax import lax
from jax.experimental import pallas as pl
from jax.experimental.pallas import tpu as pltpu
from jax.sharding import PartitionSpec as P

HD = 64
CTX = 256
FRAME_TOK = 128
PW = 16
EPSILON = 1e-06
GROUP_HEADS = 3
GROUP_WIDTH = GROUP_HEADS * HD
STACK = GROUP_HEADS * FRAME_TOK
ONES_ROWS = 16
HIGHEST = lax.Precision.HIGHEST
BF16 = jnp.bfloat16
F32 = jnp.float32
SCALE = HD ** (-0.5)
EXP2_SCALE = SCALE * math.log2(math.e)
MIB = 1 << 20


def mxu(a, b, dims=((1,), (0,))):
    return lax.dot_general(a, b, (dims, ((), ())), preferred_element_type=F32)


class Moves:
    def __init__(self, axis, size):
        self.axis = axis
        self.size = size
        self.me = lax.axis_index(axis)

    def swap(self, value, mask):
        return lax.ppermute(value, self.axis, [(i, i ^ mask) for i in range(self.size)])

    def gather(self, value):
        return [value] + [self.swap(value, s) for s in range(1, self.size)]

    def scatter_sum(self, parts):
        total = parts[0].astype(F32)
        for s in range(1, self.size):
            total = total + self.swap(parts[s].astype(BF16), s).astype(F32)
        return total

    def reorder(self, value, axis):
        block = value.shape[axis] // self.size
        return jnp.concatenate(
            [
                lax.dynamic_slice_in_dim(value, (self.me ^ s) * block, block, axis)
                for s in range(self.size)
            ],
            axis,
        )

    def own_block(self, value, axis, s=0):
        block = value.shape[axis] // self.size
        return lax.dynamic_slice_in_dim(value, (self.me ^ s) * block, block, axis)


def lane_tiles(width):
    return -(-width // 128) * 128


def turn(values, cosine, sine):
    lane = lax.broadcasted_iota(jnp.int32, values.shape, 1)
    other = jnp.where(lane % 2 == 0, pltpu.roll(values, 127, 1), pltpu.roll(values, 1, 1))
    return values * cosine + other * sine


def head_sums(values, ones):
    return lax.dot_general(
        values, ones, (((1,), (0,)), ((), ())), precision=HIGHEST, preferred_element_type=F32
    )


def norm_fwd_kernel(raw_ref, cos_ref, sin_ref, gain_ref, ones_ref, out_ref, *, kinds, wide, groups):
    for part, (normed, turned) in enumerate(kinds):
        pieces = []
        for t in range(wide // 128):
            x = raw_ref[:, part * wide + 128 * t : part * wide + 128 * (t + 1)]
            if normed:
                mean = head_sums(x * x, ones_ref[...]) * (1.0 / HD)
                x = x * lax.rsqrt(mean + EPSILON) * gain_ref[part : part + 1, :]
            if turned:
                x = turn(x, cos_ref[...], sin_ref[...])
            pieces.append(x)
        full = jnp.concatenate(pieces, axis=1) if len(pieces) > 1 else pieces[0]
        for g in range(groups):
            out_ref[part, g] = full[:, GROUP_WIDTH * g : GROUP_WIDTH * (g + 1)].astype(BF16)


def norm_bwd_kernel(
    raw_ref, grad_ref, cos_ref, sin_ref, gain_ref, ones_ref, out_ref, dgain_ref, *, kinds, wide, groups
):
    @pl.when(pl.program_id(0) == 0)
    def _():
        dgain_ref[...] = jnp.zeros_like(dgain_ref)

    rows = raw_ref.shape[0]
    for part, (normed, turned) in enumerate(kinds):
        pieces = [grad_ref[part, g].astype(F32) for g in range(groups)]
        if wide > groups * GROUP_WIDTH:
            pieces.append(jnp.zeros((rows, wide - groups * GROUP_WIDTH), F32))
        full = jnp.concatenate(pieces, axis=1) if len(pieces) > 1 else pieces[0]
        total = jnp.zeros((1, 128), F32)
        for t in range(wide // 128):
            dy = full[:, 128 * t : 128 * (t + 1)]
            if turned:
                dy = turn(dy, cos_ref[...], -sin_ref[...])
            if normed:
                x = raw_ref[:, part * wide + 128 * t : part * wide + 128 * (t + 1)]
                mean = head_sums(x * x, ones_ref[...]) * (1.0 / HD)
                inv = lax.rsqrt(mean + EPSILON)
                unit = x * inv
                total = total + jnp.sum(dy * unit, axis=0, keepdims=True)
                dn = dy * gain_ref[part : part + 1, :]
                dy = inv * (dn - unit * (head_sums(dn * unit, ones_ref[...]) * (1.0 / HD)))
            out_ref[:, part * wide + 128 * t : part * wide + 128 * (t + 1)] = dy.astype(BF16)
        if normed:
            dgain_ref[part : part + 1, :] += total


def head_ones():
    lane = np.arange(128) // HD
    return jnp.asarray((lane[:, None] == lane[None, :]).astype(np.float32))


def norm_fwd(raw, cosine, sine, gains, kinds, groups):
    rows = raw.shape[0]
    wide = raw.shape[1] // len(kinds)
    block = min(rows, 128)
    return pl.pallas_call(
        functools.partial(norm_fwd_kernel, kinds=kinds, wide=wide, groups=groups),
        grid=(rows // block,),
        in_specs=[
            pl.BlockSpec((block, raw.shape[1]), lambda i: (i, 0)),
            pl.BlockSpec((block, 128), lambda i: (i, 0)),
            pl.BlockSpec((block, 128), lambda i: (i, 0)),
            pl.BlockSpec((8, 128), lambda i: (0, 0)),
            pl.BlockSpec((128, 128), lambda i: (0, 0)),
        ],
        out_specs=pl.BlockSpec((len(kinds), groups, block, GROUP_WIDTH), lambda i: (0, 0, i, 0)),
        out_shape=jax.ShapeDtypeStruct((len(kinds), groups, rows, GROUP_WIDTH), BF16),
        compiler_params=pltpu.CompilerParams(vmem_limit_bytes=32 * MIB),
        name="head_norm",
    )(raw, cosine, sine, gains, head_ones())


def norm_bwd(raw, grad, cosine, sine, gains, kinds, groups):
    rows = raw.shape[0]
    wide = raw.shape[1] // len(kinds)
    block = min(rows, 128)
    return pl.pallas_call(
        functools.partial(norm_bwd_kernel, kinds=kinds, wide=wide, groups=groups),
        grid=(rows // block,),
        in_specs=[
            pl.BlockSpec((block, raw.shape[1]), lambda i: (i, 0)),
            pl.BlockSpec((len(kinds), groups, block, GROUP_WIDTH), lambda i: (0, 0, i, 0)),
            pl.BlockSpec((block, 128), lambda i: (i, 0)),
            pl.BlockSpec((block, 128), lambda i: (i, 0)),
            pl.BlockSpec((8, 128), lambda i: (0, 0)),
            pl.BlockSpec((128, 128), lambda i: (0, 0)),
        ],
        out_specs=[
            pl.BlockSpec((block, raw.shape[1]), lambda i: (i, 0)),
            pl.BlockSpec((8, 128), lambda i: (0, 0)),
        ],
        out_shape=[
            jax.ShapeDtypeStruct(raw.shape, BF16),
            jax.ShapeDtypeStruct((8, 128), F32),
        ],
        compiler_params=pltpu.CompilerParams(vmem_limit_bytes=32 * MIB),
        name="head_norm_back",
    )(raw, grad, cosine, sine, gains, head_ones())


BIG = 4


def over_tiles(start, count, body):
    big = count // BIG

    def big_step(t, carry):
        body(pl.multiple_of((start + t * BIG) * FRAME_TOK, FRAME_TOK), BIG * FRAME_TOK)
        return carry

    def small_step(t, carry):
        body(pl.multiple_of((start + big * BIG + t) * FRAME_TOK, FRAME_TOK), FRAME_TOK)
        return carry

    lax.fori_loop(0, big, big_step, 0)
    lax.fori_loop(0, count - big * BIG, small_step, 0)


def stacked(values, mask):
    return jnp.concatenate([values] * GROUP_HEADS, axis=0) * mask


def diagonal(values):
    own = [
        values[HD * h : HD * (h + 1), FRAME_TOK * h : FRAME_TOK * (h + 1)]
        for h in range(GROUP_HEADS)
    ]
    return jnp.transpose(jnp.concatenate(own, axis=0))


def head_row(values):
    flipped = jnp.transpose(values)
    return jnp.concatenate(
        [
            jnp.sum(flipped[HD * h : HD * (h + 1), :], axis=0, keepdims=True)
            for h in range(GROUP_HEADS)
        ],
        axis=1,
    )


def attn_fwd_kernel(
    rank_ref,
    start_ref,
    count_ref,
    clip_ref,
    place_ref,
    kv_ref,
    q_ref,
    gate_ref,
    mask_ref,
    mixed_ref,
    self_ref,
    text_ref,
    lse_ref,
    keys,
    values,
    rows_text,
    acc,
    *,
    chunks,
    frames,
    chunk_text,
):
    s = pl.program_id(0)
    j = pl.program_id(1)
    self_rows = chunks * frames * FRAME_TOK
    tokens = frames * FRAME_TOK

    @pl.when(j == 0)
    def _():
        values[GROUP_WIDTH:, :] = jnp.ones((ONES_ROWS, values.shape[1]), BF16)

        def chunk(i, carry):
            for f in range(frames):
                at = pl.multiple_of(rank_ref[s, i * frames + f] * FRAME_TOK, FRAME_TOK)
                rows = slice(f * FRAME_TOK, (f + 1) * FRAME_TOK)
                keys[pl.ds(at, FRAME_TOK), :] = kv_ref[i, 0, rows, :]
                values[:GROUP_WIDTH, pl.ds(at, FRAME_TOK)] = jnp.transpose(kv_ref[i, 1, rows, :])
            at = pl.multiple_of(place_ref[i] * chunk_text, chunk_text)
            rows = slice(tokens, tokens + chunk_text)
            keys[pl.ds(self_rows + at, chunk_text), :] = kv_ref[i, 0, rows, :]
            rows_text[pl.ds(at, chunk_text), :] = kv_ref[i, 1, rows, :]
            return carry

        lax.fori_loop(0, chunks, chunk, 0)
        for b in range(chunks * chunk_text // 128):
            values[:GROUP_WIDTH, self_rows + 128 * b : self_rows + 128 * (b + 1)] = jnp.transpose(
                rows_text[128 * b : 128 * (b + 1), :]
            )

    query = stacked(q_ref[0, 0, 0], mask_ref[...])

    def tile(base, size):
        scores = mxu(keys[pl.ds(base, size), :], query, ((1,), (1,)))
        weights = jnp.exp2(scores * EXP2_SCALE).astype(BF16)
        acc[...] += mxu(values[:, pl.ds(base, size)], weights)

    def finish(row):
        total = acc[GROUP_WIDTH : GROUP_WIDTH + 1, :]
        lse_ref[0, 0, row : row + 1, :] = jnp.log(total) * math.log2(math.e)
        return diagonal(acc[:GROUP_WIDTH, :] * (1.0 / total))

    acc[...] = jnp.zeros_like(acc)
    over_tiles(start_ref[s, j], count_ref[s, j], tile)
    self_out = finish(0)
    acc[...] = jnp.zeros_like(acc)
    tile(pl.multiple_of(self_rows + clip_ref[s, j] * CTX, 128), CTX)
    text_out = finish(1)
    self_ref[0, 0, 0] = self_out
    text_ref[0, 0, 0] = text_out
    mixed_ref[0, 0, 0] = (self_out + gate_ref[...] * text_out).astype(BF16)


def attn_bwd_kernel(
    rank_ref,
    start_ref,
    count_ref,
    clip_ref,
    place_ref,
    kv_ref,
    q_ref,
    grad_ref,
    self_ref,
    text_ref,
    lse_ref,
    gate_ref,
    mask_ref,
    dq_ref,
    dkv_ref,
    dgate_ref,
    keys,
    keys_flip,
    values,
    dkeys,
    dvalues,
    dquery,
    rows_text,
    *,
    chunks,
    frames,
    chunk_text,
):
    s = pl.program_id(0)
    j = pl.program_id(1)
    self_rows = chunks * frames * FRAME_TOK
    tokens = frames * FRAME_TOK

    @pl.when(jnp.logical_and(s == 0, j == 0))
    def _():
        dgate_ref[...] = jnp.zeros_like(dgate_ref)

    @pl.when(j == 0)
    def _():
        dkeys[...] = jnp.zeros_like(dkeys)
        dvalues[...] = jnp.zeros_like(dvalues)

        def chunk(i, carry):
            for f in range(frames):
                at = pl.multiple_of(rank_ref[s, i * frames + f] * FRAME_TOK, FRAME_TOK)
                rows = slice(f * FRAME_TOK, (f + 1) * FRAME_TOK)
                keys[pl.ds(at, FRAME_TOK), :] = kv_ref[i, 0, rows, :]
                keys_flip[:, pl.ds(at, FRAME_TOK)] = jnp.transpose(kv_ref[i, 0, rows, :])
                values[pl.ds(at, FRAME_TOK), :] = kv_ref[i, 1, rows, :]
            at = pl.multiple_of(place_ref[i] * chunk_text, chunk_text)
            rows = slice(tokens, tokens + chunk_text)
            keys[pl.ds(self_rows + at, chunk_text), :] = kv_ref[i, 0, rows, :]
            values[pl.ds(self_rows + at, chunk_text), :] = kv_ref[i, 1, rows, :]
            return carry

        lax.fori_loop(0, chunks, chunk, 0)
        for b in range(chunks * chunk_text // 128):
            rows = slice(self_rows + 128 * b, self_rows + 128 * (b + 1))
            keys_flip[:, rows] = jnp.transpose(keys[rows, :])

    mask = mask_ref[...]
    query = stacked(q_ref[0, 0, 0], mask)
    grad_low = grad_ref[0, 0, 0]
    grad_wide = grad_low.astype(F32)
    grad_text = (grad_wide * gate_ref[...]).astype(BF16)
    text_out = text_ref[0, 0, 0]
    dgate_ref[...] += jnp.sum(grad_wide * text_out, axis=0, keepdims=True)
    dquery[...] = jnp.zeros_like(dquery)

    def over(grad, out, lse):
        grad_stack = stacked(grad, mask)
        delta = head_row(grad.astype(F32) * out)

        def tile(base, size):
            rows = pl.ds(base, size)
            scores = mxu(keys[rows, :], query, ((1,), (1,)))
            weights = jnp.exp2(scores * EXP2_SCALE - lse)
            dweights = mxu(values[rows, :], grad_stack, ((1,), (1,)))
            dscores = (weights * (dweights - delta)).astype(BF16)
            dvalues[rows, :] += mxu(weights.astype(BF16), grad_stack)
            dkeys[rows, :] += mxu(dscores, query)
            dquery[...] += mxu(keys_flip[:, rows], dscores)

        return tile

    over_tiles(start_ref[s, j], count_ref[s, j], over(grad_low, self_ref[0, 0, 0], lse_ref[0, 0, 0:1, :]))
    over(grad_text, text_out, lse_ref[0, 0, 1:2, :])(
        pl.multiple_of(self_rows + clip_ref[s, j] * CTX, 128), CTX
    )
    dq_ref[0, 0, 0] = (diagonal(dquery[...]) * SCALE).astype(BF16)

    @pl.when(j == pl.num_programs(1) - 1)
    def _():
        def chunk(i, carry):
            for f in range(frames):
                at = pl.multiple_of(rank_ref[s, i * frames + f] * FRAME_TOK, FRAME_TOK)
                rows = slice(f * FRAME_TOK, (f + 1) * FRAME_TOK)
                dkv_ref[i, 0, rows, :] = (dkeys[pl.ds(at, FRAME_TOK), :] * SCALE).astype(BF16)
                dkv_ref[i, 1, rows, :] = dvalues[pl.ds(at, FRAME_TOK), :].astype(BF16)
            at = pl.multiple_of(self_rows + place_ref[i] * chunk_text, chunk_text)
            rows = slice(tokens, tokens + chunk_text)
            dkv_ref[i, 0, rows, :] = (dkeys[pl.ds(at, chunk_text), :] * SCALE).astype(BF16)
            dkv_ref[i, 1, rows, :] = dvalues[pl.ds(at, chunk_text), :].astype(BF16)
            return carry

        lax.fori_loop(0, chunks, chunk, 0)


def attention_specs(kv, query):
    chunks, _, streams, chunk_rows, _ = kv.shape
    groups, _, frames = query.shape[:3]
    chunk_text = chunk_rows - frames * FRAME_TOK
    sizes = dict(chunks=chunks, frames=frames, chunk_text=chunk_text)
    grid = (streams, groups * frames)
    kv_spec = pl.BlockSpec(
        (chunks, 2, None, chunk_rows, GROUP_WIDTH),
        lambda s, j, *_: (0, 0, s, 0, 0),
        pipeline_mode=pl.Buffered(1),
    )
    tok_spec = pl.BlockSpec(
        (1, 1, 1, FRAME_TOK, GROUP_WIDTH), lambda s, j, *_: (j // frames, s, j % frames, 0, 0)
    )
    lse_spec = pl.BlockSpec((1, 1, 2, STACK), lambda s, j, *_: (s, j, 0, 0))
    gate_spec = pl.BlockSpec((1, GROUP_WIDTH), lambda s, j, *_: (0, 0))
    mask_spec = pl.BlockSpec((STACK, GROUP_WIDTH), lambda s, j, *_: (0, 0))
    return sizes, grid, kv_spec, tok_spec, lse_spec, gate_spec, mask_spec


def stack_mask():
    head_of_row = np.arange(STACK) // FRAME_TOK
    head_of_lane = np.arange(GROUP_WIDTH) // HD
    return jnp.asarray((head_of_row[:, None] == head_of_lane[None, :]).astype(np.float32), BF16)


def attn_fwd(tables, kv, query, gate):
    sizes, grid, kv_spec, tok_spec, lse_spec, gate_spec, mask_spec = attention_specs(kv, query)
    total = kv.shape[0] * kv.shape[3]
    text_rows = sizes["chunks"] * sizes["chunk_text"]
    wide = jax.ShapeDtypeStruct(query.shape, F32)
    return pl.pallas_call(
        functools.partial(attn_fwd_kernel, **sizes),
        grid_spec=pltpu.PrefetchScalarGridSpec(
            num_scalar_prefetch=5,
            grid=grid,
            in_specs=[kv_spec, tok_spec, gate_spec, mask_spec],
            out_specs=[tok_spec, tok_spec, tok_spec, lse_spec],
            scratch_shapes=[
                pltpu.VMEM((total, GROUP_WIDTH), BF16),
                pltpu.VMEM((GROUP_WIDTH + ONES_ROWS, total), BF16),
                pltpu.VMEM((text_rows, GROUP_WIDTH), BF16),
                pltpu.VMEM((GROUP_WIDTH + ONES_ROWS, STACK), F32),
            ],
        ),
        out_shape=[
            jax.ShapeDtypeStruct(query.shape, BF16),
            wide,
            wide,
            jax.ShapeDtypeStruct((grid[0], grid[1], 2, STACK), F32),
        ],
        compiler_params=pltpu.CompilerParams(
            dimension_semantics=("arbitrary", "arbitrary"),
            vmem_limit_bytes=min(60 * MIB, total * 2600 + 16 * MIB),
        ),
        cost_estimate=pl.CostEstimate(
            flops=grid[0] * grid[1] * STACK * 2304 * GROUP_WIDTH * 4,
            bytes_accessed=kv.size * 2 + query.size * 12,
            transcendentals=grid[0] * grid[1] * STACK * 2304,
        ),
        name="attention",
    )(*tables, kv, query, gate, stack_mask())


def attn_bwd(tables, kv, query, grad, self_out, text_out, lse, gate):
    sizes, grid, kv_spec, tok_spec, lse_spec, gate_spec, mask_spec = attention_specs(kv, query)
    total = kv.shape[0] * kv.shape[3]
    text_rows = sizes["chunks"] * sizes["chunk_text"]
    return pl.pallas_call(
        functools.partial(attn_bwd_kernel, **sizes),
        grid_spec=pltpu.PrefetchScalarGridSpec(
            num_scalar_prefetch=5,
            grid=grid,
            in_specs=[
                kv_spec,
                tok_spec,
                tok_spec,
                tok_spec,
                tok_spec,
                lse_spec,
                gate_spec,
                mask_spec,
            ],
            out_specs=[tok_spec, kv_spec, gate_spec],
            scratch_shapes=[
                pltpu.VMEM((total, GROUP_WIDTH), BF16),
                pltpu.VMEM((GROUP_WIDTH, total), BF16),
                pltpu.VMEM((total, GROUP_WIDTH), BF16),
                pltpu.VMEM((total, GROUP_WIDTH), F32),
                pltpu.VMEM((total, GROUP_WIDTH), F32),
                pltpu.VMEM((GROUP_WIDTH, STACK), F32),
                pltpu.VMEM((text_rows, GROUP_WIDTH), BF16),
            ],
        ),
        out_shape=[
            jax.ShapeDtypeStruct(query.shape, BF16),
            jax.ShapeDtypeStruct(kv.shape, BF16),
            jax.ShapeDtypeStruct((1, GROUP_WIDTH), F32),
        ],
        compiler_params=pltpu.CompilerParams(
            dimension_semantics=("arbitrary", "arbitrary"),
            vmem_limit_bytes=min(62 * MIB, total * 5800 + 16 * MIB),
        ),
        cost_estimate=pl.CostEstimate(
            flops=grid[0] * grid[1] * STACK * 2304 * GROUP_WIDTH * 10,
            bytes_accessed=kv.size * 4 + query.size * 14,
            transcendentals=grid[0] * grid[1] * STACK * 2304,
        ),
        name="attention_back",
    )(*tables, kv, query, grad, self_out, text_out, lse, gate, stack_mask())


def unit_rms(values):
    inv = lax.rsqrt(jnp.mean(values * values, axis=-1, keepdims=True) + EPSILON)
    return values * inv, inv


def unit_back(grad_unit, unit, inv):
    return inv * (grad_unit - unit * jnp.mean(grad_unit * unit, axis=-1, keepdims=True))


def rope_lanes(frames):
    half = HD // 2
    frame_pairs = HD // 8
    row_pairs = (half - frame_pairs) // 2
    col_pairs = half - frame_pairs - row_pairs
    pair = (np.arange(128) % HD) // 2

    def lanes(first, count):
        freq = 10000.0 ** (-(np.arange(count, dtype=np.float32)) / np.float32(count))
        out = np.zeros((128,), np.float32)
        inside = (pair >= first) & (pair < first + count)
        out[inside] = freq.astype(np.float32)[pair[inside] - first]
        return jnp.asarray(out)[None, :]

    rows = frames.shape[0]
    inner = jnp.arange(rows) % FRAME_TOK
    row_pos = (inner // PW).astype(F32)
    col_pos = (inner % PW).astype(F32)
    angle = (
        frames[:, None] * lanes(0, frame_pairs)
        + row_pos[:, None] * lanes(frame_pairs, row_pairs)
        + col_pos[:, None] * lanes(frame_pairs + row_pairs, col_pairs)
    )
    sign = jnp.asarray(np.where(np.arange(128) % 2 == 0, -1.0, 1.0).astype(np.float32))[None, :]
    return jnp.cos(angle), jnp.sin(angle) * sign


def gain_rows(*gains):
    rows = [jnp.concatenate([g, g]) for g in gains]
    rows += [jnp.zeros((128,), F32)] * (8 - len(rows))
    return jnp.stack(rows)


def pad_parts(values, parts):
    width = values.shape[1] // parts
    wide = lane_tiles(width)
    if wide == width:
        return values
    cut = values.reshape(values.shape[0], parts, width)
    cut = jnp.pad(cut, ((0, 0), (0, 0), (0, wide - width)))
    return cut.reshape(values.shape[0], parts * wide)


def cut_parts(values, parts, width):
    wide = values.shape[1] // parts
    if wide == width:
        return values
    return values.reshape(values.shape[0], parts, wide)[:, :, :width].reshape(
        values.shape[0], parts * width
    )


def bit_reverse(index, bits):
    return sum(((index >> b) & 1) << (bits - 1 - b) for b in range(bits))


def per_device(
    fsdp,
    dps,
    states,
    cotangent,
    segment_ids,
    frame_ids,
    condition,
    context,
    w_modulate,
    w_qkv,
    w_text_kv,
    w_out,
    w_gate_up,
    w_down,
    gain_attn_in,
    gain_attn_out,
    gain_ffn_in,
    gain_ffn_out,
    gain_query,
    gain_key,
    gain_text_key,
    cross_gate,
):
    xs = Moves("fsdp", fsdp)
    ds = Moves("dp", dps)
    rows_in = states[0]
    tokens, width = rows_in.shape
    frames = tokens // FRAME_TOK
    heads = cross_gate.shape[0]
    own_heads = heads // fsdp
    own_width = own_heads * HD
    groups = own_heads // GROUP_HEADS
    ranks = dps // groups
    clips = condition.shape[1]
    text_local = context[0]
    text_own = text_local.shape[0]
    all_tokens = fsdp * tokens
    group_me = ds.me // ranks
    rank_me = ds.me % ranks

    def frame_view(values):
        return values.reshape(frames, FRAME_TOK, values.shape[-1])

    def group_exchange(blocks):
        pick = lambda s: lax.dynamic_index_in_dim(blocks, group_me ^ s, 0, keepdims=False)
        return [pick(0)] + [ds.swap(pick(s), s * ranks) for s in range(1, groups)]

    def group_return(blocks):
        got = jnp.stack([blocks[0]] + [ds.swap(blocks[s], s * ranks) for s in range(1, groups)])
        return [
            lax.dynamic_index_in_dim(got, group_me ^ g, 0, keepdims=False) for g in range(groups)
        ]

    rank_bits = ranks.bit_length() - 1

    def rank_gather(value):
        for b in reversed(range(rank_bits)):
            value = jnp.stack([value, ds.swap(value, 1 << b)])
        return value.reshape((ranks,) + value.shape[rank_bits:])

    def rank_scatter(value):
        value = value.reshape((2,) * rank_bits + value.shape[1:])
        for b in range(rank_bits):
            got = ds.swap(value[1], 1 << b)
            value = (value[0].astype(F32) + got.astype(F32)).astype(BF16)
        return value

    own_frames = segment_ids[0][::FRAME_TOK].astype(F32)
    stream_seg = jnp.stack(xs.gather(own_frames)).astype(jnp.int32)
    rel_of_place = [bit_reverse(p, rank_bits) for p in range(ranks)]
    place_dev = jnp.stack(
        [
            (group_me ^ g) * ranks + (rank_me ^ rel_of_place[p])
            for p in range(ranks)
            for g in range(groups)
        ]
    )
    kv_frame = (place_dev[:, None] * frames + jnp.arange(frames)[None, :]).reshape(-1)
    q_dev = jnp.stack([(group_me ^ g) * ranks + rank_me for g in range(groups)])
    q_frame = (q_dev[:, None] * frames + jnp.arange(frames)[None, :]).reshape(-1)
    kv_seg = jnp.take(stream_seg, kv_frame, axis=1)
    q_seg = jnp.take(stream_seg, q_frame, axis=1)
    order = jnp.arange(kv_seg.shape[1])
    less = kv_seg[:, None, :] < kv_seg[:, :, None]
    tie = (kv_seg[:, None, :] == kv_seg[:, :, None]) & (order[None, None, :] < order[None, :, None])
    kv_rank = jnp.sum((less | tie).astype(jnp.int32), axis=2)
    q_start = jnp.sum((kv_seg[:, None, :] < q_seg[:, :, None]).astype(jnp.int32), axis=2)
    q_count = jnp.sum((kv_seg[:, None, :] == q_seg[:, :, None]).astype(jnp.int32), axis=2)
    tables = (
        kv_rank,
        q_start,
        q_count,
        jnp.maximum(q_seg, 0),
        place_dev.astype(jnp.int32),
    )

    silu_cond = jax.nn.silu(condition[0]).astype(BF16)
    cond_rel = jnp.concatenate(xs.gather(silu_cond))
    cond_own = xs.own_block(cond_rel, 1)
    mod_part = mxu(cond_own, w_modulate).reshape(fsdp, clips, -1)
    modulation = mod_part[0]
    for s in range(1, fsdp):
        modulation = modulation + xs.swap(mod_part[s], s)
    own_seg = lax.dynamic_slice_in_dim(stream_seg[0], ds.me * frames, frames)
    onehot = (own_seg[:, None] == jnp.arange(clips)[None, :]).astype(F32)
    per_frame = jnp.dot(onehot, modulation, precision=HIGHEST)[:, None, :]
    scale_attn, gate_attn, scale_ffn, gate_ffn = jnp.split(per_frame, 4, axis=2)

    def own_columns(weight, parts):
        rows = weight.shape[0]
        cut = weight.reshape(rows, parts, fsdp, own_width)
        pick = lambda s: lax.dynamic_index_in_dim(cut, xs.me ^ s, 2, keepdims=False)
        blocks = [pick(0)]
        core = ds.me % 2
        for s in range(1, fsdp):
            half = lax.dynamic_slice_in_dim(pick(s), core * (rows // 2), rows // 2)
            got = xs.swap(half, s)
            other = ds.swap(got, 1)
            blocks.append(
                jnp.where(
                    core == 0,
                    jnp.concatenate([got, other]),
                    jnp.concatenate([other, got]),
                )
            )
        return jnp.concatenate(blocks).reshape(fsdp * rows, parts * own_width)

    w_cols = own_columns(w_qkv, 3)
    states_f = frame_view(rows_in)
    unit_in, inv_in = unit_rms(states_f)
    normed = (unit_in * gain_attn_in * (1.0 + scale_attn)).astype(BF16).reshape(tokens, width)
    normed_all = xs.reorder(jnp.concatenate(xs.gather(normed)), 1)
    projected = pad_parts(mxu(normed_all, w_cols), 3)
    frames_all = jnp.concatenate(xs.gather(frame_ids[0].astype(F32)))
    cosine, sine = rope_lanes(frames_all)
    qk_kinds = ((True, True), (True, True), (False, False))
    qk_gains = gain_rows(gain_query, gain_key)
    heads_qkv = norm_fwd(projected, cosine, sine, qk_gains, qk_kinds, groups)

    text_rel = jnp.concatenate(
        [xs.own_block(text_local, 1)]
        + [xs.swap(xs.own_block(text_local, 1, s), s) for s in range(1, fsdp)]
    )
    text_part = mxu(text_rel, w_text_kv).reshape(fsdp, text_own, 2, fsdp, own_width)
    text_raw = lax.dynamic_index_in_dim(text_part, xs.me, 3, keepdims=False)
    for s in range(1, fsdp):
        piece = lax.dynamic_index_in_dim(text_part, xs.me ^ s, 3, keepdims=False)
        piece = jnp.stack([piece[s ^ k] for k in range(fsdp)])
        text_raw = text_raw + xs.swap(piece.astype(BF16), s).astype(F32)
    text_raw = pad_parts(text_raw.reshape(fsdp * text_own, 2 * own_width), 2)
    text_kinds = ((True, False), (False, False))
    text_gains = gain_rows(gain_text_key)
    text_flat = jnp.ones((fsdp * text_own, 128), F32)
    heads_text = norm_fwd(text_raw, text_flat, text_flat, text_gains, text_kinds, groups)

    def joined(parts, text):
        return jnp.concatenate(
            [
                parts.reshape(parts.shape[:2] + (fsdp, tokens, GROUP_WIDTH)),
                text.reshape(text.shape[:2] + (fsdp, text_own, GROUP_WIDTH)),
            ],
            axis=3,
        )

    kv_blocks = jnp.swapaxes(joined(heads_qkv[1:], heads_text), 0, 1)
    kv = rank_gather(jnp.stack(group_exchange(kv_blocks)))
    kv = kv.reshape((ranks * groups,) + kv.shape[2:])
    query = jnp.stack(group_exchange(heads_qkv[0]))
    query = query.reshape(groups, fsdp, frames, FRAME_TOK, GROUP_WIDTH)
    tanh_gate = jnp.tanh(cross_gate)
    first_head = xs.me * own_heads + group_me * GROUP_HEADS
    gate_row = jnp.repeat(lax.dynamic_slice_in_dim(tanh_gate, first_head, GROUP_HEADS), HD)[None, :]
    mixed_group, self_out, text_out, lse = attn_fwd(tables, kv, query, gate_row)
    mixed_low = jnp.concatenate(
        group_return(mixed_group.reshape(groups, all_tokens, GROUP_WIDTH)), axis=1
    )

    def by_stream(values):
        return values.reshape(fsdp, tokens, values.shape[-1])

    mixed_out = frame_view(xs.scatter_sum(by_stream(mxu(mixed_low, w_out))))
    unit_mix, inv_mix = unit_rms(mixed_out)
    tanh_attn = jnp.tanh(gate_attn)
    after = states_f + tanh_attn * unit_mix * gain_attn_out
    unit_ffn, inv_ffn = unit_rms(after)
    ffn_low = (unit_ffn * gain_ffn_in * (1.0 + scale_ffn)).astype(BF16).reshape(tokens, width)
    ffn_all = jnp.concatenate(xs.gather(ffn_low))
    gate_part = mxu(ffn_all, w_gate_up[0])
    up_part = mxu(ffn_all, w_gate_up[1])
    sig = jax.nn.sigmoid(gate_part)
    silu = gate_part * sig
    hidden = (silu * up_part).astype(BF16)
    ffn_out = frame_view(xs.scatter_sum(by_stream(mxu(hidden, w_down))))
    unit_out, inv_out = unit_rms(ffn_out)
    tanh_ffn = jnp.tanh(gate_ffn)
    output = after + tanh_ffn * unit_out * gain_ffn_out

    def frame_sum(values):
        return jnp.sum(values, axis=1)

    def gain_sum(values):
        return jnp.sum(values, axis=(0, 1))

    cot = frame_view(cotangent[0])
    cot_unit = cot * unit_out
    grad_gate_ffn = frame_sum(cot_unit) * gain_ffn_out * (1.0 - tanh_ffn[:, 0] ** 2)
    grad_gain_ffn_out = jnp.sum(frame_sum(cot_unit) * tanh_ffn[:, 0], axis=0)
    grad_ffn_low = (
        unit_back(cot * (tanh_ffn * gain_ffn_out), unit_out, inv_out)
        .astype(BF16)
        .reshape(tokens, width)
    )
    grad_ffn_all = jnp.concatenate(xs.gather(grad_ffn_low))
    grad_hidden = mxu(grad_ffn_all, w_down, ((1,), (1,)))
    grad_gate = grad_hidden * up_part * (sig * (1.0 + gate_part * (1.0 - sig)))
    grad_up = grad_hidden * silu
    grad_gate_low = grad_gate.astype(BF16)
    grad_up_low = grad_up.astype(BF16)

    def reduce_rows(term):
        return lax.psum_scatter(
            term.astype(BF16), "dp", scatter_dimension=0, tiled=True
        ).astype(F32)

    rows_first = ((0,), (0,))
    grad_w_down = jnp.transpose(reduce_rows(mxu(grad_ffn_all, hidden, rows_first)))
    grad_w_gate_up = jnp.stack(
        [
            reduce_rows(mxu(ffn_all, grad_gate_low, rows_first)),
            reduce_rows(mxu(ffn_all, grad_up_low, rows_first)),
        ]
    )
    grad_ffn_in = frame_view(
        xs.scatter_sum(
            by_stream(
                mxu(grad_gate_low, w_gate_up[0], ((1,), (1,)))
                + mxu(grad_up_low, w_gate_up[1], ((1,), (1,)))
            )
        )
    )
    grad_unit = grad_ffn_in * unit_ffn
    grad_scale_ffn = frame_sum(grad_unit) * gain_ffn_in
    grad_gain_ffn_in = jnp.sum(frame_sum(grad_unit) * (1.0 + scale_ffn[:, 0]), axis=0)
    grad_after = cot + unit_back(
        grad_ffn_in * (gain_ffn_in * (1.0 + scale_ffn)), unit_ffn, inv_ffn
    )
    after_unit = grad_after * unit_mix
    grad_gate_attn = frame_sum(after_unit) * gain_attn_out * (1.0 - tanh_attn[:, 0] ** 2)
    grad_gain_attn_out = jnp.sum(frame_sum(after_unit) * tanh_attn[:, 0], axis=0)
    grad_mix_low = (
        unit_back(grad_after * (tanh_attn * gain_attn_out), unit_mix, inv_mix)
        .astype(BF16)
        .reshape(tokens, width)
    )
    grad_mix_all = jnp.concatenate(xs.gather(grad_mix_low))
    grad_mixed = mxu(grad_mix_all, w_out, ((1,), (1,))).astype(BF16)
    grad_w_out = jnp.transpose(reduce_rows(mxu(grad_mix_all, mixed_low, rows_first)))

    grad_blocks = jnp.stack(
        [grad_mixed[:, GROUP_WIDTH * g : GROUP_WIDTH * (g + 1)] for g in range(groups)]
    )
    grad_group = jnp.stack(group_exchange(grad_blocks)).reshape(query.shape)
    dquery, dkv, dgate = attn_bwd(tables, kv, query, grad_group, self_out, text_out, lse, gate_row)
    dkv = rank_scatter(dkv.reshape((ranks, groups) + dkv.shape[1:]))
    dq_back = jnp.stack(group_return(dquery.reshape(groups, all_tokens, GROUP_WIDTH)))
    dkv_back = jnp.stack(group_return(dkv))
    dkv_tok = dkv_back[:, :, :, :tokens].reshape(groups, 2, all_tokens, GROUP_WIDTH)
    dkv_text = dkv_back[:, :, :, tokens:].reshape(groups, 2, fsdp * text_own, GROUP_WIDTH)
    grad_heads = jnp.concatenate([dq_back[None], jnp.swapaxes(dkv_tok, 0, 1)])
    grad_proj, gain_qk = norm_bwd(projected, grad_heads, cosine, sine, qk_gains, qk_kinds, groups)
    grad_proj = cut_parts(grad_proj, 3, own_width)
    grad_text, gain_text = norm_bwd(
        text_raw,
        jnp.swapaxes(dkv_text, 0, 1),
        text_flat,
        text_flat,
        text_gains,
        text_kinds,
        groups,
    )
    grad_text = cut_parts(grad_text, 2, own_width)

    grad_normed_rel = mxu(grad_proj, w_cols, ((1,), (1,)))
    grad_normed = frame_view(xs.scatter_sum(by_stream(xs.reorder(grad_normed_rel, 1))))
    in_unit = grad_normed * unit_in
    grad_scale_attn = frame_sum(in_unit) * gain_attn_in
    grad_gain_attn_in = jnp.sum(frame_sum(in_unit) * (1.0 + scale_attn[:, 0]), axis=0)
    grad_input = grad_after + unit_back(
        grad_normed * (gain_attn_in * (1.0 + scale_attn)), unit_in, inv_in
    )

    def gather_columns(values, rows, parts):
        cut = values.reshape(fsdp, rows, parts, own_width)
        got = [cut]
        for s in range(1, fsdp):
            other = xs.swap(cut, s)
            got.append(jnp.stack([other[s ^ k] for k in range(fsdp)]))
        got = jnp.stack(got)
        whole = jnp.stack(
            [lax.dynamic_index_in_dim(got, xs.me ^ k, 0, keepdims=False) for k in range(fsdp)],
            axis=3,
        )
        return whole.reshape(fsdp * rows, parts * fsdp * own_width)

    grad_proj_all = gather_columns(grad_proj, tokens, 3)
    normed_own = normed_all[:, : width // fsdp]
    grad_w_qkv = jnp.transpose(reduce_rows(mxu(grad_proj_all, normed_own, rows_first)))

    grad_text_all = gather_columns(grad_text, text_own, 2)
    text_cols = grad_text_all.shape[1] // dps
    grad_text_cols = jnp.swapaxes(
        grad_text_all.reshape(fsdp * text_own, dps, text_cols), 0, 1
    )
    grad_text_cols = lax.all_to_all(grad_text_cols, "dp", 0, 0, tiled=True)
    text_every = lax.all_gather(text_rel, "dp", axis=0, tiled=True)
    grad_w_text_kv = mxu(text_every, grad_text_cols.reshape(-1, text_cols), rows_first)

    frame_grads = jnp.concatenate(
        [grad_scale_attn, grad_gate_attn, grad_scale_ffn, grad_gate_ffn], axis=1
    )
    clip_grads = jnp.dot(jnp.transpose(onehot), frame_grads, precision=HIGHEST)
    mod_cols = clip_grads.shape[1] // dps
    clip_grads = jnp.swapaxes(clip_grads.reshape(clips, dps, mod_cols), 0, 1)
    clip_grads = jnp.sum(lax.all_to_all(clip_grads, "dp", 0, 0, tiled=True), axis=0)
    clip_rel = jnp.concatenate(xs.gather(clip_grads))
    grad_w_modulate = jnp.dot(
        jnp.transpose(cond_own.astype(F32)), clip_rel, precision=HIGHEST
    )
    head_term = jnp.sum(dgate.reshape(GROUP_HEADS, HD), axis=1)
    gate_term = lax.dynamic_update_slice_in_dim(
        jnp.zeros((heads,), F32), head_term, first_head, 0
    )
    gate_term = gate_term * (1.0 - tanh_gate * tanh_gate)
    fold = lambda row: row[:HD] + row[HD:]
    small = [
        grad_gain_attn_in,
        grad_gain_attn_out,
        grad_gain_ffn_in,
        grad_gain_ffn_out,
        fold(gain_qk[0]),
        fold(gain_qk[1]),
        fold(gain_text[0]),
        gate_term,
    ]
    sizes = [v.shape[0] for v in small]
    packed = jnp.concatenate(small)
    packed = jnp.pad(packed, (0, -packed.shape[0] % 1024)).reshape(-1, 128)
    for moves in (ds, xs):
        for b in range(moves.size.bit_length() - 1):
            packed = packed + moves.swap(packed, 1 << b)
    packed = packed.reshape(-1)
    sums = []
    at = 0
    for size in sizes:
        sums.append(packed[at : at + size])
        at += size
    return (
        output.reshape(1, tokens, width),
        grad_input.reshape(1, tokens, width),
        grad_w_modulate,
        grad_w_qkv,
        grad_w_text_kv,
        grad_w_out,
        grad_w_gate_up,
        grad_w_down,
        *sums,
    )


def solution(mesh):
    rows = P("fsdp", "dp", None)
    first = P("fsdp", None)
    split = P("fsdp", "dp")
    return jax.shard_map(
        functools.partial(per_device, mesh.shape["fsdp"], mesh.shape["dp"]),
        mesh=mesh,
        in_specs=(
            rows,
            rows,
            first,
            split,
            P("fsdp", None, None),
            rows,
            first,
            first,
            first,
            first,
            P(None, None, "fsdp"),
            first,
        )
        + (P(),) * 8,
        out_specs=(
            rows,
            rows,
            split,
            split,
            split,
            split,
            P(None, "dp", "fsdp"),
            split,
        )
        + (P(),) * 8,
        check_vma=False,
    )
```

```python
import functools
import math

import jax
import jax.numpy as jnp
import numpy as np
from jax import lax
from jax.experimental import pallas as pl
from jax.experimental.pallas import tpu as pltpu
from jax.sharding import PartitionSpec as P

HD = 64
CTX = 256
FRAME_TOK = 128
PW = 16
EPSILON = 1e-06
GROUP_HEADS = 3
GROUP_WIDTH = GROUP_HEADS * HD
STACK = GROUP_HEADS * FRAME_TOK
ONES_ROWS = 16
HIGHEST = lax.Precision.HIGHEST
BF16 = jnp.bfloat16
F32 = jnp.float32
SCALE = HD ** (-0.5)
EXP2_SCALE = SCALE * math.log2(math.e)
MIB = 1 << 20
COST_CUT = 100


def mxu(a, b, dims=((1,), (0,))):
    return lax.dot_general(a, b, (dims, ((), ())), preferred_element_type=F32)


class Moves:
    def __init__(self, axis, size):
        self.axis = axis
        self.size = size
        self.me = lax.axis_index(axis)

    def swap(self, value, mask):
        return lax.ppermute(value, self.axis, [(i, i ^ mask) for i in range(self.size)])

    def gather(self, value):
        return [value] + [self.swap(value, s) for s in range(1, self.size)]

    def scatter_sum(self, parts):
        total = parts[0].astype(F32)
        for s in range(1, self.size):
            total = total + self.swap(parts[s].astype(BF16), s).astype(F32)
        return total

    def reorder(self, value, axis):
        block = value.shape[axis] // self.size
        return jnp.concatenate(
            [
                lax.dynamic_slice_in_dim(value, (self.me ^ s) * block, block, axis)
                for s in range(self.size)
            ],
            axis,
        )

    def own_block(self, value, axis, s=0):
        block = value.shape[axis] // self.size
        return lax.dynamic_slice_in_dim(value, (self.me ^ s) * block, block, axis)


def lane_tiles(width):
    return -(-width // 128) * 128


def turn(values, cosine, sine):
    lane = lax.broadcasted_iota(jnp.int32, values.shape, 1)
    other = jnp.where(lane % 2 == 0, pltpu.roll(values, 127, 1), pltpu.roll(values, 1, 1))
    return values * cosine + other * sine


def head_means(values, ones):
    total = lax.dot_general(
        values, ones, (((1,), (0,)), ((), ())), precision=HIGHEST, preferred_element_type=F32
    )
    return total * (1.0 / HD)


def joined(pieces, axis):
    return jnp.concatenate(pieces, axis=axis) if len(pieces) > 1 else pieces[0]


def widened(values):
    missing = lane_tiles(values.shape[1]) - values.shape[1]
    if not missing:
        return values
    return jnp.concatenate([values, jnp.zeros((values.shape[0], missing), values.dtype)], axis=1)


def tiles_of(values):
    return [values[:, 128 * t : 128 * (t + 1)] for t in range(values.shape[1] // 128)]


def normed_heads(raw, ones, gain):
    return [x * lax.rsqrt(head_means(x * x, ones) + EPSILON) * gain for x in tiles_of(raw)]


def head_ones():
    lane = np.arange(128) // HD
    return jnp.asarray((lane[:, None] == lane[None, :]).astype(np.float32))


def group_cut(values, g):
    return values[:, GROUP_WIDTH * g : GROUP_WIDTH * (g + 1)]


def packed_frames(values, frames):
    return joined([values[FRAME_TOK * f : FRAME_TOK * (f + 1)] for f in range(frames)], 1)


def call(kernel, name, grid, prefetch, in_specs, out_specs, out_shape, scratch, vmem, flops, moved, args):
    return pl.pallas_call(
        kernel,
        grid_spec=pltpu.PrefetchScalarGridSpec(
            num_scalar_prefetch=prefetch,
            grid=grid,
            in_specs=in_specs,
            out_specs=out_specs,
            scratch_shapes=scratch,
        ),
        out_shape=out_shape,
        compiler_params=pltpu.CompilerParams(
            dimension_semantics=("arbitrary",) * len(grid), vmem_limit_bytes=vmem
        ),
        cost_estimate=pl.CostEstimate(
            flops=int(flops) // COST_CUT, bytes_accessed=int(moved) // COST_CUT, transcendentals=0
        ),
        name=name,
    )(*args)


def whole_spec(shape):
    zeros = (0,) * len(shape)
    return pl.BlockSpec(shape, lambda *_: zeros)


def heads_kernel(
    core_ref,
    x_ref,
    w_ref,
    text_ref,
    cos_ref,
    sin_ref,
    gain_ref,
    ones_ref,
    send_q,
    send_kv,
    keep_q,
    keep_kv,
    *,
    half,
    groups,
    frames,
    own_width,
):
    step = pl.program_id(0)
    tokens = frames * FRAME_TOK
    ones = ones_ref[...]
    parts = []
    for p in range(3):
        raw = widened(mxu(x_ref[0], w_ref[:, own_width * p : own_width * (p + 1)]))
        if p < 2:
            raw = joined(
                [
                    turn(x, cos_ref[0], sin_ref[0])
                    for x in normed_heads(raw, ones, gain_ref[p : p + 1, :])
                ],
                1,
            )
        parts.append(raw.astype(BF16))
    wide = text_ref.shape[2] // 2
    text_key = joined(normed_heads(text_ref[0, :, :wide], ones, gain_ref[2:3, :]), 1).astype(BF16)
    text_value = text_ref[0, :, wide:].astype(BF16)

    def put(q_ref, kv_ref):
        for g in range(groups):
            q_ref[0, g] = packed_frames(group_cut(parts[0], g), frames)
            kv_ref[0, g, :tokens] = joined([group_cut(parts[1], g), group_cut(parts[2], g)], 1)
            kv_ref[0, g, tokens:] = joined([group_cut(text_key, g), group_cut(text_value, g)], 1)

    @pl.when(step < half)
    def _():
        put(send_q, send_kv)

    @pl.when(step >= half)
    def _():
        put(keep_q, keep_kv)


def set_stream(step, core, half):
    other = jnp.where(step < half, 1 - core, core)
    return other * half + step % half


def make_heads(core, x, w_cols, text_raw, cosine, sine, gains, groups):
    streams, tokens, width = x.shape
    half = streams // 2
    frames = tokens // FRAME_TOK
    own_width = w_cols.shape[1] // 3
    text_own = text_raw.shape[1]
    by_stream = lambda i, core: (set_stream(i, core[0], half), 0, 0)
    q_block = (1, groups, FRAME_TOK, frames * GROUP_WIDTH)
    kv_block = (1, groups, tokens + text_own, 2 * GROUP_WIDTH)
    first = lambda i, core: (jnp.minimum(i, half - 1), 0, 0, 0)
    second = lambda i, core: (jnp.maximum(i - half, 0), 0, 0, 0)
    return call(
        functools.partial(
            heads_kernel, half=half, groups=groups, frames=frames, own_width=own_width
        ),
        "make_heads",
        (streams,),
        1,
        [
            pl.BlockSpec((1, tokens, width), by_stream),
            whole_spec(w_cols.shape),
            pl.BlockSpec((1,) + text_raw.shape[1:], by_stream),
            pl.BlockSpec((1, tokens, 128), by_stream),
            pl.BlockSpec((1, tokens, 128), by_stream),
            whole_spec((8, 128)),
            whole_spec((128, 128)),
        ],
        [
            pl.BlockSpec(q_block, first),
            pl.BlockSpec(kv_block, first),
            pl.BlockSpec(q_block, second),
            pl.BlockSpec(kv_block, second),
        ],
        [
            jax.ShapeDtypeStruct((half,) + q_block[1:], BF16),
            jax.ShapeDtypeStruct((half,) + kv_block[1:], BF16),
        ]
        * 2,
        [],
        48 * MIB,
        2 * x.size * w_cols.shape[1],
        x.size * 2 + w_cols.size * 2 + x.size * 3,
        (core, x, w_cols, text_raw, cosine, sine, gains, head_ones()),
    )


BIG = 4


def over_tiles(start, count, body):
    big = count // BIG

    def big_step(t, carry):
        body(pl.multiple_of((start + t * BIG) * FRAME_TOK, FRAME_TOK), BIG * FRAME_TOK)
        return carry

    def small_step(t, carry):
        body(pl.multiple_of((start + big * BIG + t) * FRAME_TOK, FRAME_TOK), FRAME_TOK)
        return carry

    lax.fori_loop(0, big, big_step, 0)
    lax.fori_loop(0, count - big * BIG, small_step, 0)


def stacked(values, mask):
    return jnp.concatenate([values] * GROUP_HEADS, axis=0) * mask


def diagonal(values):
    own = [
        values[HD * h : HD * (h + 1), FRAME_TOK * h : FRAME_TOK * (h + 1)]
        for h in range(GROUP_HEADS)
    ]
    return jnp.transpose(jnp.concatenate(own, axis=0))


def head_row(values):
    flipped = jnp.transpose(values)
    return jnp.concatenate(
        [
            jnp.sum(flipped[HD * h : HD * (h + 1), :], axis=0, keepdims=True)
            for h in range(GROUP_HEADS)
        ],
        axis=1,
    )


def each_chunk(kv_refs, rank_ref, place_ref, s, frames, chunk_text, self_rows, frame_body, text_body):
    tokens = frames * FRAME_TOK
    for i, ref in enumerate(kv_refs):

        def one(c, carry, i=i, ref=ref):
            chunk = 2 * i + c
            for f in range(frames):
                at = pl.multiple_of(rank_ref[s, chunk * frames + f] * FRAME_TOK, FRAME_TOK)
                frame_body(ref, c, slice(f * FRAME_TOK, (f + 1) * FRAME_TOK), at)
            at = pl.multiple_of(self_rows + place_ref[chunk] * chunk_text, chunk_text)
            text_body(ref, c, slice(tokens, tokens + chunk_text), at)
            return carry

        lax.fori_loop(0, 2, one, 0)


def unpack_frames(refs, scratch, frames):
    for i, ref in enumerate(refs):
        for c in range(2):
            for f in range(frames):
                scratch[(2 * i + c) * frames + f] = ref[
                    c, :, GROUP_WIDTH * f : GROUP_WIDTH * (f + 1)
                ]


def attn_fwd_kernel(*refs, pieces, groups, frames, chunk_text):
    rank_ref, start_ref, count_ref, clip_ref, place_ref = refs[:5]
    refs = refs[5:]
    kv_refs, refs = refs[:pieces], refs[pieces:]
    q_refs, refs = refs[:groups], refs[groups:]
    gate_ref, mask_ref = refs[:2]
    mixed_refs, refs = refs[2 : 2 + groups], refs[2 + groups :]
    self_ref, text_ref, lse_ref, keys, values, rows_text, queries, mixes, acc = refs
    s = pl.program_id(0)
    j = pl.program_id(1)
    self_rows = pieces * 2 * frames * FRAME_TOK
    text_rows = rows_text.shape[0]
    K = slice(0, GROUP_WIDTH)
    V = slice(GROUP_WIDTH, 2 * GROUP_WIDTH)

    @pl.when(j == 0)
    def _():
        values[GROUP_WIDTH:, :] = jnp.ones((ONES_ROWS, values.shape[1]), BF16)

        def frame_body(ref, c, rows, at):
            keys[pl.ds(at, FRAME_TOK), :] = ref[c, rows, K]
            values[:GROUP_WIDTH, pl.ds(at, FRAME_TOK)] = jnp.transpose(ref[c, rows, V])

        def text_body(ref, c, rows, at):
            keys[pl.ds(at, chunk_text), :] = ref[c, rows, K]
            rows_text[pl.ds(at - self_rows, chunk_text), :] = ref[c, rows, V]

        each_chunk(
            kv_refs, rank_ref, place_ref, s, frames, chunk_text, self_rows, frame_body, text_body
        )
        for b in range(text_rows // 128):
            values[:GROUP_WIDTH, self_rows + 128 * b : self_rows + 128 * (b + 1)] = jnp.transpose(
                rows_text[128 * b : 128 * (b + 1), :]
            )
        unpack_frames(q_refs, queries, frames)

    query = stacked(queries[j], mask_ref[...])

    def tile(base, size):
        scores = mxu(keys[pl.ds(base, size), :], query, ((1,), (1,)))
        weights = jnp.exp2(scores * EXP2_SCALE).astype(BF16)
        acc[...] += mxu(values[:, pl.ds(base, size)], weights)

    def finish(row):
        total = acc[GROUP_WIDTH : GROUP_WIDTH + 1, :]
        lse_ref[0, 0, row : row + 1, :] = jnp.log(total) * math.log2(math.e)
        return diagonal(acc[:GROUP_WIDTH, :] * (1.0 / total))

    acc[...] = jnp.zeros_like(acc)
    over_tiles(start_ref[s, j], count_ref[s, j], tile)
    self_out = finish(0)
    acc[...] = jnp.zeros_like(acc)
    tile(pl.multiple_of(self_rows + clip_ref[s, j] * CTX, 128), CTX)
    text_out = finish(1)
    self_ref[0, 0] = self_out
    text_ref[0, 0] = text_out
    mixes[j] = (self_out + gate_ref[...] * text_out).astype(BF16)

    @pl.when(j == pl.num_programs(1) - 1)
    def _():
        for g, ref in enumerate(mixed_refs):
            for c in range(2):
                at = (2 * g + c) * frames
                ref[c] = joined([mixes[at + f] for f in range(frames)], 1)


def attn_bwd_kernel(*refs, pieces, groups, frames, chunk_text):
    rank_ref, start_ref, count_ref, clip_ref, place_ref = refs[:5]
    refs = refs[5:]
    kv_refs, refs = refs[:pieces], refs[pieces:]
    q_refs, refs = refs[:groups], refs[groups:]
    grad_refs, refs = refs[:groups], refs[groups:]
    self_ref, text_ref, lse_ref, gate_ref, mask_ref, dq_ref = refs[:6]
    dkv_refs, refs = refs[6 : 6 + pieces], refs[6 + pieces :]
    dgate_ref, keys, keys_flip, values, dkeys, dvalues, dquery, queries, grads = refs
    s = pl.program_id(0)
    j = pl.program_id(1)
    self_rows = pieces * 2 * frames * FRAME_TOK
    text_rows = pieces * 2 * chunk_text
    K = slice(0, GROUP_WIDTH)
    V = slice(GROUP_WIDTH, 2 * GROUP_WIDTH)

    @pl.when(jnp.logical_and(s == 0, j == 0))
    def _():
        dgate_ref[...] = jnp.zeros_like(dgate_ref)

    @pl.when(j == 0)
    def _():
        dkeys[...] = jnp.zeros_like(dkeys)
        dvalues[...] = jnp.zeros_like(dvalues)

        def frame_body(ref, c, rows, at):
            keys[pl.ds(at, FRAME_TOK), :] = ref[c, rows, K]
            keys_flip[:, pl.ds(at, FRAME_TOK)] = jnp.transpose(ref[c, rows, K])
            values[pl.ds(at, FRAME_TOK), :] = ref[c, rows, V]

        def text_body(ref, c, rows, at):
            keys[pl.ds(at, chunk_text), :] = ref[c, rows, K]
            values[pl.ds(at, chunk_text), :] = ref[c, rows, V]

        each_chunk(
            kv_refs, rank_ref, place_ref, s, frames, chunk_text, self_rows, frame_body, text_body
        )
        for b in range(text_rows // 128):
            rows = slice(self_rows + 128 * b, self_rows + 128 * (b + 1))
            keys_flip[:, rows] = jnp.transpose(keys[rows, :])
        unpack_frames(q_refs, queries, frames)
        unpack_frames(grad_refs, grads, frames)

    mask = mask_ref[...]
    query = stacked(queries[j], mask)
    grad_low = grads[j]
    grad_wide = grad_low.astype(F32)
    grad_text = (grad_wide * gate_ref[...]).astype(BF16)
    text_out = text_ref[0, 0]
    dgate_ref[...] += jnp.sum(grad_wide * text_out, axis=0, keepdims=True)
    dquery[...] = jnp.zeros_like(dquery)

    def over(grad, out, lse):
        grad_stack = stacked(grad, mask)
        delta = head_row(grad.astype(F32) * out)

        def tile(base, size):
            rows = pl.ds(base, size)
            scores = mxu(keys[rows, :], query, ((1,), (1,)))
            weights = jnp.exp2(scores * EXP2_SCALE - lse)
            dweights = mxu(values[rows, :], grad_stack, ((1,), (1,)))
            dscores = (weights * (dweights - delta)).astype(BF16)
            dvalues[rows, :] += mxu(weights.astype(BF16), grad_stack)
            dkeys[rows, :] += mxu(dscores, query)
            dquery[...] += mxu(keys_flip[:, rows], dscores)

        return tile

    over_tiles(start_ref[s, j], count_ref[s, j], over(grad_low, self_ref[0, 0], lse_ref[0, 0, 0:1, :]))
    over(grad_text, text_out, lse_ref[0, 0, 1:2, :])(
        pl.multiple_of(self_rows + clip_ref[s, j] * CTX, 128), CTX
    )
    dq_ref[0, 0] = (diagonal(dquery[...]) * SCALE).astype(BF16)

    @pl.when(j == pl.num_programs(1) - 1)
    def _():
        def frame_body(ref, c, rows, at):
            taken = pl.ds(at, FRAME_TOK)
            ref[c, rows, :] = jnp.concatenate(
                [dkeys[taken, :] * SCALE, dvalues[taken, :]], axis=1
            ).astype(BF16)

        def text_body(ref, c, rows, at):
            taken = pl.ds(at, chunk_text)
            ref[c, rows, :] = jnp.concatenate(
                [dkeys[taken, :] * SCALE, dvalues[taken, :]], axis=1
            ).astype(BF16)

        each_chunk(
            dkv_refs, rank_ref, place_ref, s, frames, chunk_text, self_rows, frame_body, text_body
        )


def attention_specs(kv, query):
    _, streams, chunk_rows, _ = kv[0].shape
    frames = query[0].shape[3] // GROUP_WIDTH
    chunk_text = chunk_rows - frames * FRAME_TOK
    sizes = dict(pieces=len(kv), groups=len(query), frames=frames, chunk_text=chunk_text)
    count = len(query) * 2 * frames
    grid = (streams, count)
    piece = lambda shape: pl.BlockSpec(
        (2, None) + shape, lambda s, j, *_: (0, s, 0, 0), pipeline_mode=pl.Buffered(1)
    )
    kv_spec = piece((chunk_rows, 2 * GROUP_WIDTH))
    q_spec = piece((FRAME_TOK, frames * GROUP_WIDTH))
    tok_spec = pl.BlockSpec((1, 1, FRAME_TOK, GROUP_WIDTH), lambda s, j, *_: (s, j, 0, 0))
    lse_spec = pl.BlockSpec((1, 1, 2, STACK), lambda s, j, *_: (s, j, 0, 0))
    const_specs = [whole_spec((1, GROUP_WIDTH)), whole_spec((STACK, GROUP_WIDTH))]
    return sizes, grid, kv_spec, q_spec, tok_spec, lse_spec, const_specs


def stack_mask():
    head_of_row = np.arange(STACK) // FRAME_TOK
    head_of_lane = np.arange(GROUP_WIDTH) // HD
    return jnp.asarray((head_of_row[:, None] == head_of_lane[None, :]).astype(np.float32), BF16)


def attn_fwd(tables, kv, query, gate):
    sizes, grid, kv_spec, q_spec, tok_spec, lse_spec, const_specs = attention_specs(kv, query)
    total = len(kv) * 2 * kv[0].shape[2]
    text_rows = len(kv) * 2 * sizes["chunk_text"]
    wide = jax.ShapeDtypeStruct(grid + (FRAME_TOK, GROUP_WIDTH), F32)
    got = call(
        functools.partial(attn_fwd_kernel, **sizes),
        "attention",
        grid,
        5,
        [kv_spec] * len(kv) + [q_spec] * len(query) + const_specs,
        [q_spec] * len(query) + [tok_spec, tok_spec, lse_spec],
        [jax.ShapeDtypeStruct(q.shape, BF16) for q in query]
        + [wide, wide, jax.ShapeDtypeStruct(grid + (2, STACK), F32)],
        [
            pltpu.VMEM((total, GROUP_WIDTH), BF16),
            pltpu.VMEM((GROUP_WIDTH + ONES_ROWS, total), BF16),
            pltpu.VMEM((text_rows, GROUP_WIDTH), BF16),
            pltpu.VMEM((grid[1], FRAME_TOK, GROUP_WIDTH), BF16),
            pltpu.VMEM((grid[1], FRAME_TOK, GROUP_WIDTH), BF16),
            pltpu.VMEM((GROUP_WIDTH + ONES_ROWS, STACK), F32),
        ],
        min(60 * MIB, total * 2600 + 16 * MIB),
        grid[0] * grid[1] * STACK * 2304 * GROUP_WIDTH * 8,
        grid[0] * grid[1] * 300000,
        (*tables, *kv, *query, gate, stack_mask()),
    )
    return got[: len(query)], got[len(query) :]


def attn_bwd(tables, kv, query, grad, kept, gate):
    sizes, grid, kv_spec, q_spec, tok_spec, lse_spec, const_specs = attention_specs(kv, query)
    total = len(kv) * 2 * kv[0].shape[2]
    got = call(
        functools.partial(attn_bwd_kernel, **sizes),
        "attention_back",
        grid,
        5,
        [kv_spec] * len(kv)
        + [q_spec] * (2 * len(query))
        + [tok_spec, tok_spec, lse_spec]
        + const_specs,
        [tok_spec] + [kv_spec] * len(kv) + [whole_spec((1, GROUP_WIDTH))],
        [jax.ShapeDtypeStruct(grid + (FRAME_TOK, GROUP_WIDTH), BF16)]
        + [jax.ShapeDtypeStruct(v.shape, BF16) for v in kv]
        + [jax.ShapeDtypeStruct((1, GROUP_WIDTH), F32)],
        [
            pltpu.VMEM((total, GROUP_WIDTH), BF16),
            pltpu.VMEM((GROUP_WIDTH, total), BF16),
            pltpu.VMEM((total, GROUP_WIDTH), BF16),
            pltpu.VMEM((total, GROUP_WIDTH), F32),
            pltpu.VMEM((total, GROUP_WIDTH), F32),
            pltpu.VMEM((GROUP_WIDTH, STACK), F32),
            pltpu.VMEM((grid[1], FRAME_TOK, GROUP_WIDTH), BF16),
            pltpu.VMEM((grid[1], FRAME_TOK, GROUP_WIDTH), BF16),
        ],
        min(62 * MIB, total * 5800 + 16 * MIB),
        grid[0] * grid[1] * STACK * 2304 * GROUP_WIDTH * 20,
        grid[0] * grid[1] * 500000,
        (*tables, *kv, *query, *grad, *kept, gate, stack_mask()),
    )
    return got[0], got[1 : 1 + len(kv)], got[-1]


def for_group(group, groups, body):
    for v in range(groups):

        @pl.when(group == v)
        def _(v=v):
            body(v)


def out_kernel(info_ref, *refs, half, groups, frames):
    own_refs, refs = refs[:groups], refs[groups:]
    other_ref, w_ref, mixed_ref, first_ref, rest_ref = refs
    k = pl.program_id(0)
    here = (k // half) == info_ref[0]

    def fill(v, take):
        for s in range(groups):
            piece = take(s)
            for f in range(frames):
                mixed_ref[0, FRAME_TOK * f : FRAME_TOK * (f + 1), GROUP_WIDTH * (v ^ s) : GROUP_WIDTH * ((v ^ s) + 1)] = piece[
                    :, GROUP_WIDTH * f : GROUP_WIDTH * (f + 1)
                ]

    @pl.when(here)
    def _():
        for_group(info_ref[1], groups, lambda v: fill(v, lambda s: own_refs[s][0, 0]))

    @pl.when(jnp.logical_not(here))
    def _():
        for_group(info_ref[1], groups, lambda v: fill(v, lambda s: other_ref[s, 0]))

    part = mxu(mixed_ref[0], w_ref[...])

    @pl.when(k == 0)
    def _():
        first_ref[...] = part

    @pl.when(k > 0)
    def _():
        rest_ref[0] = part.astype(BF16)


def out_project(info, own, other, w_out, streams, tokens):
    groups = len(own)
    half = streams // 2
    frames = tokens // FRAME_TOK
    own_width, width = w_out.shape
    lanes = frames * GROUP_WIDTH
    return call(
        functools.partial(out_kernel, half=half, groups=groups, frames=frames),
        "out_project",
        (streams,),
        1,
        [pl.BlockSpec((1, 1, FRAME_TOK, lanes), lambda k, _: (0, k % half, 0, 0))] * groups
        + [
            pl.BlockSpec((groups, 1, FRAME_TOK, lanes), lambda k, _: (0, k % half, 0, 0)),
            whole_spec(w_out.shape),
        ],
        [
            pl.BlockSpec((1, tokens, own_width), lambda k, _: (k, 0, 0)),
            whole_spec((tokens, width)),
            pl.BlockSpec((1, tokens, width), lambda k, _: (jnp.maximum(k - 1, 0), 0, 0)),
        ],
        [
            jax.ShapeDtypeStruct((streams, tokens, own_width), BF16),
            jax.ShapeDtypeStruct((tokens, width), F32),
            jax.ShapeDtypeStruct((streams - 1, tokens, width), BF16),
        ],
        [],
        32 * MIB,
        2 * streams * tokens * own_width * width,
        streams * tokens * width * 6 + w_out.size * 2,
        (info, *own, other, w_out),
    )


def out_back_kernel(core_ref, grad_ref, w_ref, send_ref, keep_ref, *, half, groups, frames):
    step = pl.program_id(0)
    grad = mxu(grad_ref[0], w_ref[...], ((1,), (1,))).astype(BF16)

    def put(ref):
        for g in range(groups):
            ref[0, g] = packed_frames(group_cut(grad, g), frames)

    @pl.when(step < half)
    def _():
        put(send_ref)

    @pl.when(step >= half)
    def _():
        put(keep_ref)


def out_back(core, grad, w_out, groups):
    streams, tokens, width = grad.shape
    half = streams // 2
    frames = tokens // FRAME_TOK
    block = (1, groups, FRAME_TOK, frames * GROUP_WIDTH)
    return call(
        functools.partial(out_back_kernel, half=half, groups=groups, frames=frames),
        "out_back",
        (streams,),
        1,
        [
            pl.BlockSpec((1, tokens, width), lambda i, core: (set_stream(i, core[0], half), 0, 0)),
            whole_spec(w_out.shape),
        ],
        [
            pl.BlockSpec(block, lambda i, core: (jnp.minimum(i, half - 1), 0, 0, 0)),
            pl.BlockSpec(block, lambda i, core: (jnp.maximum(i - half, 0), 0, 0, 0)),
        ],
        [jax.ShapeDtypeStruct((half,) + block[1:], BF16)] * 2,
        [],
        32 * MIB,
        2 * streams * tokens * w_out.size,
        streams * tokens * width * 3 + w_out.size * 2,
        (core, grad, w_out),
    )


def proj_back_kernel(*refs, groups, frames, half, chunk_text):
    group_ref, x_ref, w_ref, dq_ref = refs[:4]
    dkv_refs, refs = refs[4 : 4 + groups], refs[4 + groups :]
    cos_ref, sin_ref, gain_ref, ones_ref = refs[:4]
    out_refs, refs = refs[4 : 4 + groups], refs[4 + groups :]
    dw_ref, dgain_ref, dkv, total = refs
    i = pl.program_id(0)
    tokens = frames * FRAME_TOK

    @pl.when(i == 0)
    def _():
        total[...] = jnp.zeros_like(total)
        dgain_ref[...] = jnp.zeros_like(dgain_ref)

    for g, ref in enumerate(dkv_refs):

        @pl.when(i // half == g)
        def _(ref=ref):
            dkv[...] = ref[...]

    ones = ones_ref[...]
    x = jnp.concatenate([x_ref[0, c, 0] for c in range(2)], axis=0)
    raw = mxu(x, w_ref[...])
    key_grad = jnp.concatenate([dkv[c, :tokens, :GROUP_WIDTH] for c in range(2)], axis=0)
    value_grad = jnp.concatenate([dkv[c, :tokens, GROUP_WIDTH:] for c in range(2)], axis=0)
    query_grad = jnp.concatenate([dq_ref[0, n] for n in range(2 * frames)], axis=0)
    turned = jnp.concatenate([query_grad, key_grad], axis=1).astype(F32)
    done = []
    for t, (x_t, dy) in enumerate(zip(tiles_of(raw), tiles_of(turned))):
        dy = turn(dy, cos_ref[0, 0], -sin_ref[0, 0])
        inv = lax.rsqrt(head_means(x_t * x_t, ones) + EPSILON)
        unit = x_t * inv
        lanes = slice(128 * t, 128 * (t + 1))
        dgain_ref[0:1, lanes] += jnp.sum(dy * unit, axis=0, keepdims=True)
        dn = dy * gain_ref[0:1, lanes]
        done.append((inv * (dn - unit * head_means(dn * unit, ones))).astype(BF16))
    grads = jnp.concatenate(done + [value_grad], axis=1)
    total[...] += mxu(grads, x, ((0,), (0,)))

    def put(ref):
        for c in range(2):
            ref[c, :FRAME_TOK, :] = packed_frames(grads[tokens * c : tokens * (c + 1)], frames)
            rows = slice(tokens, tokens + chunk_text)
            text = dkv[c, rows, :]
            lower = chunk_text // 2
            ref[c, FRAME_TOK:, : 4 * GROUP_WIDTH] = jnp.concatenate(
                [text[:lower], text[lower:]], axis=1
            )
            ref[c, FRAME_TOK:, 4 * GROUP_WIDTH :] = jnp.zeros(
                (lower, ref.shape[2] - 4 * GROUP_WIDTH), BF16
            )

    for g, ref in enumerate(out_refs):

        @pl.when(i // half == g)
        def _(ref=ref):
            put(ref)

    @pl.when(i == pl.num_programs(0) - 1)
    def _():
        for b in range(total.shape[1] // 256):
            lanes = slice(256 * b, 256 * (b + 1))
            dw_ref[lanes, :] = jnp.transpose(total[:, lanes]).astype(BF16)


def proj_back(group, x, w_tri, dq, dkv, cosine, sine, gains):
    groups = len(dkv)
    half = x.shape[2]
    tokens, width = x.shape[3:]
    frames = tokens // FRAME_TOK
    chunk_text = dkv[0].shape[2] - tokens
    lanes = frames * 3 * GROUP_WIDTH
    rows = FRAME_TOK + chunk_text // 2
    got = call(
        functools.partial(
            proj_back_kernel, groups=groups, frames=frames, half=half, chunk_text=chunk_text
        ),
        "proj_back",
        (groups * half,),
        1,
        [
            pl.BlockSpec(
                (1, 2, 1, tokens, width), lambda i, g: (g[0] ^ (i // half), 0, i % half, 0, 0)
            ),
            whole_spec(w_tri.shape),
            pl.BlockSpec(
                (1, 2 * frames, FRAME_TOK, GROUP_WIDTH), lambda i, g: (i % half, i // half, 0, 0)
            ),
        ]
        + [
            pl.BlockSpec((2, None) + dkv[0].shape[2:], lambda i, g: (0, i % half, 0, 0))
        ]
        * groups
        + [
            pl.BlockSpec((1, 1, 2 * tokens, 128), lambda i, g: (i // half, i % half, 0, 0)),
            pl.BlockSpec((1, 1, 2 * tokens, 128), lambda i, g: (i // half, i % half, 0, 0)),
            whole_spec(gains.shape),
            whole_spec((128, 128)),
        ],
        [
            pl.BlockSpec(
                (2, None, rows, lanes),
                lambda i, g, n=n: (0, jnp.clip(i - n * half, 0, half - 1), 0, 0),
            )
            for n in range(groups)
        ]
        + [whole_spec((width, 3 * GROUP_WIDTH)), whole_spec((8, 2 * GROUP_WIDTH))],
        [jax.ShapeDtypeStruct((2, half, rows, lanes), BF16)] * groups
        + [
            jax.ShapeDtypeStruct((width, 3 * GROUP_WIDTH), BF16),
            jax.ShapeDtypeStruct((8, 2 * GROUP_WIDTH), F32),
        ],
        [
            pltpu.VMEM(dkv[0].shape[:1] + dkv[0].shape[2:], BF16),
            pltpu.VMEM((3 * GROUP_WIDTH, width), F32),
        ],
        48 * MIB,
        2 * x.size * GROUP_WIDTH * 5,
        x.size * 4 + w_tri.size * 2,
        (group, x, w_tri, dq, *dkv, cosine, sine, gains, head_ones()),
    )
    return got[:groups], got[groups], got[groups + 1]


def in_back_kernel(info_ref, *refs, half, groups, frames, own_width, chunk_text):
    own_refs, refs = refs[:groups], refs[groups:]
    other_ref, w_ref, raw_ref, gain_ref, ones_ref = refs[:5]
    first_ref, rest_ref, text_ref, dgain_ref, grads, texts = refs[5:]
    k = pl.program_id(0)
    here = (k // half) == info_ref[0]
    wide = lane_tiles(own_width)
    lower = chunk_text // 2

    @pl.when(k == 0)
    def _():
        dgain_ref[...] = jnp.zeros_like(dgain_ref)
        texts[...] = jnp.zeros_like(texts)

    def fill(v, take):
        for s in range(groups):
            piece = take(s)
            at = GROUP_WIDTH * (v ^ s)
            for f in range(frames):
                for p in range(3):
                    from_lane = GROUP_WIDTH * (3 * f + p)
                    grads[
                        FRAME_TOK * f : FRAME_TOK * (f + 1),
                        own_width * p + at : own_width * p + at + GROUP_WIDTH,
                    ] = piece[:FRAME_TOK, from_lane : from_lane + GROUP_WIDTH]
            for f in range(2):
                for p in range(2):
                    from_lane = GROUP_WIDTH * (2 * f + p)
                    texts[lower * f : lower * (f + 1), wide * p + at : wide * p + at + GROUP_WIDTH] = piece[
                        FRAME_TOK:, from_lane : from_lane + GROUP_WIDTH
                    ].astype(F32)

    @pl.when(here)
    def _():
        for_group(info_ref[1], groups, lambda v: fill(v, lambda s: own_refs[s][0, 0]))

    @pl.when(jnp.logical_not(here))
    def _():
        for_group(info_ref[1], groups, lambda v: fill(v, lambda s: other_ref[s, 0]))

    part = mxu(grads[...], w_ref[...], ((1,), (1,)))

    @pl.when(k == 0)
    def _():
        first_ref[...] = part

    @pl.when(k > 0)
    def _():
        rest_ref[0] = part.astype(BF16)

    ones = ones_ref[...]
    for t in range(wide // 128):
        lanes = slice(128 * t, 128 * (t + 1))
        x = raw_ref[0, :, lanes]
        dy = texts[:, lanes]
        inv = lax.rsqrt(head_means(x * x, ones) + EPSILON)
        unit = x * inv
        dgain_ref[0:1, :] += jnp.sum(dy * unit, axis=0, keepdims=True)
        dn = dy * gain_ref[2:3, :]
        text_ref[0, :, lanes] = (inv * (dn - unit * head_means(dn * unit, ones))).astype(BF16)
    text_ref[0, :, wide:] = texts[:, wide:].astype(BF16)


def in_back(info, own, other, w_cols, text_raw, gains, tokens):
    streams, chunk_text, text_lanes = text_raw.shape
    groups = len(own)
    half = streams // 2
    frames = tokens // FRAME_TOK
    width = w_cols.shape[0]
    own_width = w_cols.shape[1] // 3
    rows, lanes = own[0].shape[2:]
    return call(
        functools.partial(
            in_back_kernel,
            half=half,
            groups=groups,
            frames=frames,
            own_width=own_width,
            chunk_text=chunk_text,
        ),
        "in_back",
        (streams,),
        1,
        [pl.BlockSpec((1, 1, rows, lanes), lambda k, _: (0, k % half, 0, 0))] * groups
        + [
            pl.BlockSpec((groups, 1, rows, lanes), lambda k, _: (0, k % half, 0, 0)),
            whole_spec(w_cols.shape),
            pl.BlockSpec((1, chunk_text, text_lanes), lambda k, _: (k, 0, 0)),
            whole_spec((8, 128)),
            whole_spec((128, 128)),
        ],
        [
            whole_spec((tokens, width)),
            pl.BlockSpec((1, tokens, width), lambda k, _: (jnp.maximum(k - 1, 0), 0, 0)),
            pl.BlockSpec((1, chunk_text, text_lanes), lambda k, _: (k, 0, 0)),
            whole_spec((8, 128)),
        ],
        [
            jax.ShapeDtypeStruct((tokens, width), F32),
            jax.ShapeDtypeStruct((streams - 1, tokens, width), BF16),
            jax.ShapeDtypeStruct(text_raw.shape, BF16),
            jax.ShapeDtypeStruct((8, 128), F32),
        ],
        [
            pltpu.VMEM((tokens, 3 * own_width), BF16),
            pltpu.VMEM((chunk_text, text_lanes), F32),
        ],
        48 * MIB,
        2 * streams * tokens * w_cols.size,
        streams * tokens * width * 6 + w_cols.size * 2,
        (info, *own, other, w_cols, text_raw, gains, head_ones()),
    )


def weights_kernel(*refs, tiles, streams):
    cut = [refs[streams * n : streams * (n + 1)] for n in range(5)]
    x_refs, g_refs, gate_refs, up_refs, hidden_refs = cut
    out_ref, x_flip, g_flip = refs[5 * streams :]
    i = pl.program_id(0)
    rows = x_refs[0].shape[0]

    @pl.when(i == 0)
    def _():
        for k in range(streams):
            x_flip[:, rows * k : rows * (k + 1)] = jnp.transpose(x_refs[k][...])
            g_flip[:, rows * k : rows * (k + 1)] = jnp.transpose(g_refs[k][...])

    def total(flip, refs):
        right = joined([ref[...] for ref in refs], 0)
        out_ref[...] = mxu(flip[...], right).astype(BF16)

    @pl.when(i < tiles)
    def _():
        total(x_flip, gate_refs)

    @pl.when(jnp.logical_and(i >= tiles, i < 2 * tiles))
    def _():
        total(x_flip, up_refs)

    @pl.when(i >= 2 * tiles)
    def _():
        total(g_flip, hidden_refs)


def ffn_weights(x, g, gate, up, hidden):
    streams = len(x)
    rows, width = x[0].shape
    inner = hidden[0].shape[1]
    tile = min(512, inner)
    tiles = inner // tile
    at = lambda first: pl.BlockSpec(
        (rows, tile), lambda i: (0, jnp.clip(i - first * tiles, 0, tiles - 1))
    )
    return call(
        functools.partial(weights_kernel, tiles=tiles, streams=streams),
        "ffn_weights",
        (3 * tiles,),
        0,
        [whole_spec((rows, width))] * (2 * streams)
        + [at(0)] * streams
        + [at(1)] * streams
        + [at(2)] * streams,
        pl.BlockSpec((width, tile), lambda i: (0, i)),
        jax.ShapeDtypeStruct((width, 3 * inner), BF16),
        [pltpu.VMEM((width, streams * rows), BF16)] * 2,
        56 * MIB,
        6 * streams * rows * width * inner,
        6 * width * inner + 10 * streams * rows * width,
        (*x, *g, *gate, *up, *hidden),
    )


def unit_rms(values):
    inv = lax.rsqrt(jnp.mean(values * values, axis=-1, keepdims=True) + EPSILON)
    return values * inv, inv


def unit_back(grad_unit, unit, inv):
    return inv * (grad_unit - unit * jnp.mean(grad_unit * unit, axis=-1, keepdims=True))


def rope_lanes(frames):
    half = HD // 2
    frame_pairs = HD // 8
    row_pairs = (half - frame_pairs) // 2
    col_pairs = half - frame_pairs - row_pairs
    pair = (np.arange(128) % HD) // 2

    def lanes(first, count):
        freq = 10000.0 ** (-(np.arange(count, dtype=np.float32)) / np.float32(count))
        out = np.zeros((128,), np.float32)
        inside = (pair >= first) & (pair < first + count)
        out[inside] = freq.astype(np.float32)[pair[inside] - first]
        return jnp.asarray(out)[None, :]

    rows = frames.shape[0]
    inner = jnp.arange(rows) % FRAME_TOK
    row_pos = (inner // PW).astype(F32)
    col_pos = (inner % PW).astype(F32)
    angle = (
        frames[:, None] * lanes(0, frame_pairs)
        + row_pos[:, None] * lanes(frame_pairs, row_pairs)
        + col_pos[:, None] * lanes(frame_pairs + row_pairs, col_pairs)
    )
    sign = jnp.asarray(np.where(np.arange(128) % 2 == 0, -1.0, 1.0).astype(np.float32))[None, :]
    return jnp.cos(angle), jnp.sin(angle) * sign


def gain_rows(*gains):
    rows = [jnp.concatenate([g, g]) for g in gains]
    rows += [jnp.zeros((128,), F32)] * (8 - len(rows))
    return jnp.stack(rows)


def pad_parts(values, parts):
    width = values.shape[-1] // parts
    wide = lane_tiles(width)
    if wide == width:
        return values
    cut = values.reshape(values.shape[:-1] + (parts, width))
    cut = jnp.pad(cut, [(0, 0)] * (cut.ndim - 1) + [(0, wide - width)])
    return cut.reshape(values.shape[:-1] + (parts * wide,))


def pick(values, index, axis=0):
    return lax.dynamic_index_in_dim(values, index, axis, keepdims=False)


def beside(value, *others):
    return lax.optimization_barrier((value,) + others)


def held(value, *others):
    return lax.optimization_barrier((value,) + others)[0]


def per_device(
    fsdp,
    dps,
    states,
    cotangent,
    segment_ids,
    frame_ids,
    condition,
    context,
    w_modulate,
    w_qkv,
    w_text_kv,
    w_out,
    w_gate_up,
    w_down,
    gain_attn_in,
    gain_attn_out,
    gain_ffn_in,
    gain_ffn_out,
    gain_query,
    gain_key,
    gain_text_key,
    cross_gate,
):
    xs = Moves("fsdp", fsdp)
    ds = Moves("dp", dps)
    rows_in = states[0]
    tokens, width = rows_in.shape
    frames = tokens // FRAME_TOK
    heads = cross_gate.shape[0]
    own_heads = heads // fsdp
    own_width = own_heads * HD
    groups = own_heads // GROUP_HEADS
    ranks = dps // groups
    rank_bits = ranks.bit_length() - 1
    clips = condition.shape[1]
    text_local = context[0]
    text_own = text_local.shape[0]
    half = fsdp // 2
    group_me = ds.me // ranks
    rank_me = ds.me % ranks
    core = ds.me % 2

    def frame_view(values):
        return values.reshape(frames, FRAME_TOK, values.shape[-1])

    def group_swap(pieces):
        return [pieces[0]] + [ds.swap(pieces[s], s * ranks) for s in range(1, groups)]

    def group_exchange(keep, send, *first):
        other = ds.swap(send, 1)
        pieces = [
            jnp.stack([pick(keep, group_me ^ s, 1), pick(other, group_me ^ s, 1)])
            for s in range(groups)
        ]
        return group_swap([held(piece, *first) for piece in pieces])

    def group_return(pieces):
        own = group_swap(pieces)
        return own, ds.swap(jnp.stack([piece[1] for piece in own]), 1)

    own_frames = segment_ids[0][::FRAME_TOK].astype(F32)
    own_frame_ids = frame_ids[0].reshape(frames, FRAME_TOK)[:, 0].astype(F32)
    met = jnp.stack(xs.gather(jnp.concatenate([own_frames, own_frame_ids])))
    core_info = core.astype(jnp.int32)[None]
    group_info = group_me.astype(jnp.int32)[None]
    both_info = jnp.concatenate([core_info, group_info])

    silu_cond = jax.nn.silu(condition[0]).astype(BF16)
    cond_rel = jnp.concatenate(xs.gather(silu_cond))
    rows = w_qkv.shape[0]
    quarter = rows // 4

    def columns_of(weight, first, count, s):
        return jnp.concatenate(
            [
                lax.dynamic_slice(
                    weight, (first, p * width + (xs.me ^ s) * own_width), (count, own_width)
                )
                for p in range(3)
            ],
            axis=1,
        )

    fetched = []
    for s in range(1, fsdp):
        wanted = columns_of(w_qkv, (ds.me % 4) * quarter, quarter, s)
        wanted, cond_rel = beside(wanted, cond_rel)
        quarters = [(0, xs.swap(wanted, s))]
        for mask in (2, 1):
            quarters += [(m ^ mask, ds.swap(v, mask)) for m, v in quarters]
        fetched += [(s, m, v) for m, v in quarters]
    cond_own = xs.own_block(cond_rel, 1)
    mod_part = mxu(cond_own, w_modulate).reshape(fsdp, clips, -1)
    modulation = mod_part[0]
    for s in range(1, fsdp):
        modulation = modulation + xs.swap(mod_part[s], s)

    own_seg = lax.dynamic_slice_in_dim(own_frames, ds.me * frames, frames)
    onehot = (own_seg[:, None] == jnp.arange(clips, dtype=F32)[None, :]).astype(F32)
    per_frame = jnp.dot(onehot, modulation, precision=HIGHEST)[:, None, :]
    scale_attn, gate_attn, scale_ffn, gate_ffn = jnp.split(per_frame, 4, axis=2)

    states_f = frame_view(rows_in)
    unit_in, inv_in = unit_rms(states_f)
    normed = (unit_in * gain_attn_in * (1.0 + scale_attn)).astype(BF16).reshape(tokens, width)
    normed, met, w_there = beside(normed, met, w_qkv)
    normed_all = jnp.stack(xs.gather(normed))
    w_cols = lax.dynamic_update_slice_in_dim(
        jnp.zeros((width, 3 * own_width), BF16), columns_of(w_there, 0, rows, 0), xs.me * rows, 0
    )
    for s, m, v in fetched:
        at = (xs.me ^ s) * rows + ((ds.me % 4) ^ m) * quarter
        w_cols = lax.dynamic_update_slice_in_dim(w_cols, v, at, 0)

    stream_seg = met[:, : own_frames.shape[0]].astype(jnp.int32)
    rel_frame_ids = met[:, own_frames.shape[0] :]
    core_seg = lax.dynamic_slice_in_dim(stream_seg, core * half, half, 0)
    masks = [s * ranks for s in range(groups)]
    for b in reversed(range(1, rank_bits)):
        masks = masks + [m ^ (1 << b) for m in masks]
    place_dev = jnp.stack([ds.me ^ (m ^ c) for m in masks for c in range(2)])
    q_dev = jnp.stack([ds.me ^ (s * ranks ^ c) for s in range(groups) for c in range(2)])
    in_frames = lambda dev: (dev[:, None] * frames + jnp.arange(frames)[None, :]).reshape(-1)
    kv_seg = jnp.take(core_seg, in_frames(place_dev), axis=1)
    q_seg = jnp.take(core_seg, in_frames(q_dev), axis=1)
    order = jnp.arange(kv_seg.shape[1])
    less = kv_seg[:, None, :] < kv_seg[:, :, None]
    tie = (kv_seg[:, None, :] == kv_seg[:, :, None]) & (order[None, None, :] < order[None, :, None])
    kv_rank = jnp.sum((less | tie).astype(jnp.int32), axis=2)
    q_start = jnp.sum((kv_seg[:, None, :] < q_seg[:, :, None]).astype(jnp.int32), axis=2)
    q_count = jnp.sum((kv_seg[:, None, :] == q_seg[:, :, None]).astype(jnp.int32), axis=2)
    tables = (kv_rank, q_start, q_count, jnp.maximum(q_seg, 0), place_dev.astype(jnp.int32))
    cosine, sine = rope_lanes(jnp.repeat(rel_frame_ids, FRAME_TOK, axis=1).reshape(-1))
    cosine = cosine.reshape(fsdp, tokens, 128)
    sine = sine.reshape(fsdp, tokens, 128)

    text_rel = jnp.concatenate(
        [xs.own_block(text_local, 1)]
        + [xs.swap(xs.own_block(text_local, 1, s), s) for s in range(1, fsdp)]
    )
    text_part = mxu(text_rel, w_text_kv).reshape(fsdp, text_own, 2, fsdp, own_width)
    text_raw = pick(text_part, xs.me, 3)
    for s in range(1, fsdp):
        piece = pick(text_part, xs.me ^ s, 3)
        piece = jnp.stack([piece[s ^ k] for k in range(fsdp)])
        text_raw = text_raw + xs.swap(piece.astype(BF16), s).astype(F32)
    text_raw = pad_parts(text_raw.reshape(fsdp, text_own, 2 * own_width), 2)

    gains = gain_rows(gain_query, gain_key, gain_text_key)
    send_q, send_kv, keep_q, keep_kv = make_heads(
        core_info, normed_all, w_cols, text_raw, cosine, sine, gains, groups
    )

    kv = group_exchange(keep_kv, send_kv)
    kv_first = kv[1:]
    for b in reversed(range(1, rank_bits)):
        kv = kv + [ds.swap(v, 1 << b) for v in kv]
    query = group_exchange(keep_q, send_q, *kv_first)
    tanh_gate = jnp.tanh(cross_gate)
    first_head = xs.me * own_heads + group_me * GROUP_HEADS
    gate_row = jnp.repeat(lax.dynamic_slice_in_dim(tanh_gate, first_head, GROUP_HEADS), HD)[None, :]

    mixed, kept = attn_fwd(tables, kv, query, gate_row)
    mixed_own, mixed_other = group_return(mixed)
    mixed_low, mix_first, mix_rest = out_project(
        both_info, mixed_own, mixed_other, w_out, fsdp, tokens
    )

    def swapped_sum(first, rest):
        for s in range(1, fsdp):
            first = first + xs.swap(rest[s - 1], s).astype(F32)
        return first

    late_ids = held(rel_frame_ids, mix_first)
    set_of = lambda values, which: lax.dynamic_slice_in_dim(values, which * half, half, 0)
    near_ids = jnp.stack(
        [set_of(late_ids, core), ds.swap(set_of(late_ids, 1 - core), 1)], axis=1
    )
    far_ids = jnp.stack([near_ids] + [ds.swap(near_ids, s * ranks) for s in range(1, groups)])
    normed_two = jnp.stack(
        [set_of(normed_all, core), ds.swap(set_of(normed_all, 1 - core), 1)]
    )
    late_normed = held(normed_two, *mixed_own)
    text_every = lax.all_gather(held(text_rel, *mixed_own), "dp", axis=0, tiled=True)
    if groups > 1:
        members = [[g * ranks + r for g in range(groups)] for r in range(ranks)]
        normed_group = lax.all_gather(late_normed, "dp", axis_index_groups=members)
    else:
        normed_group = late_normed[None]
    far_cos, far_sin = rope_lanes(jnp.repeat(far_ids.reshape(-1), FRAME_TOK))
    far_shape = (groups, half, 2 * tokens, 128)
    far_cos = far_cos.reshape(far_shape)
    far_sin = far_sin.reshape(far_shape)
    mix_got = [xs.swap(mix_rest[s - 1], s) for s in range(1, fsdp)]
    mix_got = [held(v, far_cos, far_sin) for v in mix_got]
    for v in mix_got:
        mix_first = mix_first + v.astype(F32)
    mixed_out = frame_view(mix_first)
    unit_mix, inv_mix = unit_rms(mixed_out)
    tanh_attn = jnp.tanh(gate_attn)
    after = states_f + tanh_attn * unit_mix * gain_attn_out
    unit_ffn, inv_ffn = unit_rms(after)
    ffn_low = (unit_ffn * gain_ffn_in * (1.0 + scale_ffn)).astype(BF16).reshape(tokens, width)
    ffn_all = xs.gather(ffn_low)
    gate_part = [mxu(x, w_gate_up[0]) for x in ffn_all]
    up_part = [mxu(x, w_gate_up[1]) for x in ffn_all]
    hidden = [(jax.nn.silu(g) * u).astype(BF16) for g, u in zip(gate_part, up_part)]
    ffn_out = swapped_sum(
        mxu(hidden[0], w_down), [mxu(h, w_down).astype(BF16) for h in hidden[1:]]
    )
    ffn_out = frame_view(ffn_out)
    unit_out, inv_out = unit_rms(ffn_out)
    tanh_ffn = jnp.tanh(gate_ffn)
    output = after + tanh_ffn * unit_out * gain_ffn_out

    def frame_sum(values):
        return jnp.sum(values, axis=1)

    cot = frame_view(cotangent[0])
    cot_unit = frame_sum(cot * unit_out)
    grad_gate_ffn = cot_unit * gain_ffn_out * (1.0 - tanh_ffn[:, 0] ** 2)
    grad_gain_ffn_out = jnp.sum(cot_unit * tanh_ffn[:, 0], axis=0)
    grad_ffn_low = (
        unit_back(cot * (tanh_ffn * gain_ffn_out), unit_out, inv_out)
        .astype(BF16)
        .reshape(tokens, width)
    )
    grad_ffn_all = xs.gather(grad_ffn_low)
    grad_gate = []
    grad_up = []
    for g, u, d in zip(gate_part, up_part, grad_ffn_all):
        grad_hidden = mxu(d, w_down, ((1,), (1,)))
        sig = jax.nn.sigmoid(g)
        grad_gate.append((grad_hidden * u * (sig * (1.0 + g * (1.0 - sig)))).astype(BF16))
        grad_up.append((grad_hidden * (g * sig)).astype(BF16))

    def ffn_in_part(s):
        return mxu(grad_gate[s], w_gate_up[0], ((1,), (1,))) + mxu(
            grad_up[s], w_gate_up[1], ((1,), (1,))
        )

    def reduce_rows(term):
        return lax.psum_scatter(term, "dp", scatter_dimension=0, tiled=True).astype(F32)

    ffn_rest = [xs.swap(ffn_in_part(s).astype(BF16), s) for s in range(1, fsdp)]
    ffn_grads = ffn_weights(ffn_all, grad_ffn_all, grad_gate, grad_up, hidden)
    ffn_grads, grad_ffn_in, *ffn_rest = beside(ffn_grads, ffn_in_part(0), *ffn_rest)
    for v in ffn_rest:
        grad_ffn_in = grad_ffn_in + v.astype(F32)
    grad_ffn_in = frame_view(grad_ffn_in)
    inner = w_down.shape[0]
    ffn_sums = reduce_rows(ffn_grads)
    grad_unit = frame_sum(grad_ffn_in * unit_ffn)
    grad_scale_ffn = grad_unit * gain_ffn_in
    grad_gain_ffn_in = jnp.sum(grad_unit * (1.0 + scale_ffn[:, 0]), axis=0)
    grad_after = cot + unit_back(
        grad_ffn_in * (gain_ffn_in * (1.0 + scale_ffn)), unit_ffn, inv_ffn
    )
    after_unit = frame_sum(grad_after * unit_mix)
    grad_gate_attn = after_unit * gain_attn_out * (1.0 - tanh_attn[:, 0] ** 2)
    grad_gain_attn_out = jnp.sum(after_unit * tanh_attn[:, 0], axis=0)
    grad_mix_low = (
        unit_back(grad_after * (tanh_attn * gain_attn_out), unit_mix, inv_mix)
        .astype(BF16)
        .reshape(tokens, width)
    )
    grad_mix_all = held(jnp.stack(xs.gather(grad_mix_low)), normed_group, text_every)

    send_grad, keep_grad = out_back(core_info, grad_mix_all, w_out, groups)
    grad_group = group_exchange(keep_grad, send_grad)
    out_grad = mxu(
        grad_mix_all.reshape(fsdp * tokens, width),
        mixed_low.reshape(fsdp * tokens, own_width),
        ((0,), (0,)),
    ).astype(BF16)
    out_grad, *grad_group = beside(out_grad, *grad_group)
    dquery, dkv, dgate = attn_bwd(tables, kv, query, grad_group, kept, gate_row)
    for b in range(1, rank_bits):
        count = len(dkv) // 2
        dkv = [
            (dkv[i].astype(F32) + ds.swap(dkv[count + i], 1 << b).astype(F32)).astype(BF16)
            for i in range(count)
        ]

    w_tri = jnp.concatenate(
        [
            lax.dynamic_slice_in_dim(
                w_cols, p * own_width + group_me * GROUP_WIDTH, GROUP_WIDTH, 1
            )
            for p in range(2)
        ],
        axis=1,
    )
    tri_gain = jnp.concatenate([jnp.tile(gain_query, GROUP_HEADS), jnp.tile(gain_key, GROUP_HEADS)])
    tri_gain = jnp.pad(tri_gain[None, :], ((0, 7), (0, 0)))
    proj_pieces, qkv_grad, gain_qk = proj_back(
        group_info,
        normed_group,
        w_tri,
        dquery,
        dkv,
        far_cos,
        far_sin,
        tri_gain,
    )
    per = width // (fsdp * ranks)
    part = qkv_grad.reshape(fsdp, ranks, per, 3 * GROUP_WIDTH)
    parts = []
    for b in range(rank_bits):
        part = part.reshape(fsdp, part.shape[1] // 2, 2, per, 3 * GROUP_WIDTH)
        mine = (rank_me >> b) & 1
        got = ds.swap(pick(part, 1 - mine, 2), 1 << b)
        part = (pick(part, mine, 2).astype(F32) + got.astype(F32)).astype(BF16)
        parts.append(part)
    proj_own = [held(piece, parts[0]) for piece in group_swap(proj_pieces)]
    proj_other = ds.swap(jnp.stack([piece[1] for piece in proj_own]), 1)
    part = part[:, 0]
    part_own = pick(part, xs.me)
    part_sent = [pick(part, xs.me ^ s) for s in range(1, fsdp)]
    proj_other = held(proj_other, part_own, *part_sent)
    in_first, in_rest, grad_text, gain_text = in_back(
        both_info, proj_own, proj_other, w_cols, text_raw, gains, tokens
    )
    part_got = [held(xs.swap(v, s + 1), in_first) for s, v in enumerate(part_sent)]
    part = jnp.stack([part_own] + part_got)
    part = jnp.stack([pick(part, xs.me ^ k) for k in range(fsdp)])
    blocks = jnp.transpose(part.reshape(fsdp, per, 3, GROUP_WIDTH), (2, 0, 1, 3))
    blocks = blocks.reshape(3 * fsdp, per, GROUP_WIDTH)
    in_got = [xs.swap(in_rest[s - 1], s) for s in range(1, fsdp)]
    if groups > 1:
        window = 3 * heads // GROUP_HEADS // groups
        slots = -(-window // groups)
        first_of = lambda target, source: (window * target - source + groups - 1) // groups
        sent = []
        for s in range(groups):
            first = first_of(group_me ^ s, group_me)
            sent.append(
                jnp.stack(
                    [pick(blocks, jnp.clip(first + t, 0, 3 * fsdp - 1)) for t in range(slots)]
                )
            )
        in_got = [held(v, *sent) for v in in_got]
    for v in in_got:
        in_first = in_first + held(v, ffn_sums).astype(F32)
    grad_normed = frame_view(in_first)
    in_unit = frame_sum(grad_normed * unit_in)
    grad_scale_attn = in_unit * gain_attn_in
    grad_gain_attn_in = jnp.sum(in_unit * (1.0 + scale_attn[:, 0]), axis=0)
    grad_input = grad_after + unit_back(
        grad_normed * (gain_attn_in * (1.0 + scale_attn)), unit_in, inv_in
    )
    if groups > 1:
        got = held(jnp.stack(group_swap(sent)), grad_gain_attn_in, grad_scale_attn)
        got = got.reshape(groups * slots, per, GROUP_WIDTH)
        ordered = []
        for k in range(window):
            block = window * group_me + k
            source = block % groups
            slot = block // groups - first_of(group_me, source)
            ordered.append(pick(got, (source ^ group_me) * slots + slot))
        blocks = jnp.stack(ordered)
    columns = jnp.swapaxes(blocks, 0, 1).reshape(per, ranks, 3 * width // dps)
    columns = jnp.swapaxes(columns, 0, 1)
    if ranks <= 4:
        got = jnp.stack(
            [pick(columns, rank_me)]
            + [ds.swap(pick(columns, rank_me ^ m), m) for m in range(1, ranks)]
        )
        got = jnp.stack([pick(got, rank_me ^ r) for r in range(ranks)])
    else:
        got = lax.all_to_all(columns, "dp", 0, 0, tiled=True)
    grad_w_qkv = got.reshape(rows, 3 * width // dps).astype(F32)

    grad_w_gate_up = jnp.stack([ffn_sums[:, :inner], ffn_sums[:, inner : 2 * inner]])
    grad_w_down = jnp.transpose(ffn_sums[:, 2 * inner :])

    out_grad, ffn_sums = beside(out_grad, ffn_sums)
    grad_w_out = jnp.transpose(reduce_rows(out_grad))
    def gather_columns(values, parts):
        wide = values.shape[2] // parts
        cut = values.reshape(fsdp, values.shape[1], parts, wide)[..., :own_width]
        got = [cut]
        for s in range(1, fsdp):
            other = xs.swap(cut, s)
            got.append(jnp.stack([other[s ^ k] for k in range(fsdp)]))
        got = jnp.stack(got)
        whole = jnp.stack([pick(got, xs.me ^ k) for k in range(fsdp)], axis=3)
        return whole.reshape(fsdp * values.shape[1], parts * fsdp * own_width)

    grad_text_all = gather_columns(grad_text, 2)
    text_cols = grad_text_all.shape[1] // dps
    grad_text_cols = jnp.swapaxes(grad_text_all.reshape(fsdp * text_own, dps, text_cols), 0, 1)
    grad_text_cols = lax.all_to_all(grad_text_cols, "dp", 0, 0, tiled=True)
    grad_w_text_kv = mxu(text_every, grad_text_cols.reshape(-1, text_cols), ((0,), (0,)))

    frame_grads = jnp.concatenate(
        [grad_scale_attn, grad_gate_attn, grad_scale_ffn, grad_gate_ffn], axis=1
    )
    clip_grads = jnp.dot(jnp.transpose(onehot), frame_grads, precision=HIGHEST)
    mod_cols = clip_grads.shape[1] // dps
    clip_grads = jnp.swapaxes(clip_grads.reshape(clips, dps, mod_cols), 0, 1)
    clip_grads = jnp.sum(lax.all_to_all(clip_grads, "dp", 0, 0, tiled=True), axis=0)
    clip_rel = jnp.concatenate(xs.gather(clip_grads))
    grad_w_modulate = jnp.dot(jnp.transpose(cond_own.astype(F32)), clip_rel, precision=HIGHEST)
    head_term = jnp.sum(dgate.reshape(GROUP_HEADS, HD), axis=1)
    gate_term = lax.dynamic_update_slice_in_dim(jnp.zeros((heads,), F32), head_term, first_head, 0)
    gate_term = gate_term * (1.0 - tanh_gate * tanh_gate)
    qk_sums = jnp.sum(gain_qk[0].reshape(2, GROUP_HEADS, HD), axis=1)
    small = [
        grad_gain_attn_in,
        grad_gain_attn_out,
        grad_gain_ffn_in,
        grad_gain_ffn_out,
        qk_sums[0],
        qk_sums[1],
        gain_text[0, :HD] + gain_text[0, HD:],
        gate_term,
    ]
    sizes = [v.shape[0] for v in small]
    packed = jnp.concatenate(small)
    packed = jnp.pad(packed, (0, -packed.shape[0] % 1024)).reshape(-1, 128)
    for moves in (ds, xs):
        for b in range(moves.size.bit_length() - 1):
            packed = packed + moves.swap(packed, 1 << b)
    packed = packed.reshape(-1)
    sums = []
    at = 0
    for size in sizes:
        sums.append(packed[at : at + size])
        at += size
    return (
        output.reshape(1, tokens, width),
        grad_input.reshape(1, tokens, width),
        grad_w_modulate,
        grad_w_qkv,
        grad_w_text_kv,
        grad_w_out,
        grad_w_gate_up,
        grad_w_down,
        *sums,
    )


def solution(mesh):
    rows = P("fsdp", "dp", None)
    first = P("fsdp", None)
    split = P("fsdp", "dp")
    return jax.shard_map(
        functools.partial(per_device, mesh.shape["fsdp"], mesh.shape["dp"]),
        mesh=mesh,
        in_specs=(
            rows,
            rows,
            first,
            split,
            P("fsdp", None, None),
            rows,
            first,
            first,
            first,
            first,
            P(None, None, "fsdp"),
            first,
        )
        + (P(),) * 8,
        out_specs=(
            rows,
            rows,
            split,
            split,
            split,
            split,
            P(None, "dp", "fsdp"),
            split,
        )
        + (P(),) * 8,
        check_vma=False,
    )
```

```python
import functools
import math

import jax
import jax.numpy as jnp
import numpy as np
from jax import lax
from jax.experimental import pallas as pl
from jax.experimental.pallas import tpu as pltpu
from jax.sharding import PartitionSpec as P

HD = 64
CTX = 256
FRAME_TOK = 128
PW = 16
EPSILON = 1e-06
GROUP_HEADS = 3
GROUP_WIDTH = GROUP_HEADS * HD
STACK = GROUP_HEADS * FRAME_TOK
ONES_ROWS = 16
HIGHEST = lax.Precision.HIGHEST
BF16 = jnp.bfloat16
F32 = jnp.float32
SCALE = HD ** (-0.5)
EXP2_SCALE = SCALE * math.log2(math.e)
MIB = 1 << 20
COST_CUT = 100


def mxu(a, b, dims=((1,), (0,))):
    return lax.dot_general(a, b, (dims, ((), ())), preferred_element_type=F32)


class Moves:
    def __init__(self, axis, size):
        self.axis = axis
        self.size = size
        self.me = lax.axis_index(axis)

    def swap(self, value, mask):
        return lax.ppermute(value, self.axis, [(i, i ^ mask) for i in range(self.size)])

    def gather(self, value):
        return [value] + [self.swap(value, s) for s in range(1, self.size)]

    def scatter_sum(self, parts):
        total = parts[0].astype(F32)
        for s in range(1, self.size):
            total = total + self.swap(parts[s].astype(BF16), s).astype(F32)
        return total

    def reorder(self, value, axis):
        block = value.shape[axis] // self.size
        return jnp.concatenate(
            [
                lax.dynamic_slice_in_dim(value, (self.me ^ s) * block, block, axis)
                for s in range(self.size)
            ],
            axis,
        )

    def own_block(self, value, axis, s=0):
        block = value.shape[axis] // self.size
        return lax.dynamic_slice_in_dim(value, (self.me ^ s) * block, block, axis)


def lane_tiles(width):
    return -(-width // 128) * 128


def turn(values, cosine, sine):
    lane = lax.broadcasted_iota(jnp.int32, values.shape, 1)
    other = jnp.where(lane % 2 == 0, pltpu.roll(values, 127, 1), pltpu.roll(values, 1, 1))
    return values * cosine + other * sine


def head_means(values, ones):
    upper = values.astype(BF16)
    lower = (values - upper.astype(F32)).astype(BF16)
    return mxu(jnp.concatenate([upper, lower], axis=1), ones) * (1.0 / HD)


def joined(pieces, axis):
    return jnp.concatenate(pieces, axis=axis) if len(pieces) > 1 else pieces[0]


def widened(values):
    missing = lane_tiles(values.shape[1]) - values.shape[1]
    if not missing:
        return values
    return jnp.concatenate([values, jnp.zeros((values.shape[0], missing), values.dtype)], axis=1)


def tiles_of(values):
    return [values[:, 128 * t : 128 * (t + 1)] for t in range(values.shape[1] // 128)]


def normed_heads(raw, ones, gain):
    return [x * lax.rsqrt(head_means(x * x, ones) + EPSILON) * gain for x in tiles_of(raw)]


def head_ones():
    lane = np.arange(128) // HD
    ones = (lane[:, None] == lane[None, :]).astype(np.float32)
    return jnp.asarray(np.concatenate([ones, ones]), BF16)


def group_cut(values, g):
    return values[:, GROUP_WIDTH * g : GROUP_WIDTH * (g + 1)]


def packed_frames(values, frames):
    return joined([values[FRAME_TOK * f : FRAME_TOK * (f + 1)] for f in range(frames)], 1)


def call(kernel, name, grid, prefetch, in_specs, out_specs, out_shape, scratch, vmem, flops, moved, args):
    return pl.pallas_call(
        kernel,
        grid_spec=pltpu.PrefetchScalarGridSpec(
            num_scalar_prefetch=prefetch,
            grid=grid,
            in_specs=in_specs,
            out_specs=out_specs,
            scratch_shapes=scratch,
        ),
        out_shape=out_shape,
        compiler_params=pltpu.CompilerParams(
            dimension_semantics=("arbitrary",) * len(grid), vmem_limit_bytes=vmem
        ),
        cost_estimate=pl.CostEstimate(
            flops=int(flops) // COST_CUT, bytes_accessed=int(moved) // COST_CUT, transcendentals=0
        ),
        name=name,
    )(*args)


def whole_spec(shape):
    zeros = (0,) * len(shape)
    return pl.BlockSpec(shape, lambda *_: zeros)


def heads_kernel(
    core_ref,
    x_ref,
    w_ref,
    text_ref,
    cos_ref,
    sin_ref,
    gain_ref,
    ones_ref,
    send_q,
    send_kv,
    keep_q,
    keep_kv,
    *,
    half,
    groups,
    frames,
    own_width,
):
    step = pl.program_id(0)
    tokens = frames * FRAME_TOK
    ones = ones_ref[...]
    parts = []
    for p in range(3):
        raw = widened(mxu(x_ref[0], w_ref[:, own_width * p : own_width * (p + 1)]))
        if p < 2:
            raw = joined(
                [
                    turn(x, cos_ref[0], sin_ref[0])
                    for x in normed_heads(raw, ones, gain_ref[p : p + 1, :])
                ],
                1,
            )
        parts.append(raw.astype(BF16))
    wide = text_ref.shape[2] // 2
    text_key = joined(normed_heads(text_ref[0, :, :wide], ones, gain_ref[2:3, :]), 1).astype(BF16)
    text_value = text_ref[0, :, wide:].astype(BF16)

    def put(q_ref, kv_ref):
        for g in range(groups):
            q_ref[0, g] = packed_frames(group_cut(parts[0], g), frames)
            kv_ref[0, g, :tokens] = joined([group_cut(parts[1], g), group_cut(parts[2], g)], 1)
            kv_ref[0, g, tokens:] = joined([group_cut(text_key, g), group_cut(text_value, g)], 1)

    @pl.when(step < half)
    def _():
        put(send_q, send_kv)

    @pl.when(step >= half)
    def _():
        put(keep_q, keep_kv)


def set_stream(step, core, half):
    other = jnp.where(step < half, 1 - core, core)
    return other * half + step % half


def make_heads(core, x, w_cols, text_raw, cosine, sine, gains, groups):
    streams, tokens, width = x.shape
    half = streams // 2
    frames = tokens // FRAME_TOK
    own_width = w_cols.shape[1] // 3
    text_own = text_raw.shape[1]
    by_stream = lambda i, core: (set_stream(i, core[0], half), 0, 0)
    q_block = (1, groups, FRAME_TOK, frames * GROUP_WIDTH)
    kv_block = (1, groups, tokens + text_own, 2 * GROUP_WIDTH)
    first = lambda i, core: (jnp.minimum(i, half - 1), 0, 0, 0)
    second = lambda i, core: (jnp.maximum(i - half, 0), 0, 0, 0)
    return call(
        functools.partial(
            heads_kernel, half=half, groups=groups, frames=frames, own_width=own_width
        ),
        "make_heads",
        (streams,),
        1,
        [
            pl.BlockSpec((1, tokens, width), by_stream),
            whole_spec(w_cols.shape),
            pl.BlockSpec((1,) + text_raw.shape[1:], by_stream),
            pl.BlockSpec((1, tokens, 128), by_stream),
            pl.BlockSpec((1, tokens, 128), by_stream),
            whole_spec((8, 128)),
            whole_spec((256, 128)),
        ],
        [
            pl.BlockSpec(q_block, first),
            pl.BlockSpec(kv_block, first),
            pl.BlockSpec(q_block, second),
            pl.BlockSpec(kv_block, second),
        ],
        [
            jax.ShapeDtypeStruct((half,) + q_block[1:], BF16),
            jax.ShapeDtypeStruct((half,) + kv_block[1:], BF16),
        ]
        * 2,
        [],
        48 * MIB,
        2 * x.size * w_cols.shape[1],
        x.size * 2 + w_cols.size * 2 + x.size * 3,
        (core, x, w_cols, text_raw, cosine, sine, gains, head_ones()),
    )


BIG = 4
CLIP = 16


def over_tiles(start, count, body):
    whole = count // CLIP
    rest = count - whole * CLIP
    big = rest // BIG
    at = lambda frame: pl.multiple_of(frame * FRAME_TOK, FRAME_TOK)

    def whole_step(t, carry):
        body(at(start + t * CLIP), BIG * FRAME_TOK, CLIP // BIG)
        return carry

    def big_step(t, carry):
        body(at(start + whole * CLIP + t * BIG), BIG * FRAME_TOK, 1)
        return carry

    def small_step(t, carry):
        body(at(start + whole * CLIP + big * BIG + t), FRAME_TOK, 1)
        return carry

    lax.fori_loop(0, whole, whole_step, 0)
    lax.fori_loop(0, big, big_step, 0)
    lax.fori_loop(0, rest - big * BIG, small_step, 0)


def stacked(values, mask):
    return jnp.concatenate([values] * GROUP_HEADS, axis=0) * mask


def diagonal(values):
    own = [
        values[HD * h : HD * (h + 1), FRAME_TOK * h : FRAME_TOK * (h + 1)]
        for h in range(GROUP_HEADS)
    ]
    return jnp.transpose(jnp.concatenate(own, axis=0))


def head_row(values):
    flipped = jnp.transpose(values)
    return jnp.concatenate(
        [
            jnp.sum(flipped[HD * h : HD * (h + 1), :], axis=0, keepdims=True)
            for h in range(GROUP_HEADS)
        ],
        axis=1,
    )


def each_chunk(kv_refs, rank_ref, place_ref, s, frames, chunk_text, self_rows, frame_body, text_body):
    tokens = frames * FRAME_TOK
    for i, ref in enumerate(kv_refs):

        def one(c, carry, i=i, ref=ref):
            chunk = 2 * i + c
            for f in range(frames):
                at = pl.multiple_of(rank_ref[s, chunk * frames + f] * FRAME_TOK, FRAME_TOK)
                frame_body(ref, c, slice(f * FRAME_TOK, (f + 1) * FRAME_TOK), at)
            at = pl.multiple_of(self_rows + place_ref[chunk] * chunk_text, chunk_text)
            text_body(ref, c, slice(tokens, tokens + chunk_text), at)
            return carry

        lax.fori_loop(0, 2, one, 0)


def unpack_frames(refs, scratch, frames):
    for i, ref in enumerate(refs):
        for c in range(2):
            for f in range(frames):
                scratch[(2 * i + c) * frames + f] = ref[
                    c, :, GROUP_WIDTH * f : GROUP_WIDTH * (f + 1)
                ]


def attn_fwd_kernel(*refs, pieces, groups, frames, chunk_text):
    rank_ref, start_ref, count_ref, clip_ref, place_ref = refs[:5]
    refs = refs[5:]
    kv_refs, refs = refs[:pieces], refs[pieces:]
    q_refs, refs = refs[:groups], refs[groups:]
    gate_ref, mask_ref = refs[:2]
    mixed_refs, refs = refs[2 : 2 + groups], refs[2 + groups :]
    self_ref, text_ref, lse_ref, keys, values, rows_text, queries, mixes, acc = refs
    s = pl.program_id(0)
    j = pl.program_id(1)
    self_rows = pieces * 2 * frames * FRAME_TOK
    text_rows = rows_text.shape[0]
    K = slice(0, GROUP_WIDTH)
    V = slice(GROUP_WIDTH, 2 * GROUP_WIDTH)

    @pl.when(j == 0)
    def _():
        values[GROUP_WIDTH:, :] = jnp.ones((ONES_ROWS, values.shape[1]), BF16)

        def frame_body(ref, c, rows, at):
            keys[pl.ds(at, FRAME_TOK), :] = ref[c, rows, K]
            values[:GROUP_WIDTH, pl.ds(at, FRAME_TOK)] = jnp.transpose(ref[c, rows, V])

        def text_body(ref, c, rows, at):
            keys[pl.ds(at, chunk_text), :] = ref[c, rows, K]
            rows_text[pl.ds(at - self_rows, chunk_text), :] = ref[c, rows, V]

        each_chunk(
            kv_refs, rank_ref, place_ref, s, frames, chunk_text, self_rows, frame_body, text_body
        )
        for b in range(text_rows // 128):
            values[:GROUP_WIDTH, self_rows + 128 * b : self_rows + 128 * (b + 1)] = jnp.transpose(
                rows_text[128 * b : 128 * (b + 1), :]
            )
        unpack_frames(q_refs, queries, frames)

    query = stacked(queries[j], mask_ref[...])

    def tile(base, size, times):
        total = None
        for t in range(times):
            rows = pl.ds(pl.multiple_of(base + t * size, FRAME_TOK), size)
            scores = mxu(keys[rows, :], query, ((1,), (1,)))
            weights = jnp.exp2(scores * EXP2_SCALE).astype(BF16)
            part = mxu(values[:, rows], weights)
            total = part if total is None else total + part
        acc[...] += total

    def finish(row):
        total = acc[GROUP_WIDTH : GROUP_WIDTH + 1, :]
        lse_ref[0, 0, row : row + 1, :] = jnp.log(total) * math.log2(math.e)
        return diagonal(acc[:GROUP_WIDTH, :] * (1.0 / total))

    acc[...] = jnp.zeros_like(acc)
    over_tiles(start_ref[s, j], count_ref[s, j], tile)
    self_out = finish(0)
    acc[...] = jnp.zeros_like(acc)
    tile(pl.multiple_of(self_rows + clip_ref[s, j] * CTX, 128), CTX, 1)
    text_out = finish(1)
    self_ref[0, 0] = self_out
    text_ref[0, 0] = text_out
    mixes[j] = (self_out + gate_ref[...] * text_out).astype(BF16)

    @pl.when(j == pl.num_programs(1) - 1)
    def _():
        for g, ref in enumerate(mixed_refs):
            for c in range(2):
                at = (2 * g + c) * frames
                ref[c] = joined([mixes[at + f] for f in range(frames)], 1)


def attn_bwd_kernel(*refs, pieces, groups, frames, chunk_text):
    rank_ref, start_ref, count_ref, clip_ref, place_ref = refs[:5]
    refs = refs[5:]
    kv_refs, refs = refs[:pieces], refs[pieces:]
    q_refs, refs = refs[:groups], refs[groups:]
    grad_refs, refs = refs[:groups], refs[groups:]
    self_ref, text_ref, lse_ref, gate_ref, mask_ref, dq_ref = refs[:6]
    dkv_refs, refs = refs[6 : 6 + pieces], refs[6 + pieces :]
    dgate_ref, keys, keys_flip, values, dkeys, dvalues, dquery, queries, grads = refs
    s = pl.program_id(0)
    j = pl.program_id(1)
    self_rows = pieces * 2 * frames * FRAME_TOK
    text_rows = pieces * 2 * chunk_text
    K = slice(0, GROUP_WIDTH)
    V = slice(GROUP_WIDTH, 2 * GROUP_WIDTH)

    @pl.when(jnp.logical_and(s == 0, j == 0))
    def _():
        dgate_ref[...] = jnp.zeros_like(dgate_ref)

    @pl.when(j == 0)
    def _():
        dkeys[...] = jnp.zeros_like(dkeys)
        dvalues[...] = jnp.zeros_like(dvalues)

        def frame_body(ref, c, rows, at):
            keys[pl.ds(at, FRAME_TOK), :] = ref[c, rows, K]
            keys_flip[:, pl.ds(at, FRAME_TOK)] = jnp.transpose(ref[c, rows, K])
            values[pl.ds(at, FRAME_TOK), :] = ref[c, rows, V]

        def text_body(ref, c, rows, at):
            keys[pl.ds(at, chunk_text), :] = ref[c, rows, K]
            values[pl.ds(at, chunk_text), :] = ref[c, rows, V]

        each_chunk(
            kv_refs, rank_ref, place_ref, s, frames, chunk_text, self_rows, frame_body, text_body
        )
        for b in range(text_rows // 128):
            rows = slice(self_rows + 128 * b, self_rows + 128 * (b + 1))
            keys_flip[:, rows] = jnp.transpose(keys[rows, :])
        unpack_frames(q_refs, queries, frames)
        unpack_frames(grad_refs, grads, frames)

    mask = mask_ref[...]
    query = stacked(queries[j], mask)
    grad_low = grads[j]
    grad_wide = grad_low.astype(F32)
    grad_text = (grad_wide * gate_ref[...]).astype(BF16)
    text_out = text_ref[0, 0]
    dgate_ref[...] += jnp.sum(grad_wide * text_out, axis=0, keepdims=True)
    dquery[...] = jnp.zeros_like(dquery)

    def over(grad, out, lse):
        grad_stack = stacked(grad, mask)
        delta = head_row(grad.astype(F32) * out)

        def tile(base, size, times):
            total = None
            for t in range(times):
                rows = pl.ds(pl.multiple_of(base + t * size, FRAME_TOK), size)
                scores = mxu(keys[rows, :], query, ((1,), (1,)))
                weights = jnp.exp2(scores * EXP2_SCALE - lse)
                dweights = mxu(values[rows, :], grad_stack, ((1,), (1,)))
                dscores = (weights * (dweights - delta)).astype(BF16)
                dvalues[rows, :] += mxu(weights.astype(BF16), grad_stack)
                dkeys[rows, :] += mxu(dscores, query)
                part = mxu(keys_flip[:, rows], dscores)
                total = part if total is None else total + part
            dquery[...] += total

        return tile

    over_tiles(start_ref[s, j], count_ref[s, j], over(grad_low, self_ref[0, 0], lse_ref[0, 0, 0:1, :]))
    over(grad_text, text_out, lse_ref[0, 0, 1:2, :])(
        pl.multiple_of(self_rows + clip_ref[s, j] * CTX, 128), CTX, 1
    )
    dq_ref[0, 0] = (diagonal(dquery[...]) * SCALE).astype(BF16)

    @pl.when(j == pl.num_programs(1) - 1)
    def _():
        def frame_body(ref, c, rows, at):
            taken = pl.ds(at, FRAME_TOK)
            ref[c, rows, :] = jnp.concatenate(
                [dkeys[taken, :] * SCALE, dvalues[taken, :]], axis=1
            ).astype(BF16)

        def text_body(ref, c, rows, at):
            taken = pl.ds(at, chunk_text)
            ref[c, rows, :] = jnp.concatenate(
                [dkeys[taken, :] * SCALE, dvalues[taken, :]], axis=1
            ).astype(BF16)

        each_chunk(
            dkv_refs, rank_ref, place_ref, s, frames, chunk_text, self_rows, frame_body, text_body
        )


def attention_specs(kv, query):
    _, streams, chunk_rows, _ = kv[0].shape
    frames = query[0].shape[3] // GROUP_WIDTH
    chunk_text = chunk_rows - frames * FRAME_TOK
    sizes = dict(pieces=len(kv), groups=len(query), frames=frames, chunk_text=chunk_text)
    count = len(query) * 2 * frames
    grid = (streams, count)
    piece = lambda shape: pl.BlockSpec(
        (2, None) + shape, lambda s, j, *_: (0, s, 0, 0), pipeline_mode=pl.Buffered(1)
    )
    kv_spec = piece((chunk_rows, 2 * GROUP_WIDTH))
    q_spec = piece((FRAME_TOK, frames * GROUP_WIDTH))
    tok_spec = pl.BlockSpec((1, 1, FRAME_TOK, GROUP_WIDTH), lambda s, j, *_: (s, j, 0, 0))
    lse_spec = pl.BlockSpec((1, 1, 2, STACK), lambda s, j, *_: (s, j, 0, 0))
    const_specs = [whole_spec((1, GROUP_WIDTH)), whole_spec((STACK, GROUP_WIDTH))]
    return sizes, grid, kv_spec, q_spec, tok_spec, lse_spec, const_specs


def stack_mask():
    head_of_row = np.arange(STACK) // FRAME_TOK
    head_of_lane = np.arange(GROUP_WIDTH) // HD
    return jnp.asarray((head_of_row[:, None] == head_of_lane[None, :]).astype(np.float32), BF16)


def attn_fwd(tables, kv, query, gate):
    sizes, grid, kv_spec, q_spec, tok_spec, lse_spec, const_specs = attention_specs(kv, query)
    total = len(kv) * 2 * kv[0].shape[2]
    text_rows = len(kv) * 2 * sizes["chunk_text"]
    wide = jax.ShapeDtypeStruct(grid + (FRAME_TOK, GROUP_WIDTH), F32)
    got = call(
        functools.partial(attn_fwd_kernel, **sizes),
        "attention",
        grid,
        5,
        [kv_spec] * len(kv) + [q_spec] * len(query) + const_specs,
        [q_spec] * len(query) + [tok_spec, tok_spec, lse_spec],
        [jax.ShapeDtypeStruct(q.shape, BF16) for q in query]
        + [wide, wide, jax.ShapeDtypeStruct(grid + (2, STACK), F32)],
        [
            pltpu.VMEM((total, GROUP_WIDTH), BF16),
            pltpu.VMEM((GROUP_WIDTH + ONES_ROWS, total), BF16),
            pltpu.VMEM((text_rows, GROUP_WIDTH), BF16),
            pltpu.VMEM((grid[1], FRAME_TOK, GROUP_WIDTH), BF16),
            pltpu.VMEM((grid[1], FRAME_TOK, GROUP_WIDTH), BF16),
            pltpu.VMEM((GROUP_WIDTH + ONES_ROWS, STACK), F32),
        ],
        min(60 * MIB, total * 2600 + 16 * MIB),
        grid[0] * grid[1] * STACK * 2304 * GROUP_WIDTH * 8,
        grid[0] * grid[1] * 300000,
        (*tables, *kv, *query, gate, stack_mask()),
    )
    return got[: len(query)], got[len(query) :]


def attn_bwd(tables, kv, query, grad, kept, gate):
    sizes, grid, kv_spec, q_spec, tok_spec, lse_spec, const_specs = attention_specs(kv, query)
    total = len(kv) * 2 * kv[0].shape[2]
    got = call(
        functools.partial(attn_bwd_kernel, **sizes),
        "attention_back",
        grid,
        5,
        [kv_spec] * len(kv)
        + [q_spec] * (2 * len(query))
        + [tok_spec, tok_spec, lse_spec]
        + const_specs,
        [tok_spec] + [kv_spec] * len(kv) + [whole_spec((1, GROUP_WIDTH))],
        [jax.ShapeDtypeStruct(grid + (FRAME_TOK, GROUP_WIDTH), BF16)]
        + [jax.ShapeDtypeStruct(v.shape, BF16) for v in kv]
        + [jax.ShapeDtypeStruct((1, GROUP_WIDTH), F32)],
        [
            pltpu.VMEM((total, GROUP_WIDTH), BF16),
            pltpu.VMEM((GROUP_WIDTH, total), BF16),
            pltpu.VMEM((total, GROUP_WIDTH), BF16),
            pltpu.VMEM((total, GROUP_WIDTH), F32),
            pltpu.VMEM((total, GROUP_WIDTH), F32),
            pltpu.VMEM((GROUP_WIDTH, STACK), F32),
            pltpu.VMEM((grid[1], FRAME_TOK, GROUP_WIDTH), BF16),
            pltpu.VMEM((grid[1], FRAME_TOK, GROUP_WIDTH), BF16),
        ],
        min(62 * MIB, total * 5800 + 16 * MIB),
        grid[0] * grid[1] * STACK * 2304 * GROUP_WIDTH * 20,
        grid[0] * grid[1] * 500000,
        (*tables, *kv, *query, *grad, *kept, gate, stack_mask()),
    )
    return got[0], got[1 : 1 + len(kv)], got[-1]


def for_group(group, groups, body):
    for v in range(groups):

        @pl.when(group == v)
        def _(v=v):
            body(v)


def out_kernel(info_ref, *refs, half, groups, frames):
    own_refs, refs = refs[:groups], refs[groups:]
    other_ref, w_ref, mixed_ref, first_ref, rest_ref = refs
    k = pl.program_id(0)
    here = (k // half) == info_ref[0]

    def fill(v, take):
        for s in range(groups):
            piece = take(s)
            for f in range(frames):
                mixed_ref[0, FRAME_TOK * f : FRAME_TOK * (f + 1), GROUP_WIDTH * (v ^ s) : GROUP_WIDTH * ((v ^ s) + 1)] = piece[
                    :, GROUP_WIDTH * f : GROUP_WIDTH * (f + 1)
                ]

    @pl.when(here)
    def _():
        for_group(info_ref[1], groups, lambda v: fill(v, lambda s: own_refs[s][0, 0]))

    @pl.when(jnp.logical_not(here))
    def _():
        for_group(info_ref[1], groups, lambda v: fill(v, lambda s: other_ref[s, 0]))

    part = mxu(mixed_ref[0], w_ref[...])

    @pl.when(k == 0)
    def _():
        first_ref[...] = part

    @pl.when(k > 0)
    def _():
        rest_ref[0] = part.astype(BF16)


def out_project(info, own, other, w_out, streams, tokens):
    groups = len(own)
    half = streams // 2
    frames = tokens // FRAME_TOK
    own_width, width = w_out.shape
    lanes = frames * GROUP_WIDTH
    return call(
        functools.partial(out_kernel, half=half, groups=groups, frames=frames),
        "out_project",
        (streams,),
        1,
        [pl.BlockSpec((1, 1, FRAME_TOK, lanes), lambda k, _: (0, k % half, 0, 0))] * groups
        + [
            pl.BlockSpec((groups, 1, FRAME_TOK, lanes), lambda k, _: (0, k % half, 0, 0)),
            whole_spec(w_out.shape),
        ],
        [
            pl.BlockSpec((1, tokens, own_width), lambda k, _: (k, 0, 0)),
            whole_spec((tokens, width)),
            pl.BlockSpec((1, tokens, width), lambda k, _: (jnp.maximum(k - 1, 0), 0, 0)),
        ],
        [
            jax.ShapeDtypeStruct((streams, tokens, own_width), BF16),
            jax.ShapeDtypeStruct((tokens, width), F32),
            jax.ShapeDtypeStruct((streams - 1, tokens, width), BF16),
        ],
        [],
        32 * MIB,
        2 * streams * tokens * own_width * width,
        streams * tokens * width * 6 + w_out.size * 2,
        (info, *own, other, w_out),
    )


def out_back_kernel(core_ref, grad_ref, w_ref, send_ref, keep_ref, *, half, groups, frames):
    step = pl.program_id(0)
    grad = mxu(grad_ref[0], w_ref[...], ((1,), (1,))).astype(BF16)

    def put(ref):
        for g in range(groups):
            ref[0, g] = packed_frames(group_cut(grad, g), frames)

    @pl.when(step < half)
    def _():
        put(send_ref)

    @pl.when(step >= half)
    def _():
        put(keep_ref)


def out_back(core, grad, w_out, groups):
    streams, tokens, width = grad.shape
    half = streams // 2
    frames = tokens // FRAME_TOK
    block = (1, groups, FRAME_TOK, frames * GROUP_WIDTH)
    return call(
        functools.partial(out_back_kernel, half=half, groups=groups, frames=frames),
        "out_back",
        (streams,),
        1,
        [
            pl.BlockSpec((1, tokens, width), lambda i, core: (set_stream(i, core[0], half), 0, 0)),
            whole_spec(w_out.shape),
        ],
        [
            pl.BlockSpec(block, lambda i, core: (jnp.minimum(i, half - 1), 0, 0, 0)),
            pl.BlockSpec(block, lambda i, core: (jnp.maximum(i - half, 0), 0, 0, 0)),
        ],
        [jax.ShapeDtypeStruct((half,) + block[1:], BF16)] * 2,
        [],
        32 * MIB,
        2 * streams * tokens * w_out.size,
        streams * tokens * width * 3 + w_out.size * 2,
        (core, grad, w_out),
    )


def proj_back_kernel(*refs, groups, frames, half, chunk_text):
    group_ref, x_ref, w_ref, dq_ref = refs[:4]
    dkv_refs, refs = refs[4 : 4 + groups], refs[4 + groups :]
    cos_ref, sin_ref, gain_ref, ones_ref = refs[:4]
    out_refs, refs = refs[4 : 4 + groups], refs[4 + groups :]
    dw_ref, dgain_ref, dkv, total = refs
    i = pl.program_id(0)
    tokens = frames * FRAME_TOK

    @pl.when(i == 0)
    def _():
        total[...] = jnp.zeros_like(total)
        dgain_ref[...] = jnp.zeros_like(dgain_ref)

    for g, ref in enumerate(dkv_refs):

        @pl.when(i // half == g)
        def _(ref=ref):
            dkv[...] = ref[...]

    ones = ones_ref[...]
    x = jnp.concatenate([x_ref[0, c, 0] for c in range(2)], axis=0)
    raw = mxu(x, w_ref[...])
    key_grad = jnp.concatenate([dkv[c, :tokens, :GROUP_WIDTH] for c in range(2)], axis=0)
    value_grad = jnp.concatenate([dkv[c, :tokens, GROUP_WIDTH:] for c in range(2)], axis=0)
    query_grad = jnp.concatenate([dq_ref[0, n] for n in range(2 * frames)], axis=0)
    turned = jnp.concatenate([query_grad, key_grad], axis=1).astype(F32)
    done = []
    for t, (x_t, dy) in enumerate(zip(tiles_of(raw), tiles_of(turned))):
        dy = turn(dy, cos_ref[0, 0], -sin_ref[0, 0])
        inv = lax.rsqrt(head_means(x_t * x_t, ones) + EPSILON)
        unit = x_t * inv
        lanes = slice(128 * t, 128 * (t + 1))
        dgain_ref[0:1, lanes] += jnp.sum(dy * unit, axis=0, keepdims=True)
        dn = dy * gain_ref[0:1, lanes]
        done.append((inv * (dn - unit * head_means(dn * unit, ones))).astype(BF16))
    grads = jnp.concatenate(done + [value_grad], axis=1)
    total[...] += mxu(grads, x, ((0,), (0,)))

    def put(ref):
        for c in range(2):
            ref[c, :FRAME_TOK, :] = packed_frames(grads[tokens * c : tokens * (c + 1)], frames)
            rows = slice(tokens, tokens + chunk_text)
            text = dkv[c, rows, :]
            lower = chunk_text // 2
            ref[c, FRAME_TOK:, : 4 * GROUP_WIDTH] = jnp.concatenate(
                [text[:lower], text[lower:]], axis=1
            )
            ref[c, FRAME_TOK:, 4 * GROUP_WIDTH :] = jnp.zeros(
                (lower, ref.shape[2] - 4 * GROUP_WIDTH), BF16
            )

    for g, ref in enumerate(out_refs):

        @pl.when(i // half == g)
        def _(ref=ref):
            put(ref)

    @pl.when(i == pl.num_programs(0) - 1)
    def _():
        for b in range(total.shape[1] // 256):
            lanes = slice(256 * b, 256 * (b + 1))
            dw_ref[lanes, :] = jnp.transpose(total[:, lanes]).astype(BF16)


def proj_back(group, x, w_tri, dq, dkv, cosine, sine, gains):
    groups = len(dkv)
    half = x.shape[2]
    tokens, width = x.shape[3:]
    frames = tokens // FRAME_TOK
    chunk_text = dkv[0].shape[2] - tokens
    lanes = frames * 3 * GROUP_WIDTH
    rows = FRAME_TOK + chunk_text // 2
    got = call(
        functools.partial(
            proj_back_kernel, groups=groups, frames=frames, half=half, chunk_text=chunk_text
        ),
        "proj_back",
        (groups * half,),
        1,
        [
            pl.BlockSpec(
                (1, 2, 1, tokens, width), lambda i, g: (g[0] ^ (i // half), 0, i % half, 0, 0)
            ),
            whole_spec(w_tri.shape),
            pl.BlockSpec(
                (1, 2 * frames, FRAME_TOK, GROUP_WIDTH), lambda i, g: (i % half, i // half, 0, 0)
            ),
        ]
        + [
            pl.BlockSpec((2, None) + dkv[0].shape[2:], lambda i, g: (0, i % half, 0, 0))
        ]
        * groups
        + [
            pl.BlockSpec((1, 1, 2 * tokens, 128), lambda i, g: (i // half, i % half, 0, 0)),
            pl.BlockSpec((1, 1, 2 * tokens, 128), lambda i, g: (i // half, i % half, 0, 0)),
            whole_spec(gains.shape),
            whole_spec((256, 128)),
        ],
        [
            pl.BlockSpec(
                (2, None, rows, lanes),
                lambda i, g, n=n: (0, jnp.clip(i - n * half, 0, half - 1), 0, 0),
            )
            for n in range(groups)
        ]
        + [whole_spec((width, 3 * GROUP_WIDTH)), whole_spec((8, 2 * GROUP_WIDTH))],
        [jax.ShapeDtypeStruct((2, half, rows, lanes), BF16)] * groups
        + [
            jax.ShapeDtypeStruct((width, 3 * GROUP_WIDTH), BF16),
            jax.ShapeDtypeStruct((8, 2 * GROUP_WIDTH), F32),
        ],
        [
            pltpu.VMEM(dkv[0].shape[:1] + dkv[0].shape[2:], BF16),
            pltpu.VMEM((3 * GROUP_WIDTH, width), F32),
        ],
        48 * MIB,
        2 * x.size * GROUP_WIDTH * 5,
        x.size * 4 + w_tri.size * 2,
        (group, x, w_tri, dq, *dkv, cosine, sine, gains, head_ones()),
    )
    return got[:groups], got[groups], got[groups + 1]


def in_back_kernel(info_ref, *refs, half, groups, frames, own_width, chunk_text):
    own_refs, refs = refs[:groups], refs[groups:]
    other_ref, w_ref, raw_ref, gain_ref, ones_ref = refs[:5]
    first_ref, rest_ref, text_ref, dgain_ref, grads, texts = refs[5:]
    k = pl.program_id(0)
    here = (k // half) == info_ref[0]
    wide = lane_tiles(own_width)
    lower = chunk_text // 2

    @pl.when(k == 0)
    def _():
        dgain_ref[...] = jnp.zeros_like(dgain_ref)
        texts[...] = jnp.zeros_like(texts)

    def fill(v, take):
        for s in range(groups):
            piece = take(s)
            at = GROUP_WIDTH * (v ^ s)
            for f in range(frames):
                for p in range(3):
                    from_lane = GROUP_WIDTH * (3 * f + p)
                    grads[
                        FRAME_TOK * f : FRAME_TOK * (f + 1),
                        own_width * p + at : own_width * p + at + GROUP_WIDTH,
                    ] = piece[:FRAME_TOK, from_lane : from_lane + GROUP_WIDTH]
            for f in range(2):
                for p in range(2):
                    from_lane = GROUP_WIDTH * (2 * f + p)
                    texts[lower * f : lower * (f + 1), wide * p + at : wide * p + at + GROUP_WIDTH] = piece[
                        FRAME_TOK:, from_lane : from_lane + GROUP_WIDTH
                    ].astype(F32)

    @pl.when(here)
    def _():
        for_group(info_ref[1], groups, lambda v: fill(v, lambda s: own_refs[s][0, 0]))

    @pl.when(jnp.logical_not(here))
    def _():
        for_group(info_ref[1], groups, lambda v: fill(v, lambda s: other_ref[s, 0]))

    part = mxu(grads[...], w_ref[...], ((1,), (1,)))

    @pl.when(k == 0)
    def _():
        first_ref[...] = part

    @pl.when(k > 0)
    def _():
        rest_ref[0] = part.astype(BF16)

    ones = ones_ref[...]
    for t in range(wide // 128):
        lanes = slice(128 * t, 128 * (t + 1))
        x = raw_ref[0, :, lanes]
        dy = texts[:, lanes]
        inv = lax.rsqrt(head_means(x * x, ones) + EPSILON)
        unit = x * inv
        dgain_ref[0:1, :] += jnp.sum(dy * unit, axis=0, keepdims=True)
        dn = dy * gain_ref[2:3, :]
        text_ref[0, :, lanes] = (inv * (dn - unit * head_means(dn * unit, ones))).astype(BF16)
    text_ref[0, :, wide:] = texts[:, wide:].astype(BF16)


def in_back(info, own, other, w_cols, text_raw, gains, tokens):
    streams, chunk_text, text_lanes = text_raw.shape
    groups = len(own)
    half = streams // 2
    frames = tokens // FRAME_TOK
    width = w_cols.shape[0]
    own_width = w_cols.shape[1] // 3
    rows, lanes = own[0].shape[2:]
    return call(
        functools.partial(
            in_back_kernel,
            half=half,
            groups=groups,
            frames=frames,
            own_width=own_width,
            chunk_text=chunk_text,
        ),
        "in_back",
        (streams,),
        1,
        [pl.BlockSpec((1, 1, rows, lanes), lambda k, _: (0, k % half, 0, 0))] * groups
        + [
            pl.BlockSpec((groups, 1, rows, lanes), lambda k, _: (0, k % half, 0, 0)),
            whole_spec(w_cols.shape),
            pl.BlockSpec((1, chunk_text, text_lanes), lambda k, _: (k, 0, 0)),
            whole_spec((8, 128)),
            whole_spec((256, 128)),
        ],
        [
            whole_spec((tokens, width)),
            pl.BlockSpec((1, tokens, width), lambda k, _: (jnp.maximum(k - 1, 0), 0, 0)),
            pl.BlockSpec((1, chunk_text, text_lanes), lambda k, _: (k, 0, 0)),
            whole_spec((8, 128)),
        ],
        [
            jax.ShapeDtypeStruct((tokens, width), F32),
            jax.ShapeDtypeStruct((streams - 1, tokens, width), BF16),
            jax.ShapeDtypeStruct(text_raw.shape, BF16),
            jax.ShapeDtypeStruct((8, 128), F32),
        ],
        [
            pltpu.VMEM((tokens, 3 * own_width), BF16),
            pltpu.VMEM((chunk_text, text_lanes), F32),
        ],
        48 * MIB,
        2 * streams * tokens * w_cols.size,
        streams * tokens * width * 6 + w_cols.size * 2,
        (info, *own, other, w_cols, text_raw, gains, head_ones()),
    )


def weights_kernel(*refs, tiles, streams):
    cut = [refs[streams * n : streams * (n + 1)] for n in range(5)]
    x_refs, g_refs, gate_refs, up_refs, hidden_refs = cut
    out_ref, x_flip, g_flip = refs[5 * streams :]
    i = pl.program_id(0)
    rows = x_refs[0].shape[0]

    @pl.when(i == 0)
    def _():
        for k in range(streams):
            x_flip[:, rows * k : rows * (k + 1)] = jnp.transpose(x_refs[k][...])
            g_flip[:, rows * k : rows * (k + 1)] = jnp.transpose(g_refs[k][...])

    def total(flip, refs):
        right = joined([ref[...] for ref in refs], 0)
        out_ref[...] = mxu(flip[...], right).astype(BF16)

    @pl.when(i < tiles)
    def _():
        total(x_flip, gate_refs)

    @pl.when(jnp.logical_and(i >= tiles, i < 2 * tiles))
    def _():
        total(x_flip, up_refs)

    @pl.when(i >= 2 * tiles)
    def _():
        total(g_flip, hidden_refs)


def ffn_weights(x, g, gate, up, hidden):
    streams = len(x)
    rows, width = x[0].shape
    inner = hidden[0].shape[1]
    tile = min(512, inner)
    tiles = inner // tile
    at = lambda first: pl.BlockSpec(
        (rows, tile), lambda i: (0, jnp.clip(i - first * tiles, 0, tiles - 1))
    )
    return call(
        functools.partial(weights_kernel, tiles=tiles, streams=streams),
        "ffn_weights",
        (3 * tiles,),
        0,
        [whole_spec((rows, width))] * (2 * streams)
        + [at(0)] * streams
        + [at(1)] * streams
        + [at(2)] * streams,
        pl.BlockSpec((width, tile), lambda i: (0, i)),
        jax.ShapeDtypeStruct((width, 3 * inner), BF16),
        [pltpu.VMEM((width, streams * rows), BF16)] * 2,
        56 * MIB,
        6 * streams * rows * width * inner,
        6 * width * inner + 10 * streams * rows * width,
        (*x, *g, *gate, *up, *hidden),
    )


def unit_rms(values):
    inv = lax.rsqrt(jnp.mean(values * values, axis=-1, keepdims=True) + EPSILON)
    return values * inv, inv


def unit_back(grad_unit, unit, inv):
    return inv * (grad_unit - unit * jnp.mean(grad_unit * unit, axis=-1, keepdims=True))


def rope_lanes(frames):
    half = HD // 2
    frame_pairs = HD // 8
    row_pairs = (half - frame_pairs) // 2
    col_pairs = half - frame_pairs - row_pairs
    pair = (np.arange(128) % HD) // 2

    def lanes(first, count):
        freq = 10000.0 ** (-(np.arange(count, dtype=np.float32)) / np.float32(count))
        out = np.zeros((128,), np.float32)
        inside = (pair >= first) & (pair < first + count)
        out[inside] = freq.astype(np.float32)[pair[inside] - first]
        return jnp.asarray(out)[None, :]

    rows = frames.shape[0]
    inner = jnp.arange(rows) % FRAME_TOK
    row_pos = (inner // PW).astype(F32)
    col_pos = (inner % PW).astype(F32)
    angle = (
        frames[:, None] * lanes(0, frame_pairs)
        + row_pos[:, None] * lanes(frame_pairs, row_pairs)
        + col_pos[:, None] * lanes(frame_pairs + row_pairs, col_pairs)
    )
    sign = jnp.asarray(np.where(np.arange(128) % 2 == 0, -1.0, 1.0).astype(np.float32))[None, :]
    return jnp.cos(angle), jnp.sin(angle) * sign


def gain_rows(*gains):
    rows = [jnp.concatenate([g, g]) for g in gains]
    rows += [jnp.zeros((128,), F32)] * (8 - len(rows))
    return jnp.stack(rows)


def pad_parts(values, parts):
    width = values.shape[-1] // parts
    wide = lane_tiles(width)
    if wide == width:
        return values
    cut = values.reshape(values.shape[:-1] + (parts, width))
    cut = jnp.pad(cut, [(0, 0)] * (cut.ndim - 1) + [(0, wide - width)])
    return cut.reshape(values.shape[:-1] + (parts * wide,))


def pick(values, index, axis=0):
    return lax.dynamic_index_in_dim(values, index, axis, keepdims=False)


def beside(value, *others):
    return lax.optimization_barrier((value,) + others)


def held(value, *others):
    return lax.optimization_barrier((value,) + others)[0]


def per_device(
    fsdp,
    dps,
    states,
    cotangent,
    segment_ids,
    frame_ids,
    condition,
    context,
    w_modulate,
    w_qkv,
    w_text_kv,
    w_out,
    w_gate_up,
    w_down,
    gain_attn_in,
    gain_attn_out,
    gain_ffn_in,
    gain_ffn_out,
    gain_query,
    gain_key,
    gain_text_key,
    cross_gate,
):
    xs = Moves("fsdp", fsdp)
    ds = Moves("dp", dps)
    rows_in = states[0]
    tokens, width = rows_in.shape
    frames = tokens // FRAME_TOK
    heads = cross_gate.shape[0]
    own_heads = heads // fsdp
    own_width = own_heads * HD
    groups = own_heads // GROUP_HEADS
    ranks = dps // groups
    rank_bits = ranks.bit_length() - 1
    clips = condition.shape[1]
    text_local = context[0]
    text_own = text_local.shape[0]
    half = fsdp // 2
    group_me = ds.me // ranks
    rank_me = ds.me % ranks
    core = ds.me % 2

    def frame_view(values):
        return values.reshape(frames, FRAME_TOK, values.shape[-1])

    def group_swap(pieces):
        return [pieces[0]] + [ds.swap(pieces[s], s * ranks) for s in range(1, groups)]

    def group_exchange(keep, send, *first):
        other = ds.swap(send, 1)
        pieces = [
            jnp.stack([pick(keep, group_me ^ s, 1), pick(other, group_me ^ s, 1)])
            for s in range(groups)
        ]
        return group_swap([held(piece, *first) for piece in pieces])

    def group_return(pieces):
        own = group_swap(pieces)
        return own, ds.swap(jnp.stack([piece[1] for piece in own]), 1)

    own_frames = segment_ids[0][::FRAME_TOK].astype(F32)
    own_frame_ids = frame_ids[0].reshape(frames, FRAME_TOK)[:, 0].astype(F32)
    met = jnp.stack(xs.gather(jnp.concatenate([own_frames, own_frame_ids])))
    core_info = core.astype(jnp.int32)[None]
    group_info = group_me.astype(jnp.int32)[None]
    both_info = jnp.concatenate([core_info, group_info])

    silu_cond = jax.nn.silu(condition[0]).astype(BF16)
    cond_rel = jnp.concatenate(xs.gather(silu_cond))
    rows = w_qkv.shape[0]
    quarter = rows // 4

    def columns_of(weight, first, count, s):
        return jnp.concatenate(
            [
                lax.dynamic_slice(
                    weight, (first, p * width + (xs.me ^ s) * own_width), (count, own_width)
                )
                for p in range(3)
            ],
            axis=1,
        )

    fetched = []
    for s in range(1, fsdp):
        wanted = columns_of(w_qkv, (ds.me % 4) * quarter, quarter, s)
        wanted, cond_rel = beside(wanted, cond_rel)
        quarters = [(0, xs.swap(wanted, s))]
        for mask in (2, 1):
            quarters += [(m ^ mask, ds.swap(v, mask)) for m, v in quarters]
        fetched += [(s, m, v) for m, v in quarters]
    cond_own = xs.own_block(cond_rel, 1)
    mod_part = mxu(cond_own, w_modulate).reshape(fsdp, clips, -1)
    modulation = mod_part[0]
    for s in range(1, fsdp):
        modulation = modulation + xs.swap(mod_part[s], s)

    own_seg = lax.dynamic_slice_in_dim(own_frames, ds.me * frames, frames)
    onehot = (own_seg[:, None] == jnp.arange(clips, dtype=F32)[None, :]).astype(F32)
    per_frame = jnp.dot(onehot, modulation, precision=HIGHEST)[:, None, :]
    scale_attn, gate_attn, scale_ffn, gate_ffn = jnp.split(per_frame, 4, axis=2)

    states_f = frame_view(rows_in)
    unit_in, inv_in = unit_rms(states_f)
    normed = (unit_in * gain_attn_in * (1.0 + scale_attn)).astype(BF16).reshape(tokens, width)
    normed, met, w_there = beside(normed, met, w_qkv)
    normed_all = jnp.stack(xs.gather(normed))
    w_cols = lax.dynamic_update_slice_in_dim(
        jnp.zeros((width, 3 * own_width), BF16), columns_of(w_there, 0, rows, 0), xs.me * rows, 0
    )
    for s, m, v in fetched:
        at = (xs.me ^ s) * rows + ((ds.me % 4) ^ m) * quarter
        w_cols = lax.dynamic_update_slice_in_dim(w_cols, v, at, 0)

    stream_seg = met[:, : own_frames.shape[0]].astype(jnp.int32)
    rel_frame_ids = met[:, own_frames.shape[0] :]
    core_seg = lax.dynamic_slice_in_dim(stream_seg, core * half, half, 0)
    masks = [s * ranks for s in range(groups)]
    for b in reversed(range(1, rank_bits)):
        masks = masks + [m ^ (1 << b) for m in masks]
    place_dev = jnp.stack([ds.me ^ (m ^ c) for m in masks for c in range(2)])
    q_dev = jnp.stack([ds.me ^ (s * ranks ^ c) for s in range(groups) for c in range(2)])
    in_frames = lambda dev: (dev[:, None] * frames + jnp.arange(frames)[None, :]).reshape(-1)
    kv_seg = jnp.take(core_seg, in_frames(place_dev), axis=1)
    q_seg = jnp.take(core_seg, in_frames(q_dev), axis=1)
    order = jnp.arange(kv_seg.shape[1])
    less = kv_seg[:, None, :] < kv_seg[:, :, None]
    tie = (kv_seg[:, None, :] == kv_seg[:, :, None]) & (order[None, None, :] < order[None, :, None])
    kv_rank = jnp.sum((less | tie).astype(jnp.int32), axis=2)
    q_start = jnp.sum((kv_seg[:, None, :] < q_seg[:, :, None]).astype(jnp.int32), axis=2)
    q_count = jnp.sum((kv_seg[:, None, :] == q_seg[:, :, None]).astype(jnp.int32), axis=2)
    tables = (kv_rank, q_start, q_count, jnp.maximum(q_seg, 0), place_dev.astype(jnp.int32))
    cosine, sine = rope_lanes(jnp.repeat(rel_frame_ids, FRAME_TOK, axis=1).reshape(-1))
    cosine = cosine.reshape(fsdp, tokens, 128)
    sine = sine.reshape(fsdp, tokens, 128)

    text_rel = jnp.concatenate(
        [xs.own_block(text_local, 1)]
        + [xs.swap(xs.own_block(text_local, 1, s), s) for s in range(1, fsdp)]
    )
    text_part = mxu(text_rel, w_text_kv).reshape(fsdp, text_own, 2, fsdp, own_width)
    text_raw = pick(text_part, xs.me, 3)
    for s in range(1, fsdp):
        piece = pick(text_part, xs.me ^ s, 3)
        piece = jnp.stack([piece[s ^ k] for k in range(fsdp)])
        text_raw = text_raw + xs.swap(piece.astype(BF16), s).astype(F32)
    text_raw = pad_parts(text_raw.reshape(fsdp, text_own, 2 * own_width), 2)

    gains = gain_rows(gain_query, gain_key, gain_text_key)
    send_q, send_kv, keep_q, keep_kv = make_heads(
        core_info, normed_all, w_cols, text_raw, cosine, sine, gains, groups
    )

    kv = group_exchange(keep_kv, send_kv)
    kv_first = kv[1:]
    for b in reversed(range(1, rank_bits)):
        kv = kv + [ds.swap(v, 1 << b) for v in kv]
    query = group_exchange(keep_q, send_q, *kv_first)
    tanh_gate = jnp.tanh(cross_gate)
    first_head = xs.me * own_heads + group_me * GROUP_HEADS
    gate_row = jnp.repeat(lax.dynamic_slice_in_dim(tanh_gate, first_head, GROUP_HEADS), HD)[None, :]

    mixed, kept = attn_fwd(tables, kv, query, gate_row)
    mixed_own, mixed_other = group_return(mixed)
    mixed_low, mix_first, mix_rest = out_project(
        both_info, mixed_own, mixed_other, w_out, fsdp, tokens
    )

    def swapped_sum(first, rest):
        for s in range(1, fsdp):
            first = first + xs.swap(rest[s - 1], s).astype(F32)
        return first

    late_ids = held(rel_frame_ids, mix_first)
    set_of = lambda values, which: lax.dynamic_slice_in_dim(values, which * half, half, 0)
    near_ids = jnp.stack(
        [set_of(late_ids, core), ds.swap(set_of(late_ids, 1 - core), 1)], axis=1
    )
    far_ids = jnp.stack([near_ids] + [ds.swap(near_ids, s * ranks) for s in range(1, groups)])
    normed_two = jnp.stack(
        [set_of(normed_all, core), ds.swap(set_of(normed_all, 1 - core), 1)]
    )
    late_normed = held(normed_two, *mixed_own)
    text_every = lax.all_gather(held(text_rel, *mixed_own), "dp", axis=0, tiled=True)
    if groups > 1:
        members = [[g * ranks + r for g in range(groups)] for r in range(ranks)]
        normed_group = lax.all_gather(late_normed, "dp", axis_index_groups=members)
    else:
        normed_group = late_normed[None]
    far_cos, far_sin = rope_lanes(jnp.repeat(far_ids.reshape(-1), FRAME_TOK))
    far_shape = (groups, half, 2 * tokens, 128)
    far_cos = far_cos.reshape(far_shape)
    far_sin = far_sin.reshape(far_shape)
    mix_got = [xs.swap(mix_rest[s - 1], s) for s in range(1, fsdp)]
    mix_got = [held(v, far_cos, far_sin) for v in mix_got]
    for v in mix_got:
        mix_first = mix_first + v.astype(F32)
    mixed_out = frame_view(mix_first)
    unit_mix, inv_mix = unit_rms(mixed_out)
    tanh_attn = jnp.tanh(gate_attn)
    after = states_f + tanh_attn * unit_mix * gain_attn_out
    unit_ffn, inv_ffn = unit_rms(after)
    ffn_low = (unit_ffn * gain_ffn_in * (1.0 + scale_ffn)).astype(BF16).reshape(tokens, width)
    ffn_all = xs.gather(ffn_low)
    gate_part = [mxu(x, w_gate_up[0]) for x in ffn_all]
    up_part = [mxu(x, w_gate_up[1]) for x in ffn_all]
    hidden = [(jax.nn.silu(g) * u).astype(BF16) for g, u in zip(gate_part, up_part)]
    ffn_out = swapped_sum(
        mxu(hidden[0], w_down), [mxu(h, w_down).astype(BF16) for h in hidden[1:]]
    )
    ffn_out = frame_view(ffn_out)
    unit_out, inv_out = unit_rms(ffn_out)
    tanh_ffn = jnp.tanh(gate_ffn)
    output = after + tanh_ffn * unit_out * gain_ffn_out

    def frame_sum(values):
        return jnp.sum(values, axis=1)

    cot = frame_view(cotangent[0])
    cot_unit = frame_sum(cot * unit_out)
    grad_gate_ffn = cot_unit * gain_ffn_out * (1.0 - tanh_ffn[:, 0] ** 2)
    grad_gain_ffn_out = jnp.sum(cot_unit * tanh_ffn[:, 0], axis=0)
    grad_ffn_low = (
        unit_back(cot * (tanh_ffn * gain_ffn_out), unit_out, inv_out)
        .astype(BF16)
        .reshape(tokens, width)
    )
    grad_ffn_all = xs.gather(grad_ffn_low)
    grad_gate = []
    grad_up = []
    for g, u, d in zip(gate_part, up_part, grad_ffn_all):
        grad_hidden = mxu(d, w_down, ((1,), (1,)))
        sig = jax.nn.sigmoid(g)
        grad_gate.append((grad_hidden * u * (sig * (1.0 + g * (1.0 - sig)))).astype(BF16))
        grad_up.append((grad_hidden * (g * sig)).astype(BF16))

    def ffn_in_part(s):
        return mxu(grad_gate[s], w_gate_up[0], ((1,), (1,))) + mxu(
            grad_up[s], w_gate_up[1], ((1,), (1,))
        )

    def reduce_rows(term):
        return lax.psum_scatter(term, "dp", scatter_dimension=0, tiled=True).astype(F32)

    ffn_rest = [xs.swap(ffn_in_part(s).astype(BF16), s) for s in range(1, fsdp)]
    ffn_grads = ffn_weights(ffn_all, grad_ffn_all, grad_gate, grad_up, hidden)
    ffn_grads, grad_ffn_in, *ffn_rest = beside(ffn_grads, ffn_in_part(0), *ffn_rest)
    for v in ffn_rest:
        grad_ffn_in = grad_ffn_in + v.astype(F32)
    grad_ffn_in = frame_view(grad_ffn_in)
    inner = w_down.shape[0]
    ffn_sums = reduce_rows(ffn_grads)
    grad_unit = frame_sum(grad_ffn_in * unit_ffn)
    grad_scale_ffn = grad_unit * gain_ffn_in
    grad_gain_ffn_in = jnp.sum(grad_unit * (1.0 + scale_ffn[:, 0]), axis=0)
    grad_after = cot + unit_back(
        grad_ffn_in * (gain_ffn_in * (1.0 + scale_ffn)), unit_ffn, inv_ffn
    )
    after_unit = frame_sum(grad_after * unit_mix)
    grad_gate_attn = after_unit * gain_attn_out * (1.0 - tanh_attn[:, 0] ** 2)
    grad_gain_attn_out = jnp.sum(after_unit * tanh_attn[:, 0], axis=0)
    grad_mix_low = (
        unit_back(grad_after * (tanh_attn * gain_attn_out), unit_mix, inv_mix)
        .astype(BF16)
        .reshape(tokens, width)
    )
    grad_mix_all = held(jnp.stack(xs.gather(grad_mix_low)), normed_group, text_every)

    send_grad, keep_grad = out_back(core_info, grad_mix_all, w_out, groups)
    grad_group = group_exchange(keep_grad, send_grad)
    out_grad = mxu(
        grad_mix_all.reshape(fsdp * tokens, width),
        mixed_low.reshape(fsdp * tokens, own_width),
        ((0,), (0,)),
    ).astype(BF16)
    out_grad, *grad_group = beside(out_grad, *grad_group)
    dquery, dkv, dgate = attn_bwd(tables, kv, query, grad_group, kept, gate_row)
    for b in range(1, rank_bits):
        count = len(dkv) // 2
        dkv = [
            (dkv[i].astype(F32) + ds.swap(dkv[count + i], 1 << b).astype(F32)).astype(BF16)
            for i in range(count)
        ]

    w_tri = jnp.concatenate(
        [
            lax.dynamic_slice_in_dim(
                w_cols, p * own_width + group_me * GROUP_WIDTH, GROUP_WIDTH, 1
            )
            for p in range(2)
        ],
        axis=1,
    )
    tri_gain = jnp.concatenate([jnp.tile(gain_query, GROUP_HEADS), jnp.tile(gain_key, GROUP_HEADS)])
    tri_gain = jnp.pad(tri_gain[None, :], ((0, 7), (0, 0)))
    proj_pieces, qkv_grad, gain_qk = proj_back(
        group_info,
        normed_group,
        w_tri,
        dquery,
        dkv,
        far_cos,
        far_sin,
        tri_gain,
    )
    per = width // (fsdp * ranks)
    part = qkv_grad.reshape(fsdp, ranks, per, 3 * GROUP_WIDTH)
    parts = []
    for b in range(rank_bits):
        part = part.reshape(fsdp, part.shape[1] // 2, 2, per, 3 * GROUP_WIDTH)
        mine = (rank_me >> b) & 1
        got = ds.swap(pick(part, 1 - mine, 2), 1 << b)
        part = (pick(part, mine, 2).astype(F32) + got.astype(F32)).astype(BF16)
        parts.append(part)
    proj_own = [held(piece, parts[0]) for piece in group_swap(proj_pieces)]
    proj_other = ds.swap(jnp.stack([piece[1] for piece in proj_own]), 1)
    part = part[:, 0]
    part_own = pick(part, xs.me)
    part_sent = [pick(part, xs.me ^ s) for s in range(1, fsdp)]
    proj_other = held(proj_other, part_own, ffn_sums, *part_sent)
    in_first, in_rest, grad_text, gain_text = in_back(
        both_info, proj_own, proj_other, w_cols, text_raw, gains, tokens
    )
    part_got = [held(xs.swap(v, s + 1), in_first) for s, v in enumerate(part_sent)]
    part = jnp.stack([part_own] + part_got)
    part = jnp.stack([pick(part, xs.me ^ k) for k in range(fsdp)])
    blocks = jnp.transpose(part.reshape(fsdp, per, 3, GROUP_WIDTH), (2, 0, 1, 3))
    blocks = blocks.reshape(3 * fsdp, per, GROUP_WIDTH)
    in_got = [xs.swap(in_rest[s - 1], s) for s in range(1, fsdp)]
    if groups > 1:
        window = 3 * heads // GROUP_HEADS // groups
        slots = -(-window // groups)
        first_of = lambda target, source: (window * target - source + groups - 1) // groups
        sent = []
        for s in range(groups):
            first = first_of(group_me ^ s, group_me)
            sent.append(
                jnp.stack(
                    [pick(blocks, jnp.clip(first + t, 0, 3 * fsdp - 1)) for t in range(slots)]
                )
            )
        in_got = [held(v, *sent) for v in in_got]
    for v in in_got:
        in_first = in_first + v.astype(F32)
    grad_normed = frame_view(in_first)
    in_unit = frame_sum(grad_normed * unit_in)
    grad_scale_attn = in_unit * gain_attn_in
    grad_gain_attn_in = jnp.sum(in_unit * (1.0 + scale_attn[:, 0]), axis=0)
    grad_input = grad_after + unit_back(
        grad_normed * (gain_attn_in * (1.0 + scale_attn)), unit_in, inv_in
    )
    if groups > 1:
        got = held(jnp.stack(group_swap(sent)), grad_gain_attn_in, grad_scale_attn)
        got = got.reshape(groups * slots, per, GROUP_WIDTH)
        ordered = []
        for k in range(window):
            block = window * group_me + k
            source = block % groups
            slot = block // groups - first_of(group_me, source)
            ordered.append(pick(got, (source ^ group_me) * slots + slot))
        blocks = jnp.stack(ordered)
    columns = jnp.swapaxes(blocks, 0, 1).reshape(per, ranks, 3 * width // dps)
    columns = jnp.swapaxes(columns, 0, 1)
    if ranks <= 4:
        got = jnp.stack(
            [pick(columns, rank_me)]
            + [ds.swap(pick(columns, rank_me ^ m), m) for m in range(1, ranks)]
        )
        got = jnp.stack([pick(got, rank_me ^ r) for r in range(ranks)])
    else:
        got = lax.all_to_all(columns, "dp", 0, 0, tiled=True)
    grad_w_qkv = got.reshape(rows, 3 * width // dps).astype(F32)

    grad_w_gate_up = jnp.stack([ffn_sums[:, :inner], ffn_sums[:, inner : 2 * inner]])
    grad_w_down = jnp.transpose(ffn_sums[:, 2 * inner :])

    out_grad, ffn_sums = beside(out_grad, ffn_sums)
    grad_w_out = jnp.transpose(reduce_rows(out_grad))
    def gather_columns(values, parts):
        wide = values.shape[2] // parts
        cut = values.reshape(fsdp, values.shape[1], parts, wide)[..., :own_width]
        got = [cut]
        for s in range(1, fsdp):
            other = xs.swap(cut, s)
            got.append(jnp.stack([other[s ^ k] for k in range(fsdp)]))
        got = jnp.stack(got)
        whole = jnp.stack([pick(got, xs.me ^ k) for k in range(fsdp)], axis=3)
        return whole.reshape(fsdp * values.shape[1], parts * fsdp * own_width)

    grad_text_all = gather_columns(grad_text, 2)
    text_cols = grad_text_all.shape[1] // dps
    grad_text_cols = jnp.swapaxes(grad_text_all.reshape(fsdp * text_own, dps, text_cols), 0, 1)
    grad_text_cols = lax.all_to_all(grad_text_cols, "dp", 0, 0, tiled=True)
    grad_w_text_kv = mxu(text_every, grad_text_cols.reshape(-1, text_cols), ((0,), (0,)))

    frame_grads = jnp.concatenate(
        [grad_scale_attn, grad_gate_attn, grad_scale_ffn, grad_gate_ffn], axis=1
    )
    clip_grads = jnp.dot(jnp.transpose(onehot), frame_grads, precision=HIGHEST)
    mod_cols = clip_grads.shape[1] // dps
    clip_grads = jnp.swapaxes(clip_grads.reshape(clips, dps, mod_cols), 0, 1)
    clip_grads = jnp.sum(lax.all_to_all(clip_grads, "dp", 0, 0, tiled=True), axis=0)
    clip_rel = jnp.concatenate(xs.gather(clip_grads))
    grad_w_modulate = jnp.dot(jnp.transpose(cond_own.astype(F32)), clip_rel, precision=HIGHEST)
    head_term = jnp.sum(dgate.reshape(GROUP_HEADS, HD), axis=1)
    gate_term = lax.dynamic_update_slice_in_dim(jnp.zeros((heads,), F32), head_term, first_head, 0)
    gate_term = gate_term * (1.0 - tanh_gate * tanh_gate)
    qk_sums = jnp.sum(gain_qk[0].reshape(2, GROUP_HEADS, HD), axis=1)
    small = [
        grad_gain_attn_in,
        grad_gain_attn_out,
        grad_gain_ffn_in,
        grad_gain_ffn_out,
        qk_sums[0],
        qk_sums[1],
        gain_text[0, :HD] + gain_text[0, HD:],
        gate_term,
    ]
    sizes = [v.shape[0] for v in small]
    packed = jnp.concatenate(small)
    packed = jnp.pad(packed, (0, -packed.shape[0] % 1024)).reshape(-1, 128)
    for moves in (ds, xs):
        for b in range(moves.size.bit_length() - 1):
            packed = packed + moves.swap(packed, 1 << b)
    packed = packed.reshape(-1)
    sums = []
    at = 0
    for size in sizes:
        sums.append(packed[at : at + size])
        at += size
    return (
        output.reshape(1, tokens, width),
        grad_input.reshape(1, tokens, width),
        grad_w_modulate,
        grad_w_qkv,
        grad_w_text_kv,
        grad_w_out,
        grad_w_gate_up,
        grad_w_down,
        *sums,
    )


def solution(mesh):
    rows = P("fsdp", "dp", None)
    first = P("fsdp", None)
    split = P("fsdp", "dp")
    return jax.shard_map(
        functools.partial(per_device, mesh.shape["fsdp"], mesh.shape["dp"]),
        mesh=mesh,
        in_specs=(
            rows,
            rows,
            first,
            split,
            P("fsdp", None, None),
            rows,
            first,
            first,
            first,
            first,
            P(None, None, "fsdp"),
            first,
        )
        + (P(),) * 8,
        out_specs=(
            rows,
            rows,
            split,
            split,
            split,
            split,
            P(None, "dp", "fsdp"),
            split,
        )
        + (P(),) * 8,
        check_vma=False,
    )
```

```python
import functools
import math

import jax
import jax.numpy as jnp
import numpy as np
from jax import lax
from jax.experimental import pallas as pl
from jax.experimental.pallas import tpu as pltpu
from jax.sharding import PartitionSpec as P

HD = 64
CTX = 256
FRAME_TOK = 128
PW = 16
EPSILON = 1e-06
GROUP_HEADS = 3
GROUP_WIDTH = GROUP_HEADS * HD
STACK = GROUP_HEADS * FRAME_TOK
ONES_ROWS = 16
HIGHEST = lax.Precision.HIGHEST
BF16 = jnp.bfloat16
F32 = jnp.float32
SCALE = HD ** (-0.5)
EXP2_SCALE = SCALE * math.log2(math.e)
MIB = 1 << 20
COST_CUT = 100


def mxu(a, b, dims=((1,), (0,))):
    return lax.dot_general(a, b, (dims, ((), ())), preferred_element_type=F32)


class Moves:
    def __init__(self, axis, size):
        self.axis = axis
        self.size = size
        self.me = lax.axis_index(axis)

    def swap(self, value, mask):
        return lax.ppermute(value, self.axis, [(i, i ^ mask) for i in range(self.size)])

    def gather(self, value):
        return [value] + [self.swap(value, s) for s in range(1, self.size)]

    def scatter_sum(self, parts):
        total = parts[0].astype(F32)
        for s in range(1, self.size):
            total = total + self.swap(parts[s].astype(BF16), s).astype(F32)
        return total

    def reorder(self, value, axis):
        block = value.shape[axis] // self.size
        return jnp.concatenate(
            [
                lax.dynamic_slice_in_dim(value, (self.me ^ s) * block, block, axis)
                for s in range(self.size)
            ],
            axis,
        )

    def own_block(self, value, axis, s=0):
        block = value.shape[axis] // self.size
        return lax.dynamic_slice_in_dim(value, (self.me ^ s) * block, block, axis)


def lane_tiles(width):
    return -(-width // 128) * 128


def turn(values, cosine, sine):
    lane = lax.broadcasted_iota(jnp.int32, values.shape, 1)
    other = jnp.where(lane % 2 == 0, pltpu.roll(values, 127, 1), pltpu.roll(values, 1, 1))
    return values * cosine + other * sine


def head_means(values, ones):
    upper = values.astype(BF16)
    lower = (values - upper.astype(F32)).astype(BF16)
    return mxu(jnp.concatenate([upper, lower], axis=1), ones) * (1.0 / HD)


def joined(pieces, axis):
    return jnp.concatenate(pieces, axis=axis) if len(pieces) > 1 else pieces[0]


def widened(values):
    missing = lane_tiles(values.shape[1]) - values.shape[1]
    if not missing:
        return values
    return jnp.concatenate([values, jnp.zeros((values.shape[0], missing), values.dtype)], axis=1)


def tiles_of(values):
    return [values[:, 128 * t : 128 * (t + 1)] for t in range(values.shape[1] // 128)]


def normed_heads(raw, ones, gain):
    return [x * lax.rsqrt(head_means(x * x, ones) + EPSILON) * gain for x in tiles_of(raw)]


def head_ones():
    lane = np.arange(128) // HD
    ones = (lane[:, None] == lane[None, :]).astype(np.float32)
    return jnp.asarray(np.concatenate([ones, ones]), BF16)


def group_cut(values, g):
    return values[:, GROUP_WIDTH * g : GROUP_WIDTH * (g + 1)]


def packed_frames(values, frames):
    return joined([values[FRAME_TOK * f : FRAME_TOK * (f + 1)] for f in range(frames)], 1)


def call(kernel, name, grid, prefetch, in_specs, out_specs, out_shape, scratch, vmem, flops, moved, args):
    return pl.pallas_call(
        kernel,
        grid_spec=pltpu.PrefetchScalarGridSpec(
            num_scalar_prefetch=prefetch,
            grid=grid,
            in_specs=in_specs,
            out_specs=out_specs,
            scratch_shapes=scratch,
        ),
        out_shape=out_shape,
        compiler_params=pltpu.CompilerParams(
            dimension_semantics=("arbitrary",) * len(grid), vmem_limit_bytes=vmem
        ),
        cost_estimate=pl.CostEstimate(
            flops=int(flops) // COST_CUT, bytes_accessed=int(moved) // COST_CUT, transcendentals=0
        ),
        name=name,
    )(*args)


def whole_spec(shape):
    zeros = (0,) * len(shape)
    return pl.BlockSpec(shape, lambda *_: zeros)


def heads_kernel(
    core_ref,
    x_ref,
    w_ref,
    text_ref,
    cos_ref,
    sin_ref,
    gain_ref,
    ones_ref,
    send_q,
    send_kv,
    keep_q,
    keep_kv,
    *,
    half,
    groups,
    frames,
    own_width,
):
    step = pl.program_id(0)
    tokens = frames * FRAME_TOK
    ones = ones_ref[...]
    parts = []
    for p in range(3):
        raw = widened(mxu(x_ref[0], w_ref[:, own_width * p : own_width * (p + 1)]))
        if p < 2:
            raw = joined(
                [
                    turn(x, cos_ref[0], sin_ref[0])
                    for x in normed_heads(raw, ones, gain_ref[p : p + 1, :])
                ],
                1,
            )
        parts.append(raw.astype(BF16))
    wide = text_ref.shape[2] // 2
    text_key = joined(normed_heads(text_ref[0, :, :wide], ones, gain_ref[2:3, :]), 1).astype(BF16)
    text_value = text_ref[0, :, wide:].astype(BF16)

    def put(q_ref, kv_ref):
        for g in range(groups):
            q_ref[0, g] = packed_frames(group_cut(parts[0], g), frames)
            kv_ref[0, g, :tokens] = joined([group_cut(parts[1], g), group_cut(parts[2], g)], 1)
            kv_ref[0, g, tokens:] = joined([group_cut(text_key, g), group_cut(text_value, g)], 1)

    @pl.when(step < half)
    def _():
        put(send_q, send_kv)

    @pl.when(step >= half)
    def _():
        put(keep_q, keep_kv)


def set_stream(step, core, half):
    other = jnp.where(step < half, 1 - core, core)
    return other * half + step % half


def make_heads(core, x, w_cols, text_raw, cosine, sine, gains, groups):
    streams, tokens, width = x.shape
    half = streams // 2
    frames = tokens // FRAME_TOK
    own_width = w_cols.shape[1] // 3
    text_own = text_raw.shape[1]
    by_stream = lambda i, core: (set_stream(i, core[0], half), 0, 0)
    q_block = (1, groups, FRAME_TOK, frames * GROUP_WIDTH)
    kv_block = (1, groups, tokens + text_own, 2 * GROUP_WIDTH)
    first = lambda i, core: (jnp.minimum(i, half - 1), 0, 0, 0)
    second = lambda i, core: (jnp.maximum(i - half, 0), 0, 0, 0)
    return call(
        functools.partial(
            heads_kernel, half=half, groups=groups, frames=frames, own_width=own_width
        ),
        "make_heads",
        (streams,),
        1,
        [
            pl.BlockSpec((1, tokens, width), by_stream),
            whole_spec(w_cols.shape),
            pl.BlockSpec((1,) + text_raw.shape[1:], by_stream),
            pl.BlockSpec((1, tokens, 128), by_stream),
            pl.BlockSpec((1, tokens, 128), by_stream),
            whole_spec((8, 128)),
            whole_spec((256, 128)),
        ],
        [
            pl.BlockSpec(q_block, first),
            pl.BlockSpec(kv_block, first),
            pl.BlockSpec(q_block, second),
            pl.BlockSpec(kv_block, second),
        ],
        [
            jax.ShapeDtypeStruct((half,) + q_block[1:], BF16),
            jax.ShapeDtypeStruct((half,) + kv_block[1:], BF16),
        ]
        * 2,
        [],
        48 * MIB,
        2 * x.size * w_cols.shape[1],
        x.size * 2 + w_cols.size * 2 + x.size * 3,
        (core, x, w_cols, text_raw, cosine, sine, gains, head_ones()),
    )


BIG = 4
CLIP = 16


def over_tiles(start, count, body):
    whole = count // CLIP
    rest = count - whole * CLIP
    big = rest // BIG
    at = lambda frame: pl.multiple_of(frame * FRAME_TOK, FRAME_TOK)

    def whole_step(t, carry):
        body(at(start + t * CLIP), BIG * FRAME_TOK, CLIP // BIG)
        return carry

    def big_step(t, carry):
        body(at(start + whole * CLIP + t * BIG), BIG * FRAME_TOK, 1)
        return carry

    def small_step(t, carry):
        body(at(start + whole * CLIP + big * BIG + t), FRAME_TOK, 1)
        return carry

    lax.fori_loop(0, whole, whole_step, 0)
    lax.fori_loop(0, big, big_step, 0)
    lax.fori_loop(0, rest - big * BIG, small_step, 0)


def stacked(values, mask):
    return jnp.concatenate([values] * GROUP_HEADS, axis=0) * mask


def diagonal(values):
    own = [
        values[HD * h : HD * (h + 1), FRAME_TOK * h : FRAME_TOK * (h + 1)]
        for h in range(GROUP_HEADS)
    ]
    return jnp.transpose(jnp.concatenate(own, axis=0))


def head_row(values):
    flipped = jnp.transpose(values)
    return jnp.concatenate(
        [
            jnp.sum(flipped[HD * h : HD * (h + 1), :], axis=0, keepdims=True)
            for h in range(GROUP_HEADS)
        ],
        axis=1,
    )


def each_chunk(kv_refs, rank_ref, place_ref, s, frames, chunk_text, self_rows, frame_body, text_body):
    tokens = frames * FRAME_TOK
    for i, ref in enumerate(kv_refs):

        def one(c, carry, i=i, ref=ref):
            chunk = 2 * i + c
            for f in range(frames):
                at = pl.multiple_of(rank_ref[s, chunk * frames + f] * FRAME_TOK, FRAME_TOK)
                frame_body(ref, c, slice(f * FRAME_TOK, (f + 1) * FRAME_TOK), at)
            at = pl.multiple_of(self_rows + place_ref[chunk] * chunk_text, chunk_text)
            text_body(ref, c, slice(tokens, tokens + chunk_text), at)
            return carry

        lax.fori_loop(0, 2, one, 0)


def unpack_frames(refs, scratch, frames):
    for i, ref in enumerate(refs):
        for c in range(2):
            for f in range(frames):
                scratch[(2 * i + c) * frames + f] = ref[
                    c, :, GROUP_WIDTH * f : GROUP_WIDTH * (f + 1)
                ]


def attn_fwd_kernel(*refs, pieces, groups, frames, chunk_text):
    rank_ref, start_ref, count_ref, clip_ref, place_ref = refs[:5]
    refs = refs[5:]
    kv_refs, refs = refs[:pieces], refs[pieces:]
    q_refs, refs = refs[:groups], refs[groups:]
    gate_ref, mask_ref = refs[:2]
    mixed_refs, refs = refs[2 : 2 + groups], refs[2 + groups :]
    self_ref, text_ref, lse_ref, keys, values, rows_text, queries, mixes, acc = refs
    s = pl.program_id(0)
    j = pl.program_id(1)
    self_rows = pieces * 2 * frames * FRAME_TOK
    text_rows = rows_text.shape[0]
    K = slice(0, GROUP_WIDTH)
    V = slice(GROUP_WIDTH, 2 * GROUP_WIDTH)

    @pl.when(j == 0)
    def _():
        values[GROUP_WIDTH:, :] = jnp.ones((ONES_ROWS, values.shape[1]), BF16)

        def frame_body(ref, c, rows, at):
            keys[pl.ds(at, FRAME_TOK), :] = ref[c, rows, K]
            values[:GROUP_WIDTH, pl.ds(at, FRAME_TOK)] = jnp.transpose(ref[c, rows, V])

        def text_body(ref, c, rows, at):
            keys[pl.ds(at, chunk_text), :] = ref[c, rows, K]
            rows_text[pl.ds(at - self_rows, chunk_text), :] = ref[c, rows, V]

        each_chunk(
            kv_refs, rank_ref, place_ref, s, frames, chunk_text, self_rows, frame_body, text_body
        )
        for b in range(text_rows // 128):
            values[:GROUP_WIDTH, self_rows + 128 * b : self_rows + 128 * (b + 1)] = jnp.transpose(
                rows_text[128 * b : 128 * (b + 1), :]
            )
        unpack_frames(q_refs, queries, frames)

    query = stacked(queries[j], mask_ref[...])

    def tile(base, size, times):
        total = None
        for t in range(times):
            rows = pl.ds(pl.multiple_of(base + t * size, FRAME_TOK), size)
            scores = mxu(keys[rows, :], query, ((1,), (1,)))
            weights = jnp.exp2(scores * EXP2_SCALE).astype(BF16)
            part = mxu(values[:, rows], weights)
            total = part if total is None else total + part
        acc[...] += total

    def finish(row):
        total = acc[GROUP_WIDTH : GROUP_WIDTH + 1, :]
        lse_ref[0, 0, row : row + 1, :] = jnp.log(total) * math.log2(math.e)
        return diagonal(acc[:GROUP_WIDTH, :] * (1.0 / total))

    acc[...] = jnp.zeros_like(acc)
    over_tiles(start_ref[s, j], count_ref[s, j], tile)
    self_out = finish(0)
    acc[...] = jnp.zeros_like(acc)
    tile(pl.multiple_of(self_rows + clip_ref[s, j] * CTX, 128), CTX, 1)
    text_out = finish(1)
    self_ref[0, 0] = self_out
    text_ref[0, 0] = text_out
    mixes[j] = (self_out + gate_ref[...] * text_out).astype(BF16)

    @pl.when(j == pl.num_programs(1) - 1)
    def _():
        for g, ref in enumerate(mixed_refs):
            for c in range(2):
                at = (2 * g + c) * frames
                ref[c] = joined([mixes[at + f] for f in range(frames)], 1)


def attn_bwd_kernel(*refs, pieces, groups, frames, chunk_text):
    rank_ref, start_ref, count_ref, clip_ref, place_ref = refs[:5]
    refs = refs[5:]
    kv_refs, refs = refs[:pieces], refs[pieces:]
    q_refs, refs = refs[:groups], refs[groups:]
    grad_refs, refs = refs[:groups], refs[groups:]
    self_ref, text_ref, lse_ref, gate_ref, mask_ref, dq_ref = refs[:6]
    dkv_refs, refs = refs[6 : 6 + pieces], refs[6 + pieces :]
    dgate_ref, keys, keys_flip, values, dkeys, dvalues, dquery, queries, grads = refs
    s = pl.program_id(0)
    j = pl.program_id(1)
    self_rows = pieces * 2 * frames * FRAME_TOK
    text_rows = pieces * 2 * chunk_text
    K = slice(0, GROUP_WIDTH)
    V = slice(GROUP_WIDTH, 2 * GROUP_WIDTH)

    @pl.when(jnp.logical_and(s == 0, j == 0))
    def _():
        dgate_ref[...] = jnp.zeros_like(dgate_ref)

    @pl.when(j == 0)
    def _():
        dkeys[...] = jnp.zeros_like(dkeys)
        dvalues[...] = jnp.zeros_like(dvalues)

        def frame_body(ref, c, rows, at):
            keys[pl.ds(at, FRAME_TOK), :] = ref[c, rows, K]
            keys_flip[:, pl.ds(at, FRAME_TOK)] = jnp.transpose(ref[c, rows, K])
            values[pl.ds(at, FRAME_TOK), :] = ref[c, rows, V]

        def text_body(ref, c, rows, at):
            keys[pl.ds(at, chunk_text), :] = ref[c, rows, K]
            values[pl.ds(at, chunk_text), :] = ref[c, rows, V]

        each_chunk(
            kv_refs, rank_ref, place_ref, s, frames, chunk_text, self_rows, frame_body, text_body
        )
        for b in range(text_rows // 128):
            rows = slice(self_rows + 128 * b, self_rows + 128 * (b + 1))
            keys_flip[:, rows] = jnp.transpose(keys[rows, :])
        unpack_frames(q_refs, queries, frames)
        unpack_frames(grad_refs, grads, frames)

    mask = mask_ref[...]
    query = stacked(queries[j], mask)
    grad_low = grads[j]
    grad_wide = grad_low.astype(F32)
    grad_text = (grad_wide * gate_ref[...]).astype(BF16)
    text_out = text_ref[0, 0]
    dgate_ref[...] += jnp.sum(grad_wide * text_out, axis=0, keepdims=True)
    dquery[...] = jnp.zeros_like(dquery)

    def over(grad, out, lse):
        grad_stack = stacked(grad, mask)
        delta = head_row(grad.astype(F32) * out)

        def tile(base, size, times):
            total = None
            for t in range(times):
                rows = pl.ds(pl.multiple_of(base + t * size, FRAME_TOK), size)
                scores = mxu(keys[rows, :], query, ((1,), (1,)))
                weights = jnp.exp2(scores * EXP2_SCALE - lse)
                dweights = mxu(values[rows, :], grad_stack, ((1,), (1,)))
                dscores = (weights * (dweights - delta)).astype(BF16)
                dvalues[rows, :] += mxu(weights.astype(BF16), grad_stack)
                dkeys[rows, :] += mxu(dscores, query)
                part = mxu(keys_flip[:, rows], dscores)
                total = part if total is None else total + part
            dquery[...] += total

        return tile

    over_tiles(start_ref[s, j], count_ref[s, j], over(grad_low, self_ref[0, 0], lse_ref[0, 0, 0:1, :]))
    over(grad_text, text_out, lse_ref[0, 0, 1:2, :])(
        pl.multiple_of(self_rows + clip_ref[s, j] * CTX, 128), CTX, 1
    )
    dq_ref[0, 0] = (diagonal(dquery[...]) * SCALE).astype(BF16)

    @pl.when(j == pl.num_programs(1) - 1)
    def _():
        def frame_body(ref, c, rows, at):
            taken = pl.ds(at, FRAME_TOK)
            ref[c, rows, :] = jnp.concatenate(
                [dkeys[taken, :] * SCALE, dvalues[taken, :]], axis=1
            ).astype(BF16)

        def text_body(ref, c, rows, at):
            taken = pl.ds(at, chunk_text)
            ref[c, rows, :] = jnp.concatenate(
                [dkeys[taken, :] * SCALE, dvalues[taken, :]], axis=1
            ).astype(BF16)

        each_chunk(
            dkv_refs, rank_ref, place_ref, s, frames, chunk_text, self_rows, frame_body, text_body
        )


def attention_specs(kv, query):
    _, streams, chunk_rows, _ = kv[0].shape
    frames = query[0].shape[3] // GROUP_WIDTH
    chunk_text = chunk_rows - frames * FRAME_TOK
    sizes = dict(pieces=len(kv), groups=len(query), frames=frames, chunk_text=chunk_text)
    count = len(query) * 2 * frames
    grid = (streams, count)
    piece = lambda shape: pl.BlockSpec(
        (2, None) + shape, lambda s, j, *_: (0, s, 0, 0), pipeline_mode=pl.Buffered(1)
    )
    kv_spec = piece((chunk_rows, 2 * GROUP_WIDTH))
    q_spec = piece((FRAME_TOK, frames * GROUP_WIDTH))
    tok_spec = pl.BlockSpec((1, 1, FRAME_TOK, GROUP_WIDTH), lambda s, j, *_: (s, j, 0, 0))
    lse_spec = pl.BlockSpec((1, 1, 2, STACK), lambda s, j, *_: (s, j, 0, 0))
    const_specs = [whole_spec((1, GROUP_WIDTH)), whole_spec((STACK, GROUP_WIDTH))]
    return sizes, grid, kv_spec, q_spec, tok_spec, lse_spec, const_specs


def stack_mask():
    head_of_row = np.arange(STACK) // FRAME_TOK
    head_of_lane = np.arange(GROUP_WIDTH) // HD
    return jnp.asarray((head_of_row[:, None] == head_of_lane[None, :]).astype(np.float32), BF16)


def attn_fwd(tables, kv, query, gate):
    sizes, grid, kv_spec, q_spec, tok_spec, lse_spec, const_specs = attention_specs(kv, query)
    total = len(kv) * 2 * kv[0].shape[2]
    text_rows = len(kv) * 2 * sizes["chunk_text"]
    wide = jax.ShapeDtypeStruct(grid + (FRAME_TOK, GROUP_WIDTH), F32)
    got = call(
        functools.partial(attn_fwd_kernel, **sizes),
        "attention",
        grid,
        5,
        [kv_spec] * len(kv) + [q_spec] * len(query) + const_specs,
        [q_spec] * len(query) + [tok_spec, tok_spec, lse_spec],
        [jax.ShapeDtypeStruct(q.shape, BF16) for q in query]
        + [wide, wide, jax.ShapeDtypeStruct(grid + (2, STACK), F32)],
        [
            pltpu.VMEM((total, GROUP_WIDTH), BF16),
            pltpu.VMEM((GROUP_WIDTH + ONES_ROWS, total), BF16),
            pltpu.VMEM((text_rows, GROUP_WIDTH), BF16),
            pltpu.VMEM((grid[1], FRAME_TOK, GROUP_WIDTH), BF16),
            pltpu.VMEM((grid[1], FRAME_TOK, GROUP_WIDTH), BF16),
            pltpu.VMEM((GROUP_WIDTH + ONES_ROWS, STACK), F32),
        ],
        min(60 * MIB, total * 2600 + 16 * MIB),
        grid[0] * grid[1] * STACK * 2304 * GROUP_WIDTH * 8,
        grid[0] * grid[1] * 300000,
        (*tables, *kv, *query, gate, stack_mask()),
    )
    return got[: len(query)], got[len(query) :]


def attn_bwd(tables, kv, query, grad, kept, gate):
    sizes, grid, kv_spec, q_spec, tok_spec, lse_spec, const_specs = attention_specs(kv, query)
    total = len(kv) * 2 * kv[0].shape[2]
    got = call(
        functools.partial(attn_bwd_kernel, **sizes),
        "attention_back",
        grid,
        5,
        [kv_spec] * len(kv)
        + [q_spec] * (2 * len(query))
        + [tok_spec, tok_spec, lse_spec]
        + const_specs,
        [tok_spec] + [kv_spec] * len(kv) + [whole_spec((1, GROUP_WIDTH))],
        [jax.ShapeDtypeStruct(grid + (FRAME_TOK, GROUP_WIDTH), BF16)]
        + [jax.ShapeDtypeStruct(v.shape, BF16) for v in kv]
        + [jax.ShapeDtypeStruct((1, GROUP_WIDTH), F32)],
        [
            pltpu.VMEM((total, GROUP_WIDTH), BF16),
            pltpu.VMEM((GROUP_WIDTH, total), BF16),
            pltpu.VMEM((total, GROUP_WIDTH), BF16),
            pltpu.VMEM((total, GROUP_WIDTH), F32),
            pltpu.VMEM((total, GROUP_WIDTH), F32),
            pltpu.VMEM((GROUP_WIDTH, STACK), F32),
            pltpu.VMEM((grid[1], FRAME_TOK, GROUP_WIDTH), BF16),
            pltpu.VMEM((grid[1], FRAME_TOK, GROUP_WIDTH), BF16),
        ],
        60 * MIB,
        grid[0] * grid[1] * STACK * 2304 * GROUP_WIDTH * 20,
        grid[0] * grid[1] * 500000,
        (*tables, *kv, *query, *grad, *kept, gate, stack_mask()),
    )
    return got[0], got[1 : 1 + len(kv)], got[-1]


def for_group(group, groups, body):
    for v in range(groups):

        @pl.when(group == v)
        def _(v=v):
            body(v)


def out_kernel(info_ref, *refs, half, groups, frames):
    own_refs, refs = refs[:groups], refs[groups:]
    other_ref, w_ref, mixed_ref, first_ref, rest_ref = refs
    k = pl.program_id(0)
    here = (k // half) == info_ref[0]

    def fill(v, take):
        for s in range(groups):
            piece = take(s)
            for f in range(frames):
                mixed_ref[0, FRAME_TOK * f : FRAME_TOK * (f + 1), GROUP_WIDTH * (v ^ s) : GROUP_WIDTH * ((v ^ s) + 1)] = piece[
                    :, GROUP_WIDTH * f : GROUP_WIDTH * (f + 1)
                ]

    @pl.when(here)
    def _():
        for_group(info_ref[1], groups, lambda v: fill(v, lambda s: own_refs[s][0, 0]))

    @pl.when(jnp.logical_not(here))
    def _():
        for_group(info_ref[1], groups, lambda v: fill(v, lambda s: other_ref[s, 0]))

    part = mxu(mixed_ref[0], w_ref[...])

    @pl.when(k == 0)
    def _():
        first_ref[...] = part

    @pl.when(k > 0)
    def _():
        rest_ref[0] = part.astype(BF16)


def out_project(info, own, other, w_out, streams, tokens):
    groups = len(own)
    half = streams // 2
    frames = tokens // FRAME_TOK
    own_width, width = w_out.shape
    lanes = frames * GROUP_WIDTH
    return call(
        functools.partial(out_kernel, half=half, groups=groups, frames=frames),
        "out_project",
        (streams,),
        1,
        [pl.BlockSpec((1, 1, FRAME_TOK, lanes), lambda k, _: (0, k % half, 0, 0))] * groups
        + [
            pl.BlockSpec((groups, 1, FRAME_TOK, lanes), lambda k, _: (0, k % half, 0, 0)),
            whole_spec(w_out.shape),
        ],
        [
            pl.BlockSpec((1, tokens, own_width), lambda k, _: (k, 0, 0)),
            whole_spec((tokens, width)),
            pl.BlockSpec((1, tokens, width), lambda k, _: (jnp.maximum(k - 1, 0), 0, 0)),
        ],
        [
            jax.ShapeDtypeStruct((streams, tokens, own_width), BF16),
            jax.ShapeDtypeStruct((tokens, width), F32),
            jax.ShapeDtypeStruct((streams - 1, tokens, width), BF16),
        ],
        [],
        32 * MIB,
        2 * streams * tokens * own_width * width,
        streams * tokens * width * 6 + w_out.size * 2,
        (info, *own, other, w_out),
    )


def out_back_kernel(core_ref, grad_ref, w_ref, send_ref, keep_ref, *, half, groups, frames):
    step = pl.program_id(0)
    grad = mxu(grad_ref[0], w_ref[...], ((1,), (1,))).astype(BF16)

    def put(ref):
        for g in range(groups):
            ref[0, g] = packed_frames(group_cut(grad, g), frames)

    @pl.when(step < half)
    def _():
        put(send_ref)

    @pl.when(step >= half)
    def _():
        put(keep_ref)


def out_back(core, grad, w_out, groups):
    streams, tokens, width = grad.shape
    half = streams // 2
    frames = tokens // FRAME_TOK
    block = (1, groups, FRAME_TOK, frames * GROUP_WIDTH)
    return call(
        functools.partial(out_back_kernel, half=half, groups=groups, frames=frames),
        "out_back",
        (streams,),
        1,
        [
            pl.BlockSpec((1, tokens, width), lambda i, core: (set_stream(i, core[0], half), 0, 0)),
            whole_spec(w_out.shape),
        ],
        [
            pl.BlockSpec(block, lambda i, core: (jnp.minimum(i, half - 1), 0, 0, 0)),
            pl.BlockSpec(block, lambda i, core: (jnp.maximum(i - half, 0), 0, 0, 0)),
        ],
        [jax.ShapeDtypeStruct((half,) + block[1:], BF16)] * 2,
        [],
        32 * MIB,
        2 * streams * tokens * w_out.size,
        streams * tokens * width * 3 + w_out.size * 2,
        (core, grad, w_out),
    )


def proj_back_kernel(*refs, groups, frames, half, chunk_text):
    group_ref, x_ref, w_ref, dq_ref = refs[:4]
    dkv_refs, refs = refs[4 : 4 + groups], refs[4 + groups :]
    cos_ref, sin_ref, gain_ref, ones_ref = refs[:4]
    out_refs, refs = refs[4 : 4 + groups], refs[4 + groups :]
    dw_ref, dgain_ref, dkv, total = refs
    i = pl.program_id(0)
    tokens = frames * FRAME_TOK

    @pl.when(i == 0)
    def _():
        total[...] = jnp.zeros_like(total)
        dgain_ref[...] = jnp.zeros_like(dgain_ref)

    for g, ref in enumerate(dkv_refs):

        @pl.when(i // half == g)
        def _(ref=ref):
            dkv[...] = ref[...]

    ones = ones_ref[...]
    x = jnp.concatenate([x_ref[0, c, 0] for c in range(2)], axis=0)
    raw = mxu(x, w_ref[...])
    key_grad = jnp.concatenate([dkv[c, :tokens, :GROUP_WIDTH] for c in range(2)], axis=0)
    value_grad = jnp.concatenate([dkv[c, :tokens, GROUP_WIDTH:] for c in range(2)], axis=0)
    query_grad = jnp.concatenate([dq_ref[0, n] for n in range(2 * frames)], axis=0)
    turned = jnp.concatenate([query_grad, key_grad], axis=1).astype(F32)
    done = []
    for t, (x_t, dy) in enumerate(zip(tiles_of(raw), tiles_of(turned))):
        dy = turn(dy, cos_ref[0, 0], -sin_ref[0, 0])
        inv = lax.rsqrt(head_means(x_t * x_t, ones) + EPSILON)
        unit = x_t * inv
        lanes = slice(128 * t, 128 * (t + 1))
        dgain_ref[0:1, lanes] += jnp.sum(dy * unit, axis=0, keepdims=True)
        dn = dy * gain_ref[0:1, lanes]
        done.append((inv * (dn - unit * head_means(dn * unit, ones))).astype(BF16))
    grads = jnp.concatenate(done + [value_grad], axis=1)
    total[...] += mxu(grads, x, ((0,), (0,)))

    def put(ref):
        for c in range(2):
            ref[c, :FRAME_TOK, :] = packed_frames(grads[tokens * c : tokens * (c + 1)], frames)
            rows = slice(tokens, tokens + chunk_text)
            text = dkv[c, rows, :]
            lower = chunk_text // 2
            ref[c, FRAME_TOK:, : 4 * GROUP_WIDTH] = jnp.concatenate(
                [text[:lower], text[lower:]], axis=1
            )
            ref[c, FRAME_TOK:, 4 * GROUP_WIDTH :] = jnp.zeros(
                (lower, ref.shape[2] - 4 * GROUP_WIDTH), BF16
            )

    for g, ref in enumerate(out_refs):

        @pl.when(i // half == g)
        def _(ref=ref):
            put(ref)

    @pl.when(i == pl.num_programs(0) - 1)
    def _():
        for b in range(total.shape[1] // 256):
            lanes = slice(256 * b, 256 * (b + 1))
            dw_ref[lanes, :] = jnp.transpose(total[:, lanes]).astype(BF16)


def proj_back(group, x, w_tri, dq, dkv, cosine, sine, gains):
    groups = len(dkv)
    half = x.shape[2]
    tokens, width = x.shape[3:]
    frames = tokens // FRAME_TOK
    chunk_text = dkv[0].shape[2] - tokens
    lanes = frames * 3 * GROUP_WIDTH
    rows = FRAME_TOK + chunk_text // 2
    got = call(
        functools.partial(
            proj_back_kernel, groups=groups, frames=frames, half=half, chunk_text=chunk_text
        ),
        "proj_back",
        (groups * half,),
        1,
        [
            pl.BlockSpec(
                (1, 2, 1, tokens, width), lambda i, g: (g[0] ^ (i // half), 0, i % half, 0, 0)
            ),
            whole_spec(w_tri.shape),
            pl.BlockSpec(
                (1, 2 * frames, FRAME_TOK, GROUP_WIDTH), lambda i, g: (i % half, i // half, 0, 0)
            ),
        ]
        + [
            pl.BlockSpec((2, None) + dkv[0].shape[2:], lambda i, g: (0, i % half, 0, 0))
        ]
        * groups
        + [
            pl.BlockSpec((1, 1, 2 * tokens, 128), lambda i, g: (i // half, i % half, 0, 0)),
            pl.BlockSpec((1, 1, 2 * tokens, 128), lambda i, g: (i // half, i % half, 0, 0)),
            whole_spec(gains.shape),
            whole_spec((256, 128)),
        ],
        [
            pl.BlockSpec(
                (2, None, rows, lanes),
                lambda i, g, n=n: (0, jnp.clip(i - n * half, 0, half - 1), 0, 0),
            )
            for n in range(groups)
        ]
        + [whole_spec((width, 3 * GROUP_WIDTH)), whole_spec((8, 2 * GROUP_WIDTH))],
        [jax.ShapeDtypeStruct((2, half, rows, lanes), BF16)] * groups
        + [
            jax.ShapeDtypeStruct((width, 3 * GROUP_WIDTH), BF16),
            jax.ShapeDtypeStruct((8, 2 * GROUP_WIDTH), F32),
        ],
        [
            pltpu.VMEM(dkv[0].shape[:1] + dkv[0].shape[2:], BF16),
            pltpu.VMEM((3 * GROUP_WIDTH, width), F32),
        ],
        48 * MIB,
        2 * x.size * GROUP_WIDTH * 5,
        x.size * 4 + w_tri.size * 2,
        (group, x, w_tri, dq, *dkv, cosine, sine, gains, head_ones()),
    )
    return got[:groups], got[groups], got[groups + 1]


def in_back_kernel(info_ref, *refs, half, groups, frames, own_width, chunk_text):
    own_refs, refs = refs[:groups], refs[groups:]
    other_ref, w_ref, raw_ref, gain_ref, ones_ref = refs[:5]
    first_ref, rest_ref, text_ref, dgain_ref, grads, texts = refs[5:]
    k = pl.program_id(0)
    here = (k // half) == info_ref[0]
    wide = lane_tiles(own_width)
    lower = chunk_text // 2

    @pl.when(k == 0)
    def _():
        dgain_ref[...] = jnp.zeros_like(dgain_ref)
        texts[...] = jnp.zeros_like(texts)

    def fill(v, take):
        for s in range(groups):
            piece = take(s)
            at = GROUP_WIDTH * (v ^ s)
            for f in range(frames):
                for p in range(3):
                    from_lane = GROUP_WIDTH * (3 * f + p)
                    grads[
                        FRAME_TOK * f : FRAME_TOK * (f + 1),
                        own_width * p + at : own_width * p + at + GROUP_WIDTH,
                    ] = piece[:FRAME_TOK, from_lane : from_lane + GROUP_WIDTH]
            for f in range(2):
                for p in range(2):
                    from_lane = GROUP_WIDTH * (2 * f + p)
                    texts[lower * f : lower * (f + 1), wide * p + at : wide * p + at + GROUP_WIDTH] = piece[
                        FRAME_TOK:, from_lane : from_lane + GROUP_WIDTH
                    ].astype(F32)

    @pl.when(here)
    def _():
        for_group(info_ref[1], groups, lambda v: fill(v, lambda s: own_refs[s][0, 0]))

    @pl.when(jnp.logical_not(here))
    def _():
        for_group(info_ref[1], groups, lambda v: fill(v, lambda s: other_ref[s, 0]))

    part = mxu(grads[...], w_ref[...], ((1,), (1,)))

    @pl.when(k == 0)
    def _():
        first_ref[...] = part

    @pl.when(k > 0)
    def _():
        rest_ref[0] = part.astype(BF16)

    ones = ones_ref[...]
    for t in range(wide // 128):
        lanes = slice(128 * t, 128 * (t + 1))
        x = raw_ref[0, :, lanes]
        dy = texts[:, lanes]
        inv = lax.rsqrt(head_means(x * x, ones) + EPSILON)
        unit = x * inv
        dgain_ref[0:1, :] += jnp.sum(dy * unit, axis=0, keepdims=True)
        dn = dy * gain_ref[2:3, :]
        text_ref[0, :, lanes] = (inv * (dn - unit * head_means(dn * unit, ones))).astype(BF16)
    text_ref[0, :, wide:] = texts[:, wide:].astype(BF16)


def in_back(info, own, other, w_cols, text_raw, gains, tokens):
    streams, chunk_text, text_lanes = text_raw.shape
    groups = len(own)
    half = streams // 2
    frames = tokens // FRAME_TOK
    width = w_cols.shape[0]
    own_width = w_cols.shape[1] // 3
    rows, lanes = own[0].shape[2:]
    return call(
        functools.partial(
            in_back_kernel,
            half=half,
            groups=groups,
            frames=frames,
            own_width=own_width,
            chunk_text=chunk_text,
        ),
        "in_back",
        (streams,),
        1,
        [pl.BlockSpec((1, 1, rows, lanes), lambda k, _: (0, k % half, 0, 0))] * groups
        + [
            pl.BlockSpec((groups, 1, rows, lanes), lambda k, _: (0, k % half, 0, 0)),
            whole_spec(w_cols.shape),
            pl.BlockSpec((1, chunk_text, text_lanes), lambda k, _: (k, 0, 0)),
            whole_spec((8, 128)),
            whole_spec((256, 128)),
        ],
        [
            whole_spec((tokens, width)),
            pl.BlockSpec((1, tokens, width), lambda k, _: (jnp.maximum(k - 1, 0), 0, 0)),
            pl.BlockSpec((1, chunk_text, text_lanes), lambda k, _: (k, 0, 0)),
            whole_spec((8, 128)),
        ],
        [
            jax.ShapeDtypeStruct((tokens, width), F32),
            jax.ShapeDtypeStruct((streams - 1, tokens, width), BF16),
            jax.ShapeDtypeStruct(text_raw.shape, BF16),
            jax.ShapeDtypeStruct((8, 128), F32),
        ],
        [
            pltpu.VMEM((tokens, 3 * own_width), BF16),
            pltpu.VMEM((chunk_text, text_lanes), F32),
        ],
        48 * MIB,
        2 * streams * tokens * w_cols.size,
        streams * tokens * width * 6 + w_cols.size * 2,
        (info, *own, other, w_cols, text_raw, gains, head_ones()),
    )


def weights_kernel(*refs, tiles, streams):
    cut = [refs[streams * n : streams * (n + 1)] for n in range(5)]
    x_refs, g_refs, gate_refs, up_refs, hidden_refs = cut
    out_ref, x_flip, g_flip = refs[5 * streams :]
    i = pl.program_id(0)
    rows = x_refs[0].shape[0]

    @pl.when(i == 0)
    def _():
        for k in range(streams):
            x_flip[:, rows * k : rows * (k + 1)] = jnp.transpose(x_refs[k][...])
            g_flip[:, rows * k : rows * (k + 1)] = jnp.transpose(g_refs[k][...])

    def total(flip, refs):
        right = joined([ref[...] for ref in refs], 0)
        out_ref[...] = mxu(flip[...], right).astype(BF16)

    @pl.when(i < tiles)
    def _():
        total(x_flip, gate_refs)

    @pl.when(jnp.logical_and(i >= tiles, i < 2 * tiles))
    def _():
        total(x_flip, up_refs)

    @pl.when(i >= 2 * tiles)
    def _():
        total(g_flip, hidden_refs)


def ffn_weights(x, g, gate, up, hidden):
    streams = len(x)
    rows, width = x[0].shape
    inner = hidden[0].shape[1]
    tile = min(512, inner)
    tiles = inner // tile
    at = lambda first: pl.BlockSpec(
        (rows, tile), lambda i: (0, jnp.clip(i - first * tiles, 0, tiles - 1))
    )
    return call(
        functools.partial(weights_kernel, tiles=tiles, streams=streams),
        "ffn_weights",
        (3 * tiles,),
        0,
        [whole_spec((rows, width))] * (2 * streams)
        + [at(0)] * streams
        + [at(1)] * streams
        + [at(2)] * streams,
        pl.BlockSpec((width, tile), lambda i: (0, i)),
        jax.ShapeDtypeStruct((width, 3 * inner), BF16),
        [pltpu.VMEM((width, streams * rows), BF16)] * 2,
        56 * MIB,
        6 * streams * rows * width * inner,
        6 * width * inner + 10 * streams * rows * width,
        (*x, *g, *gate, *up, *hidden),
    )


def unit_rms(values):
    inv = lax.rsqrt(jnp.mean(values * values, axis=-1, keepdims=True) + EPSILON)
    return values * inv, inv


def unit_back(grad_unit, unit, inv):
    return inv * (grad_unit - unit * jnp.mean(grad_unit * unit, axis=-1, keepdims=True))


def rope_lanes(frames):
    half = HD // 2
    frame_pairs = HD // 8
    row_pairs = (half - frame_pairs) // 2
    col_pairs = half - frame_pairs - row_pairs
    pair = (np.arange(128) % HD) // 2

    def lanes(first, count):
        freq = 10000.0 ** (-(np.arange(count, dtype=np.float32)) / np.float32(count))
        out = np.zeros((128,), np.float32)
        inside = (pair >= first) & (pair < first + count)
        out[inside] = freq.astype(np.float32)[pair[inside] - first]
        return jnp.asarray(out)[None, :]

    rows = frames.shape[0]
    inner = jnp.arange(rows) % FRAME_TOK
    row_pos = (inner // PW).astype(F32)
    col_pos = (inner % PW).astype(F32)
    angle = (
        frames[:, None] * lanes(0, frame_pairs)
        + row_pos[:, None] * lanes(frame_pairs, row_pairs)
        + col_pos[:, None] * lanes(frame_pairs + row_pairs, col_pairs)
    )
    sign = jnp.asarray(np.where(np.arange(128) % 2 == 0, -1.0, 1.0).astype(np.float32))[None, :]
    return jnp.cos(angle), jnp.sin(angle) * sign


def gain_rows(*gains):
    rows = [jnp.concatenate([g, g]) for g in gains]
    rows += [jnp.zeros((128,), F32)] * (8 - len(rows))
    return jnp.stack(rows)


def pad_parts(values, parts):
    width = values.shape[-1] // parts
    wide = lane_tiles(width)
    if wide == width:
        return values
    cut = values.reshape(values.shape[:-1] + (parts, width))
    cut = jnp.pad(cut, [(0, 0)] * (cut.ndim - 1) + [(0, wide - width)])
    return cut.reshape(values.shape[:-1] + (parts * wide,))


def pick(values, index, axis=0):
    return lax.dynamic_index_in_dim(values, index, axis, keepdims=False)


def beside(value, *others):
    return lax.optimization_barrier((value,) + others)


def held(value, *others):
    return lax.optimization_barrier((value,) + others)[0]


def per_device(
    fsdp,
    dps,
    states,
    cotangent,
    segment_ids,
    frame_ids,
    condition,
    context,
    w_modulate,
    w_qkv,
    w_text_kv,
    w_out,
    w_gate_up,
    w_down,
    gain_attn_in,
    gain_attn_out,
    gain_ffn_in,
    gain_ffn_out,
    gain_query,
    gain_key,
    gain_text_key,
    cross_gate,
):
    xs = Moves("fsdp", fsdp)
    ds = Moves("dp", dps)
    rows_in = states[0]
    tokens, width = rows_in.shape
    frames = tokens // FRAME_TOK
    heads = cross_gate.shape[0]
    own_heads = heads // fsdp
    own_width = own_heads * HD
    groups = own_heads // GROUP_HEADS
    ranks = dps // groups
    rank_bits = ranks.bit_length() - 1
    clips = condition.shape[1]
    text_local = context[0]
    text_own = text_local.shape[0]
    half = fsdp // 2
    group_me = ds.me // ranks
    rank_me = ds.me % ranks
    core = ds.me % 2

    def frame_view(values):
        return values.reshape(frames, FRAME_TOK, values.shape[-1])

    def group_swap(pieces):
        return [pieces[0]] + [ds.swap(pieces[s], s * ranks) for s in range(1, groups)]

    def group_exchange(keep, send, *first):
        other = ds.swap(send, 1)
        pieces = [
            jnp.stack([pick(keep, group_me ^ s, 1), pick(other, group_me ^ s, 1)])
            for s in range(groups)
        ]
        return group_swap([held(piece, *first) for piece in pieces])

    def group_return(pieces):
        own = group_swap(pieces)
        return own, ds.swap(jnp.stack([piece[1] for piece in own]), 1)

    own_frames = segment_ids[0][::FRAME_TOK].astype(F32)
    own_frame_ids = frame_ids[0].reshape(frames, FRAME_TOK)[:, 0].astype(F32)
    met = jnp.stack(xs.gather(jnp.concatenate([own_frames, own_frame_ids])))
    core_info = core.astype(jnp.int32)[None]
    group_info = group_me.astype(jnp.int32)[None]
    both_info = jnp.concatenate([core_info, group_info])

    silu_cond = jax.nn.silu(condition[0]).astype(BF16)
    cond_rel = jnp.concatenate(xs.gather(silu_cond))
    rows = w_qkv.shape[0]
    quarter = rows // 4

    def columns_of(weight, first, count, s):
        return jnp.concatenate(
            [
                lax.dynamic_slice(
                    weight, (first, p * width + (xs.me ^ s) * own_width), (count, own_width)
                )
                for p in range(3)
            ],
            axis=1,
        )

    fetched = []
    for s in range(1, fsdp):
        wanted = columns_of(w_qkv, (ds.me % 4) * quarter, quarter, s)
        wanted, cond_rel = beside(wanted, cond_rel)
        quarters = [(0, xs.swap(wanted, s))]
        for mask in (2, 1):
            quarters += [(m ^ mask, ds.swap(v, mask)) for m, v in quarters]
        fetched += [(s, m, v) for m, v in quarters]
    cond_own = xs.own_block(cond_rel, 1)
    mod_part = mxu(cond_own, w_modulate).reshape(fsdp, clips, -1)
    modulation = mod_part[0]
    for s in range(1, fsdp):
        modulation = modulation + xs.swap(mod_part[s], s)

    own_seg = lax.dynamic_slice_in_dim(own_frames, ds.me * frames, frames)
    onehot = (own_seg[:, None] == jnp.arange(clips, dtype=F32)[None, :]).astype(F32)
    per_frame = jnp.dot(onehot, modulation, precision=HIGHEST)[:, None, :]
    scale_attn, gate_attn, scale_ffn, gate_ffn = jnp.split(per_frame, 4, axis=2)

    states_f = frame_view(rows_in)
    unit_in, inv_in = unit_rms(states_f)
    normed = (unit_in * gain_attn_in * (1.0 + scale_attn)).astype(BF16).reshape(tokens, width)
    normed, met, w_there = beside(normed, met, w_qkv)
    normed_all = jnp.stack(xs.gather(normed))
    w_cols = lax.dynamic_update_slice_in_dim(
        jnp.zeros((width, 3 * own_width), BF16), columns_of(w_there, 0, rows, 0), xs.me * rows, 0
    )
    for s, m, v in fetched:
        at = (xs.me ^ s) * rows + ((ds.me % 4) ^ m) * quarter
        w_cols = lax.dynamic_update_slice_in_dim(w_cols, v, at, 0)

    stream_seg = met[:, : own_frames.shape[0]].astype(jnp.int32)
    rel_frame_ids = met[:, own_frames.shape[0] :]
    core_seg = lax.dynamic_slice_in_dim(stream_seg, core * half, half, 0)
    masks = [s * ranks for s in range(groups)]
    for b in reversed(range(1, rank_bits)):
        masks = masks + [m ^ (1 << b) for m in masks]
    place_dev = jnp.stack([ds.me ^ (m ^ c) for m in masks for c in range(2)])
    q_dev = jnp.stack([ds.me ^ (s * ranks ^ c) for s in range(groups) for c in range(2)])
    in_frames = lambda dev: (dev[:, None] * frames + jnp.arange(frames)[None, :]).reshape(-1)
    kv_seg = jnp.take(core_seg, in_frames(place_dev), axis=1)
    q_seg = jnp.take(core_seg, in_frames(q_dev), axis=1)
    order = jnp.arange(kv_seg.shape[1])
    less = kv_seg[:, None, :] < kv_seg[:, :, None]
    tie = (kv_seg[:, None, :] == kv_seg[:, :, None]) & (order[None, None, :] < order[None, :, None])
    kv_rank = jnp.sum((less | tie).astype(jnp.int32), axis=2)
    q_start = jnp.sum((kv_seg[:, None, :] < q_seg[:, :, None]).astype(jnp.int32), axis=2)
    q_count = jnp.sum((kv_seg[:, None, :] == q_seg[:, :, None]).astype(jnp.int32), axis=2)
    tables = (kv_rank, q_start, q_count, jnp.maximum(q_seg, 0), place_dev.astype(jnp.int32))
    cosine, sine = rope_lanes(jnp.repeat(rel_frame_ids, FRAME_TOK, axis=1).reshape(-1))
    cosine = cosine.reshape(fsdp, tokens, 128)
    sine = sine.reshape(fsdp, tokens, 128)

    text_rel = jnp.concatenate(
        [xs.own_block(text_local, 1)]
        + [xs.swap(xs.own_block(text_local, 1, s), s) for s in range(1, fsdp)]
    )
    text_part = mxu(text_rel, w_text_kv).reshape(fsdp, text_own, 2, fsdp, own_width)
    text_raw = pick(text_part, xs.me, 3)
    for s in range(1, fsdp):
        piece = pick(text_part, xs.me ^ s, 3)
        piece = jnp.stack([piece[s ^ k] for k in range(fsdp)])
        text_raw = text_raw + xs.swap(piece.astype(BF16), s).astype(F32)
    text_raw = pad_parts(text_raw.reshape(fsdp, text_own, 2 * own_width), 2)

    gains = gain_rows(gain_query, gain_key, gain_text_key)
    send_q, send_kv, keep_q, keep_kv = make_heads(
        core_info, normed_all, w_cols, text_raw, cosine, sine, gains, groups
    )

    kv = group_exchange(keep_kv, send_kv)
    kv_first = kv[1:]
    for b in reversed(range(1, rank_bits)):
        kv = kv + [ds.swap(v, 1 << b) for v in kv]
    query = group_exchange(keep_q, send_q, *kv_first)
    tanh_gate = jnp.tanh(cross_gate)
    first_head = xs.me * own_heads + group_me * GROUP_HEADS
    gate_row = jnp.repeat(lax.dynamic_slice_in_dim(tanh_gate, first_head, GROUP_HEADS), HD)[None, :]

    mixed, kept = attn_fwd(tables, kv, query, gate_row)
    mixed_own, mixed_other = group_return(mixed)
    mixed_low, mix_first, mix_rest = out_project(
        both_info, mixed_own, mixed_other, w_out, fsdp, tokens
    )

    def swapped_sum(first, rest):
        for s in range(1, fsdp):
            first = first + xs.swap(rest[s - 1], s).astype(F32)
        return first

    late_ids = held(rel_frame_ids, mix_first)
    set_of = lambda values, which: lax.dynamic_slice_in_dim(values, which * half, half, 0)
    near_ids = jnp.stack(
        [set_of(late_ids, core), ds.swap(set_of(late_ids, 1 - core), 1)], axis=1
    )
    far_ids = jnp.stack([near_ids] + [ds.swap(near_ids, s * ranks) for s in range(1, groups)])
    normed_two = jnp.stack(
        [set_of(normed_all, core), ds.swap(set_of(normed_all, 1 - core), 1)]
    )
    late_normed = held(normed_two, *mixed_own)
    text_every = lax.all_gather(held(text_rel, *mixed_own), "dp", axis=0, tiled=True)
    if groups > 1:
        members = [[g * ranks + r for g in range(groups)] for r in range(ranks)]
        normed_group = lax.all_gather(late_normed, "dp", axis_index_groups=members)
    else:
        normed_group = late_normed[None]
    far_cos, far_sin = rope_lanes(jnp.repeat(far_ids.reshape(-1), FRAME_TOK))
    far_shape = (groups, half, 2 * tokens, 128)
    far_cos = far_cos.reshape(far_shape)
    far_sin = far_sin.reshape(far_shape)
    mix_got = [xs.swap(mix_rest[s - 1], s) for s in range(1, fsdp)]
    mix_got = [held(v, far_cos, far_sin) for v in mix_got]
    for v in mix_got:
        mix_first = mix_first + v.astype(F32)
    mixed_out = frame_view(mix_first)
    unit_mix, inv_mix = unit_rms(mixed_out)
    tanh_attn = jnp.tanh(gate_attn)
    after = states_f + tanh_attn * unit_mix * gain_attn_out
    unit_ffn, inv_ffn = unit_rms(after)
    ffn_low = (unit_ffn * gain_ffn_in * (1.0 + scale_ffn)).astype(BF16).reshape(tokens, width)
    ffn_all = xs.gather(ffn_low)
    gate_part = [mxu(x, w_gate_up[0]) for x in ffn_all]
    up_part = [mxu(x, w_gate_up[1]) for x in ffn_all]
    hidden = [(jax.nn.silu(g) * u).astype(BF16) for g, u in zip(gate_part, up_part)]
    ffn_out = swapped_sum(
        mxu(hidden[0], w_down), [mxu(h, w_down).astype(BF16) for h in hidden[1:]]
    )
    ffn_out = frame_view(ffn_out)
    unit_out, inv_out = unit_rms(ffn_out)
    tanh_ffn = jnp.tanh(gate_ffn)
    output = after + tanh_ffn * unit_out * gain_ffn_out

    def frame_sum(values):
        return jnp.sum(values, axis=1)

    cot = frame_view(cotangent[0])
    cot_unit = frame_sum(cot * unit_out)
    grad_gate_ffn = cot_unit * gain_ffn_out * (1.0 - tanh_ffn[:, 0] ** 2)
    grad_gain_ffn_out = jnp.sum(cot_unit * tanh_ffn[:, 0], axis=0)
    grad_ffn_low = (
        unit_back(cot * (tanh_ffn * gain_ffn_out), unit_out, inv_out)
        .astype(BF16)
        .reshape(tokens, width)
    )
    grad_ffn_all = xs.gather(grad_ffn_low)
    grad_gate = []
    grad_up = []
    for g, u, d in zip(gate_part, up_part, grad_ffn_all):
        grad_hidden = mxu(d, w_down, ((1,), (1,)))
        sig = jax.nn.sigmoid(g)
        grad_gate.append((grad_hidden * u * (sig * (1.0 + g * (1.0 - sig)))).astype(BF16))
        grad_up.append((grad_hidden * (g * sig)).astype(BF16))

    def ffn_in_part(s):
        return mxu(grad_gate[s], w_gate_up[0], ((1,), (1,))) + mxu(
            grad_up[s], w_gate_up[1], ((1,), (1,))
        )

    def reduce_rows(term):
        return lax.psum_scatter(term, "dp", scatter_dimension=0, tiled=True).astype(F32)

    ffn_rest = [xs.swap(ffn_in_part(s).astype(BF16), s) for s in range(1, fsdp)]
    ffn_grads = ffn_weights(ffn_all, grad_ffn_all, grad_gate, grad_up, hidden)
    ffn_grads, grad_ffn_in, *ffn_rest = beside(ffn_grads, ffn_in_part(0), *ffn_rest)
    for v in ffn_rest:
        grad_ffn_in = grad_ffn_in + v.astype(F32)
    grad_ffn_in = frame_view(grad_ffn_in)
    inner = w_down.shape[0]
    ffn_sums = reduce_rows(ffn_grads)
    grad_unit = frame_sum(grad_ffn_in * unit_ffn)
    grad_scale_ffn = grad_unit * gain_ffn_in
    grad_gain_ffn_in = jnp.sum(grad_unit * (1.0 + scale_ffn[:, 0]), axis=0)
    grad_after = cot + unit_back(
        grad_ffn_in * (gain_ffn_in * (1.0 + scale_ffn)), unit_ffn, inv_ffn
    )
    after_unit = frame_sum(grad_after * unit_mix)
    grad_gate_attn = after_unit * gain_attn_out * (1.0 - tanh_attn[:, 0] ** 2)
    grad_gain_attn_out = jnp.sum(after_unit * tanh_attn[:, 0], axis=0)
    grad_mix_low = (
        unit_back(grad_after * (tanh_attn * gain_attn_out), unit_mix, inv_mix)
        .astype(BF16)
        .reshape(tokens, width)
    )
    grad_mix_all = held(jnp.stack(xs.gather(grad_mix_low)), normed_group, text_every)

    send_grad, keep_grad = out_back(core_info, grad_mix_all, w_out, groups)
    grad_group = group_exchange(keep_grad, send_grad)
    out_grad = mxu(
        grad_mix_all.reshape(fsdp * tokens, width),
        mixed_low.reshape(fsdp * tokens, own_width),
        ((0,), (0,)),
    ).astype(BF16)
    out_grad, *grad_group = beside(out_grad, *grad_group)
    dquery, dkv, dgate = attn_bwd(tables, kv, query, grad_group, kept, gate_row)
    for b in range(1, rank_bits):
        count = len(dkv) // 2
        dkv = [
            (dkv[i].astype(F32) + ds.swap(dkv[count + i], 1 << b).astype(F32)).astype(BF16)
            for i in range(count)
        ]

    w_tri = jnp.concatenate(
        [
            lax.dynamic_slice_in_dim(
                w_cols, p * own_width + group_me * GROUP_WIDTH, GROUP_WIDTH, 1
            )
            for p in range(2)
        ],
        axis=1,
    )
    tri_gain = jnp.concatenate([jnp.tile(gain_query, GROUP_HEADS), jnp.tile(gain_key, GROUP_HEADS)])
    tri_gain = jnp.pad(tri_gain[None, :], ((0, 7), (0, 0)))
    proj_pieces, qkv_grad, gain_qk = proj_back(
        group_info,
        normed_group,
        w_tri,
        dquery,
        dkv,
        far_cos,
        far_sin,
        tri_gain,
    )
    per = width // (fsdp * ranks)
    part = qkv_grad.reshape(fsdp, ranks, per, 3 * GROUP_WIDTH)
    parts = []
    for b in range(rank_bits):
        part = part.reshape(fsdp, part.shape[1] // 2, 2, per, 3 * GROUP_WIDTH)
        mine = (rank_me >> b) & 1
        got = ds.swap(pick(part, 1 - mine, 2), 1 << b)
        part = (pick(part, mine, 2).astype(F32) + got.astype(F32)).astype(BF16)
        parts.append(part)
    proj_own = [held(piece, parts[0]) for piece in group_swap(proj_pieces)]
    proj_other = ds.swap(jnp.stack([piece[1] for piece in proj_own]), 1)
    part = part[:, 0]
    part_own = pick(part, xs.me)
    part_sent = [pick(part, xs.me ^ s) for s in range(1, fsdp)]
    proj_other = held(proj_other, part_own, ffn_sums, *part_sent)
    in_first, in_rest, grad_text, gain_text = in_back(
        both_info, proj_own, proj_other, w_cols, text_raw, gains, tokens
    )
    part_got = [held(xs.swap(v, s + 1), in_first) for s, v in enumerate(part_sent)]
    part = jnp.stack([part_own] + part_got)
    part = jnp.stack([pick(part, xs.me ^ k) for k in range(fsdp)])
    blocks = jnp.transpose(part.reshape(fsdp, per, 3, GROUP_WIDTH), (2, 0, 1, 3))
    blocks = blocks.reshape(3 * fsdp, per, GROUP_WIDTH)
    in_got = [xs.swap(in_rest[s - 1], s) for s in range(1, fsdp)]
    if groups > 1:
        window = 3 * heads // GROUP_HEADS // groups
        slots = -(-window // groups)
        first_of = lambda target, source: (window * target - source + groups - 1) // groups
        sent = []
        for s in range(groups):
            first = first_of(group_me ^ s, group_me)
            sent.append(
                jnp.stack(
                    [pick(blocks, jnp.clip(first + t, 0, 3 * fsdp - 1)) for t in range(slots)]
                )
            )
        in_got = [held(v, *sent) for v in in_got]
    for v in in_got:
        in_first = in_first + v.astype(F32)
    grad_normed = frame_view(in_first)
    in_unit = frame_sum(grad_normed * unit_in)
    grad_scale_attn = in_unit * gain_attn_in
    grad_gain_attn_in = jnp.sum(in_unit * (1.0 + scale_attn[:, 0]), axis=0)
    grad_input = grad_after + unit_back(
        grad_normed * (gain_attn_in * (1.0 + scale_attn)), unit_in, inv_in
    )
    if groups > 1:
        got = held(jnp.stack(group_swap(sent)), grad_gain_attn_in, grad_scale_attn)
        got = got.reshape(groups * slots, per, GROUP_WIDTH)
        ordered = []
        for k in range(window):
            block = window * group_me + k
            source = block % groups
            slot = block // groups - first_of(group_me, source)
            ordered.append(pick(got, (source ^ group_me) * slots + slot))
        blocks = jnp.stack(ordered)
    columns = jnp.swapaxes(blocks, 0, 1).reshape(per, ranks, 3 * width // dps)
    columns = jnp.swapaxes(columns, 0, 1)
    if ranks <= 4:
        got = jnp.stack(
            [pick(columns, rank_me)]
            + [ds.swap(pick(columns, rank_me ^ m), m) for m in range(1, ranks)]
        )
        got = jnp.stack([pick(got, rank_me ^ r) for r in range(ranks)])
    else:
        got = lax.all_to_all(columns, "dp", 0, 0, tiled=True)
    grad_w_qkv = got.reshape(rows, 3 * width // dps).astype(F32)

    grad_w_gate_up = jnp.stack([ffn_sums[:, :inner], ffn_sums[:, inner : 2 * inner]])
    grad_w_down = jnp.transpose(ffn_sums[:, 2 * inner :])

    out_grad, ffn_sums = beside(out_grad, ffn_sums)
    grad_w_out = jnp.transpose(reduce_rows(out_grad))
    def gather_columns(values, parts):
        wide = values.shape[2] // parts
        cut = values.reshape(fsdp, values.shape[1], parts, wide)[..., :own_width]
        got = [cut]
        for s in range(1, fsdp):
            other = xs.swap(cut, s)
            got.append(jnp.stack([other[s ^ k] for k in range(fsdp)]))
        got = jnp.stack(got)
        whole = jnp.stack([pick(got, xs.me ^ k) for k in range(fsdp)], axis=3)
        return whole.reshape(fsdp * values.shape[1], parts * fsdp * own_width)

    grad_text_all = gather_columns(grad_text, 2)
    text_cols = grad_text_all.shape[1] // dps
    grad_text_cols = jnp.swapaxes(grad_text_all.reshape(fsdp * text_own, dps, text_cols), 0, 1)
    grad_text_cols = lax.all_to_all(grad_text_cols, "dp", 0, 0, tiled=True)
    grad_w_text_kv = mxu(text_every, grad_text_cols.reshape(-1, text_cols), ((0,), (0,)))

    frame_grads = jnp.concatenate(
        [grad_scale_attn, grad_gate_attn, grad_scale_ffn, grad_gate_ffn], axis=1
    )
    clip_grads = jnp.dot(jnp.transpose(onehot), frame_grads, precision=HIGHEST)
    mod_cols = clip_grads.shape[1] // dps
    clip_grads = jnp.swapaxes(clip_grads.reshape(clips, dps, mod_cols), 0, 1)
    clip_grads = jnp.sum(lax.all_to_all(clip_grads, "dp", 0, 0, tiled=True), axis=0)
    clip_rel = jnp.concatenate(xs.gather(clip_grads))
    grad_w_modulate = jnp.dot(jnp.transpose(cond_own.astype(F32)), clip_rel, precision=HIGHEST)
    head_term = jnp.sum(dgate.reshape(GROUP_HEADS, HD), axis=1)
    gate_term = lax.dynamic_update_slice_in_dim(jnp.zeros((heads,), F32), head_term, first_head, 0)
    gate_term = gate_term * (1.0 - tanh_gate * tanh_gate)
    qk_sums = jnp.sum(gain_qk[0].reshape(2, GROUP_HEADS, HD), axis=1)
    small = [
        grad_gain_attn_in,
        grad_gain_attn_out,
        grad_gain_ffn_in,
        grad_gain_ffn_out,
        qk_sums[0],
        qk_sums[1],
        gain_text[0, :HD] + gain_text[0, HD:],
        gate_term,
    ]
    sizes = [v.shape[0] for v in small]
    packed = jnp.concatenate(small)
    packed = jnp.pad(packed, (0, -packed.shape[0] % 1024)).reshape(-1, 128)
    for moves in (ds, xs):
        for b in range(moves.size.bit_length() - 1):
            packed = packed + moves.swap(packed, 1 << b)
    packed = packed.reshape(-1)
    sums = []
    at = 0
    for size in sizes:
        sums.append(packed[at : at + size])
        at += size
    return (
        output.reshape(1, tokens, width),
        grad_input.reshape(1, tokens, width),
        grad_w_modulate,
        grad_w_qkv,
        grad_w_text_kv,
        grad_w_out,
        grad_w_gate_up,
        grad_w_down,
        *sums,
    )


def solution(mesh):
    rows = P("fsdp", "dp", None)
    first = P("fsdp", None)
    split = P("fsdp", "dp")
    return jax.shard_map(
        functools.partial(per_device, mesh.shape["fsdp"], mesh.shape["dp"]),
        mesh=mesh,
        in_specs=(
            rows,
            rows,
            first,
            split,
            P("fsdp", None, None),
            rows,
            first,
            first,
            first,
            first,
            P(None, None, "fsdp"),
            first,
        )
        + (P(),) * 8,
        out_specs=(
            rows,
            rows,
            split,
            split,
            split,
            split,
            P(None, "dp", "fsdp"),
            split,
        )
        + (P(),) * 8,
        check_vma=False,
    )
```

```python
import functools
import math

import jax
import jax.numpy as jnp
import numpy as np
from jax import lax
from jax.experimental import pallas as pl
from jax.experimental.pallas import tpu as pltpu
from jax.sharding import PartitionSpec as P

HD = 64
CTX = 256
FRAME_TOK = 128
PW = 16
EPSILON = 1e-06
GROUP_HEADS = 3
GROUP_WIDTH = GROUP_HEADS * HD
STACK = GROUP_HEADS * FRAME_TOK
ONES_ROWS = 16
HIGHEST = lax.Precision.HIGHEST
BF16 = jnp.bfloat16
F32 = jnp.float32
SCALE = HD ** (-0.5)
EXP2_SCALE = SCALE * math.log2(math.e)
MIB = 1 << 20
COST_CUT = 100


def mxu(a, b, dims=((1,), (0,))):
    return lax.dot_general(a, b, (dims, ((), ())), preferred_element_type=F32)


class Moves:
    def __init__(self, axis, size):
        self.axis = axis
        self.size = size
        self.me = lax.axis_index(axis)

    def swap(self, value, mask):
        return lax.ppermute(value, self.axis, [(i, i ^ mask) for i in range(self.size)])

    def gather(self, value):
        return [value] + [self.swap(value, s) for s in range(1, self.size)]

    def scatter_sum(self, parts):
        total = parts[0].astype(F32)
        for s in range(1, self.size):
            total = total + self.swap(parts[s].astype(BF16), s).astype(F32)
        return total

    def reorder(self, value, axis):
        block = value.shape[axis] // self.size
        return jnp.concatenate(
            [
                lax.dynamic_slice_in_dim(value, (self.me ^ s) * block, block, axis)
                for s in range(self.size)
            ],
            axis,
        )

    def own_block(self, value, axis, s=0):
        block = value.shape[axis] // self.size
        return lax.dynamic_slice_in_dim(value, (self.me ^ s) * block, block, axis)


def lane_tiles(width):
    return -(-width // 128) * 128


def turn(values, cosine, sine):
    lane = lax.broadcasted_iota(jnp.int32, values.shape, 1)
    other = jnp.where(lane % 2 == 0, pltpu.roll(values, 127, 1), pltpu.roll(values, 1, 1))
    return values * cosine + other * sine


def head_means(values, ones):
    upper = values.astype(BF16)
    lower = (values - upper.astype(F32)).astype(BF16)
    return mxu(jnp.concatenate([upper, lower], axis=1), ones) * (1.0 / HD)


def joined(pieces, axis):
    return jnp.concatenate(pieces, axis=axis) if len(pieces) > 1 else pieces[0]


def widened(values):
    missing = lane_tiles(values.shape[1]) - values.shape[1]
    if not missing:
        return values
    return jnp.concatenate([values, jnp.zeros((values.shape[0], missing), values.dtype)], axis=1)


def tiles_of(values):
    return [values[:, 128 * t : 128 * (t + 1)] for t in range(values.shape[1] // 128)]


def normed_heads(raw, ones, gain):
    return [x * lax.rsqrt(head_means(x * x, ones) + EPSILON) * gain for x in tiles_of(raw)]


def head_ones():
    lane = np.arange(128) // HD
    ones = (lane[:, None] == lane[None, :]).astype(np.float32)
    return jnp.asarray(np.concatenate([ones, ones]), BF16)


def group_cut(values, g):
    return values[:, GROUP_WIDTH * g : GROUP_WIDTH * (g + 1)]


def packed_frames(values, frames):
    return joined([values[FRAME_TOK * f : FRAME_TOK * (f + 1)] for f in range(frames)], 1)


def call(kernel, name, grid, prefetch, in_specs, out_specs, out_shape, scratch, vmem, flops, moved, args):
    return pl.pallas_call(
        kernel,
        grid_spec=pltpu.PrefetchScalarGridSpec(
            num_scalar_prefetch=prefetch,
            grid=grid,
            in_specs=in_specs,
            out_specs=out_specs,
            scratch_shapes=scratch,
        ),
        out_shape=out_shape,
        compiler_params=pltpu.CompilerParams(
            dimension_semantics=("arbitrary",) * len(grid), vmem_limit_bytes=vmem
        ),
        cost_estimate=pl.CostEstimate(
            flops=int(flops) // COST_CUT, bytes_accessed=int(moved) // COST_CUT, transcendentals=0
        ),
        name=name,
    )(*args)


def whole_spec(shape):
    zeros = (0,) * len(shape)
    return pl.BlockSpec(shape, lambda *_: zeros)


def heads_kernel(
    core_ref,
    x_ref,
    w_ref,
    text_ref,
    cos_ref,
    sin_ref,
    gain_ref,
    ones_ref,
    send_q,
    send_kv,
    keep_q,
    keep_kv,
    *,
    half,
    groups,
    frames,
    own_width,
):
    step = pl.program_id(0)
    tokens = frames * FRAME_TOK
    ones = ones_ref[...]
    parts = []
    for p in range(3):
        raw = widened(mxu(x_ref[0], w_ref[:, own_width * p : own_width * (p + 1)]))
        if p < 2:
            raw = joined(
                [
                    turn(x, cos_ref[0], sin_ref[0])
                    for x in normed_heads(raw, ones, gain_ref[p : p + 1, :])
                ],
                1,
            )
        parts.append(raw.astype(BF16))
    wide = text_ref.shape[2] // 2
    text_key = joined(normed_heads(text_ref[0, :, :wide], ones, gain_ref[2:3, :]), 1).astype(BF16)
    text_value = text_ref[0, :, wide:].astype(BF16)

    def put(q_ref, kv_ref):
        for g in range(groups):
            q_ref[0, g] = packed_frames(group_cut(parts[0], g), frames)
            kv_ref[0, g, :tokens] = joined([group_cut(parts[1], g), group_cut(parts[2], g)], 1)
            kv_ref[0, g, tokens:] = joined([group_cut(text_key, g), group_cut(text_value, g)], 1)

    @pl.when(step < half)
    def _():
        put(send_q, send_kv)

    @pl.when(step >= half)
    def _():
        put(keep_q, keep_kv)


def set_stream(step, core, half):
    other = jnp.where(step < half, 1 - core, core)
    return other * half + step % half


def make_heads(core, x, w_cols, text_raw, cosine, sine, gains, groups):
    streams, tokens, width = x.shape
    half = streams // 2
    frames = tokens // FRAME_TOK
    own_width = w_cols.shape[1] // 3
    text_own = text_raw.shape[1]
    by_stream = lambda i, core: (set_stream(i, core[0], half), 0, 0)
    q_block = (1, groups, FRAME_TOK, frames * GROUP_WIDTH)
    kv_block = (1, groups, tokens + text_own, 2 * GROUP_WIDTH)
    first = lambda i, core: (jnp.minimum(i, half - 1), 0, 0, 0)
    second = lambda i, core: (jnp.maximum(i - half, 0), 0, 0, 0)
    return call(
        functools.partial(
            heads_kernel, half=half, groups=groups, frames=frames, own_width=own_width
        ),
        "make_heads",
        (streams,),
        1,
        [
            pl.BlockSpec((1, tokens, width), by_stream),
            whole_spec(w_cols.shape),
            pl.BlockSpec((1,) + text_raw.shape[1:], by_stream),
            pl.BlockSpec((1, tokens, 128), by_stream),
            pl.BlockSpec((1, tokens, 128), by_stream),
            whole_spec((8, 128)),
            whole_spec((256, 128)),
        ],
        [
            pl.BlockSpec(q_block, first),
            pl.BlockSpec(kv_block, first),
            pl.BlockSpec(q_block, second),
            pl.BlockSpec(kv_block, second),
        ],
        [
            jax.ShapeDtypeStruct((half,) + q_block[1:], BF16),
            jax.ShapeDtypeStruct((half,) + kv_block[1:], BF16),
        ]
        * 2,
        [],
        48 * MIB,
        2 * x.size * w_cols.shape[1],
        x.size * 2 + w_cols.size * 2 + x.size * 3,
        (core, x, w_cols, text_raw, cosine, sine, gains, head_ones()),
    )


BIG = 4
CLIP = 16


def over_tiles(start, count, body):
    whole = count // CLIP
    rest = count - whole * CLIP
    big = rest // BIG
    at = lambda frame: pl.multiple_of(frame * FRAME_TOK, FRAME_TOK)

    def whole_step(t, carry):
        body(at(start + t * CLIP), BIG * FRAME_TOK, CLIP // BIG)
        return carry

    def big_step(t, carry):
        body(at(start + whole * CLIP + t * BIG), BIG * FRAME_TOK, 1)
        return carry

    def small_step(t, carry):
        body(at(start + whole * CLIP + big * BIG + t), FRAME_TOK, 1)
        return carry

    lax.fori_loop(0, whole, whole_step, 0)
    lax.fori_loop(0, big, big_step, 0)
    lax.fori_loop(0, rest - big * BIG, small_step, 0)


def stacked(values, mask):
    return jnp.concatenate([values] * GROUP_HEADS, axis=0) * mask


def diagonal(values):
    own = [
        values[HD * h : HD * (h + 1), FRAME_TOK * h : FRAME_TOK * (h + 1)]
        for h in range(GROUP_HEADS)
    ]
    return jnp.transpose(jnp.concatenate(own, axis=0))


def head_row(values):
    flipped = jnp.transpose(values)
    return jnp.concatenate(
        [
            jnp.sum(flipped[HD * h : HD * (h + 1), :], axis=0, keepdims=True)
            for h in range(GROUP_HEADS)
        ],
        axis=1,
    )


def each_chunk(kv_refs, rank_ref, place_ref, s, frames, chunk_text, self_rows, frame_body, text_body):
    tokens = frames * FRAME_TOK
    for i, ref in enumerate(kv_refs):

        def one(c, carry, i=i, ref=ref):
            chunk = 2 * i + c
            for f in range(frames):
                at = pl.multiple_of(rank_ref[s, chunk * frames + f] * FRAME_TOK, FRAME_TOK)
                frame_body(ref, c, slice(f * FRAME_TOK, (f + 1) * FRAME_TOK), at)
            at = pl.multiple_of(self_rows + place_ref[chunk] * chunk_text, chunk_text)
            text_body(ref, c, slice(tokens, tokens + chunk_text), at)
            return carry

        lax.fori_loop(0, 2, one, 0)


def unpack_frames(refs, scratch, frames):
    for i, ref in enumerate(refs):
        for c in range(2):
            for f in range(frames):
                scratch[(2 * i + c) * frames + f] = ref[
                    c, :, GROUP_WIDTH * f : GROUP_WIDTH * (f + 1)
                ]


def attn_fwd_kernel(*refs, pieces, groups, frames, chunk_text):
    rank_ref, start_ref, count_ref, clip_ref, place_ref = refs[:5]
    refs = refs[5:]
    kv_refs, refs = refs[:pieces], refs[pieces:]
    q_refs, refs = refs[:groups], refs[groups:]
    gate_ref, mask_ref = refs[:2]
    mixed_refs, refs = refs[2 : 2 + groups], refs[2 + groups :]
    self_ref, text_ref, lse_ref, keys, values, rows_text, queries, mixes, acc = refs
    s = pl.program_id(0)
    j = pl.program_id(1)
    self_rows = pieces * 2 * frames * FRAME_TOK
    text_rows = rows_text.shape[0]
    K = slice(0, GROUP_WIDTH)
    V = slice(GROUP_WIDTH, 2 * GROUP_WIDTH)

    @pl.when(j == 0)
    def _():
        values[GROUP_WIDTH:, :] = jnp.ones((ONES_ROWS, values.shape[1]), BF16)

        def frame_body(ref, c, rows, at):
            keys[pl.ds(at, FRAME_TOK), :] = ref[c, rows, K]
            values[:GROUP_WIDTH, pl.ds(at, FRAME_TOK)] = jnp.transpose(ref[c, rows, V])

        def text_body(ref, c, rows, at):
            keys[pl.ds(at, chunk_text), :] = ref[c, rows, K]
            rows_text[pl.ds(at - self_rows, chunk_text), :] = ref[c, rows, V]

        each_chunk(
            kv_refs, rank_ref, place_ref, s, frames, chunk_text, self_rows, frame_body, text_body
        )
        for b in range(text_rows // 128):
            values[:GROUP_WIDTH, self_rows + 128 * b : self_rows + 128 * (b + 1)] = jnp.transpose(
                rows_text[128 * b : 128 * (b + 1), :]
            )
        unpack_frames(q_refs, queries, frames)

    query = stacked(queries[j], mask_ref[...])

    def tile(base, size, times):
        total = None
        for t in range(times):
            rows = pl.ds(pl.multiple_of(base + t * size, FRAME_TOK), size)
            scores = mxu(keys[rows, :], query, ((1,), (1,)))
            weights = jnp.exp2(scores * EXP2_SCALE).astype(BF16)
            part = mxu(values[:, rows], weights)
            total = part if total is None else total + part
        acc[...] += total

    def finish(row):
        total = acc[GROUP_WIDTH : GROUP_WIDTH + 1, :]
        lse_ref[0, 0, row : row + 1, :] = jnp.log(total) * math.log2(math.e)
        return diagonal(acc[:GROUP_WIDTH, :] * (1.0 / total))

    acc[...] = jnp.zeros_like(acc)
    over_tiles(start_ref[s, j], count_ref[s, j], tile)
    self_out = finish(0)
    acc[...] = jnp.zeros_like(acc)
    tile(pl.multiple_of(self_rows + clip_ref[s, j] * CTX, 128), CTX, 1)
    text_out = finish(1)
    self_ref[0, 0] = self_out
    text_ref[0, 0] = text_out
    mixes[j] = (self_out + gate_ref[...] * text_out).astype(BF16)

    @pl.when(j == pl.num_programs(1) - 1)
    def _():
        for g, ref in enumerate(mixed_refs):
            for c in range(2):
                at = (2 * g + c) * frames
                ref[c] = joined([mixes[at + f] for f in range(frames)], 1)


def attn_bwd_kernel(*refs, pieces, groups, frames, chunk_text):
    rank_ref, start_ref, count_ref, clip_ref, place_ref = refs[:5]
    refs = refs[5:]
    kv_refs, refs = refs[:pieces], refs[pieces:]
    q_refs, refs = refs[:groups], refs[groups:]
    grad_refs, refs = refs[:groups], refs[groups:]
    self_ref, text_ref, lse_ref, gate_ref, mask_ref, dq_ref = refs[:6]
    dkv_refs, refs = refs[6 : 6 + pieces], refs[6 + pieces :]
    dgate_ref, keys, keys_flip, values, dkeys, dvalues, dquery, queries, grads = refs
    s = pl.program_id(0)
    j = pl.program_id(1)
    self_rows = pieces * 2 * frames * FRAME_TOK
    text_rows = pieces * 2 * chunk_text
    K = slice(0, GROUP_WIDTH)
    V = slice(GROUP_WIDTH, 2 * GROUP_WIDTH)

    @pl.when(jnp.logical_and(s == 0, j == 0))
    def _():
        dgate_ref[...] = jnp.zeros_like(dgate_ref)

    @pl.when(j == 0)
    def _():
        dkeys[...] = jnp.zeros_like(dkeys)
        dvalues[...] = jnp.zeros_like(dvalues)

        def frame_body(ref, c, rows, at):
            keys[pl.ds(at, FRAME_TOK), :] = ref[c, rows, K]
            keys_flip[:, pl.ds(at, FRAME_TOK)] = jnp.transpose(ref[c, rows, K])
            values[pl.ds(at, FRAME_TOK), :] = ref[c, rows, V]

        def text_body(ref, c, rows, at):
            keys[pl.ds(at, chunk_text), :] = ref[c, rows, K]
            values[pl.ds(at, chunk_text), :] = ref[c, rows, V]

        each_chunk(
            kv_refs, rank_ref, place_ref, s, frames, chunk_text, self_rows, frame_body, text_body
        )
        for b in range(text_rows // 128):
            rows = slice(self_rows + 128 * b, self_rows + 128 * (b + 1))
            keys_flip[:, rows] = jnp.transpose(keys[rows, :])
        unpack_frames(q_refs, queries, frames)
        unpack_frames(grad_refs, grads, frames)

    mask = mask_ref[...]
    query = stacked(queries[j], mask)
    grad_low = grads[j]
    grad_wide = grad_low.astype(F32)
    grad_text = (grad_wide * gate_ref[...]).astype(BF16)
    text_out = text_ref[0, 0]
    dgate_ref[...] += jnp.sum(grad_wide * text_out, axis=0, keepdims=True)
    dquery[...] = jnp.zeros_like(dquery)

    def over(grad, out, lse):
        grad_stack = stacked(grad, mask)
        delta = head_row(grad.astype(F32) * out)

        def tile(base, size, times):
            total = None
            for t in range(times):
                rows = pl.ds(pl.multiple_of(base + t * size, FRAME_TOK), size)
                scores = mxu(keys[rows, :], query, ((1,), (1,)))
                weights = jnp.exp2(scores * EXP2_SCALE - lse)
                dweights = mxu(values[rows, :], grad_stack, ((1,), (1,)))
                dscores = (weights * (dweights - delta)).astype(BF16)
                dvalues[rows, :] += mxu(weights.astype(BF16), grad_stack)
                dkeys[rows, :] += mxu(dscores, query)
                part = mxu(keys_flip[:, rows], dscores)
                total = part if total is None else total + part
            dquery[...] += total

        return tile

    over_tiles(start_ref[s, j], count_ref[s, j], over(grad_low, self_ref[0, 0], lse_ref[0, 0, 0:1, :]))
    over(grad_text, text_out, lse_ref[0, 0, 1:2, :])(
        pl.multiple_of(self_rows + clip_ref[s, j] * CTX, 128), CTX, 1
    )
    dq_ref[0, 0] = (diagonal(dquery[...]) * SCALE).astype(BF16)

    @pl.when(j == pl.num_programs(1) - 1)
    def _():
        def frame_body(ref, c, rows, at):
            taken = pl.ds(at, FRAME_TOK)
            ref[c, rows, :] = jnp.concatenate(
                [dkeys[taken, :] * SCALE, dvalues[taken, :]], axis=1
            ).astype(BF16)

        def text_body(ref, c, rows, at):
            taken = pl.ds(at, chunk_text)
            ref[c, rows, :] = jnp.concatenate(
                [dkeys[taken, :] * SCALE, dvalues[taken, :]], axis=1
            ).astype(BF16)

        each_chunk(
            dkv_refs, rank_ref, place_ref, s, frames, chunk_text, self_rows, frame_body, text_body
        )


def attention_specs(kv, query):
    _, streams, chunk_rows, _ = kv[0].shape
    frames = query[0].shape[3] // GROUP_WIDTH
    chunk_text = chunk_rows - frames * FRAME_TOK
    sizes = dict(pieces=len(kv), groups=len(query), frames=frames, chunk_text=chunk_text)
    count = len(query) * 2 * frames
    grid = (streams, count)
    piece = lambda shape: pl.BlockSpec(
        (2, None) + shape, lambda s, j, *_: (0, s, 0, 0), pipeline_mode=pl.Buffered(1)
    )
    kv_spec = piece((chunk_rows, 2 * GROUP_WIDTH))
    q_spec = piece((FRAME_TOK, frames * GROUP_WIDTH))
    tok_spec = pl.BlockSpec((1, 1, FRAME_TOK, GROUP_WIDTH), lambda s, j, *_: (s, j, 0, 0))
    lse_spec = pl.BlockSpec((1, 1, 2, STACK), lambda s, j, *_: (s, j, 0, 0))
    const_specs = [whole_spec((1, GROUP_WIDTH)), whole_spec((STACK, GROUP_WIDTH))]
    return sizes, grid, kv_spec, q_spec, tok_spec, lse_spec, const_specs


def stack_mask():
    head_of_row = np.arange(STACK) // FRAME_TOK
    head_of_lane = np.arange(GROUP_WIDTH) // HD
    return jnp.asarray((head_of_row[:, None] == head_of_lane[None, :]).astype(np.float32), BF16)


def attn_fwd(tables, kv, query, gate):
    sizes, grid, kv_spec, q_spec, tok_spec, lse_spec, const_specs = attention_specs(kv, query)
    total = len(kv) * 2 * kv[0].shape[2]
    text_rows = len(kv) * 2 * sizes["chunk_text"]
    wide = jax.ShapeDtypeStruct(grid + (FRAME_TOK, GROUP_WIDTH), F32)
    got = call(
        functools.partial(attn_fwd_kernel, **sizes),
        "attention",
        grid,
        5,
        [kv_spec] * len(kv) + [q_spec] * len(query) + const_specs,
        [q_spec] * len(query) + [tok_spec, tok_spec, lse_spec],
        [jax.ShapeDtypeStruct(q.shape, BF16) for q in query]
        + [wide, wide, jax.ShapeDtypeStruct(grid + (2, STACK), F32)],
        [
            pltpu.VMEM((total, GROUP_WIDTH), BF16),
            pltpu.VMEM((GROUP_WIDTH + ONES_ROWS, total), BF16),
            pltpu.VMEM((text_rows, GROUP_WIDTH), BF16),
            pltpu.VMEM((grid[1], FRAME_TOK, GROUP_WIDTH), BF16),
            pltpu.VMEM((grid[1], FRAME_TOK, GROUP_WIDTH), BF16),
            pltpu.VMEM((GROUP_WIDTH + ONES_ROWS, STACK), F32),
        ],
        min(60 * MIB, total * 2600 + 16 * MIB),
        grid[0] * grid[1] * STACK * 2304 * GROUP_WIDTH * 8,
        grid[0] * grid[1] * 300000,
        (*tables, *kv, *query, gate, stack_mask()),
    )
    return got[: len(query)], got[len(query) :]


def attn_bwd(tables, kv, query, grad, kept, gate):
    sizes, grid, kv_spec, q_spec, tok_spec, lse_spec, const_specs = attention_specs(kv, query)
    total = len(kv) * 2 * kv[0].shape[2]
    got = call(
        functools.partial(attn_bwd_kernel, **sizes),
        "attention_back",
        grid,
        5,
        [kv_spec] * len(kv)
        + [q_spec] * (2 * len(query))
        + [tok_spec, tok_spec, lse_spec]
        + const_specs,
        [tok_spec] + [kv_spec] * len(kv) + [whole_spec((1, GROUP_WIDTH))],
        [jax.ShapeDtypeStruct(grid + (FRAME_TOK, GROUP_WIDTH), BF16)]
        + [jax.ShapeDtypeStruct(v.shape, BF16) for v in kv]
        + [jax.ShapeDtypeStruct((1, GROUP_WIDTH), F32)],
        [
            pltpu.VMEM((total, GROUP_WIDTH), BF16),
            pltpu.VMEM((GROUP_WIDTH, total), BF16),
            pltpu.VMEM((total, GROUP_WIDTH), BF16),
            pltpu.VMEM((total, GROUP_WIDTH), F32),
            pltpu.VMEM((total, GROUP_WIDTH), F32),
            pltpu.VMEM((GROUP_WIDTH, STACK), F32),
            pltpu.VMEM((grid[1], FRAME_TOK, GROUP_WIDTH), BF16),
            pltpu.VMEM((grid[1], FRAME_TOK, GROUP_WIDTH), BF16),
        ],
        60 * MIB,
        grid[0] * grid[1] * STACK * 2304 * GROUP_WIDTH * 20,
        grid[0] * grid[1] * 500000,
        (*tables, *kv, *query, *grad, *kept, gate, stack_mask()),
    )
    return got[0], got[1 : 1 + len(kv)], got[-1]


def for_group(group, groups, body):
    for v in range(groups):

        @pl.when(group == v)
        def _(v=v):
            body(v)


def out_kernel(info_ref, *refs, half, groups, frames):
    own_refs, refs = refs[:groups], refs[groups:]
    other_ref, w_ref, mixed_ref, first_ref, rest_ref = refs
    k = pl.program_id(0)
    here = (k // half) == info_ref[0]

    def fill(v, take):
        for s in range(groups):
            piece = take(s)
            for f in range(frames):
                mixed_ref[0, FRAME_TOK * f : FRAME_TOK * (f + 1), GROUP_WIDTH * (v ^ s) : GROUP_WIDTH * ((v ^ s) + 1)] = piece[
                    :, GROUP_WIDTH * f : GROUP_WIDTH * (f + 1)
                ]

    @pl.when(here)
    def _():
        for_group(info_ref[1], groups, lambda v: fill(v, lambda s: own_refs[s][0, 0]))

    @pl.when(jnp.logical_not(here))
    def _():
        for_group(info_ref[1], groups, lambda v: fill(v, lambda s: other_ref[s, 0]))

    part = mxu(mixed_ref[0], w_ref[...])

    @pl.when(k == 0)
    def _():
        first_ref[...] = part

    @pl.when(k > 0)
    def _():
        rest_ref[0] = part.astype(BF16)


def out_project(info, own, other, w_out, streams, tokens):
    groups = len(own)
    half = streams // 2
    frames = tokens // FRAME_TOK
    own_width, width = w_out.shape
    lanes = frames * GROUP_WIDTH
    return call(
        functools.partial(out_kernel, half=half, groups=groups, frames=frames),
        "out_project",
        (streams,),
        1,
        [pl.BlockSpec((1, 1, FRAME_TOK, lanes), lambda k, _: (0, k % half, 0, 0))] * groups
        + [
            pl.BlockSpec((groups, 1, FRAME_TOK, lanes), lambda k, _: (0, k % half, 0, 0)),
            whole_spec(w_out.shape),
        ],
        [
            pl.BlockSpec((1, tokens, own_width), lambda k, _: (k, 0, 0)),
            whole_spec((tokens, width)),
            pl.BlockSpec((1, tokens, width), lambda k, _: (jnp.maximum(k - 1, 0), 0, 0)),
        ],
        [
            jax.ShapeDtypeStruct((streams, tokens, own_width), BF16),
            jax.ShapeDtypeStruct((tokens, width), F32),
            jax.ShapeDtypeStruct((streams - 1, tokens, width), BF16),
        ],
        [],
        32 * MIB,
        2 * streams * tokens * own_width * width,
        streams * tokens * width * 6 + w_out.size * 2,
        (info, *own, other, w_out),
    )


def out_back_kernel(core_ref, grad_ref, w_ref, send_ref, keep_ref, *, half, groups, frames):
    step = pl.program_id(0)
    grad = mxu(grad_ref[0], w_ref[...], ((1,), (1,))).astype(BF16)

    def put(ref):
        for g in range(groups):
            ref[0, g] = packed_frames(group_cut(grad, g), frames)

    @pl.when(step < half)
    def _():
        put(send_ref)

    @pl.when(step >= half)
    def _():
        put(keep_ref)


def out_back(core, grad, w_out, groups):
    streams, tokens, width = grad.shape
    half = streams // 2
    frames = tokens // FRAME_TOK
    block = (1, groups, FRAME_TOK, frames * GROUP_WIDTH)
    return call(
        functools.partial(out_back_kernel, half=half, groups=groups, frames=frames),
        "out_back",
        (streams,),
        1,
        [
            pl.BlockSpec((1, tokens, width), lambda i, core: (set_stream(i, core[0], half), 0, 0)),
            whole_spec(w_out.shape),
        ],
        [
            pl.BlockSpec(block, lambda i, core: (jnp.minimum(i, half - 1), 0, 0, 0)),
            pl.BlockSpec(block, lambda i, core: (jnp.maximum(i - half, 0), 0, 0, 0)),
        ],
        [jax.ShapeDtypeStruct((half,) + block[1:], BF16)] * 2,
        [],
        32 * MIB,
        2 * streams * tokens * w_out.size,
        streams * tokens * width * 3 + w_out.size * 2,
        (core, grad, w_out),
    )


def proj_back_kernel(*refs, groups, frames, half, chunk_text):
    group_ref, x_ref, w_ref, dq_ref = refs[:4]
    dkv_refs, refs = refs[4 : 4 + groups], refs[4 + groups :]
    cos_ref, sin_ref, gain_ref, ones_ref = refs[:4]
    out_refs, refs = refs[4 : 4 + groups], refs[4 + groups :]
    dw_ref, dgain_ref, dkv, total = refs
    i = pl.program_id(0)
    tokens = frames * FRAME_TOK

    @pl.when(i == 0)
    def _():
        total[...] = jnp.zeros_like(total)
        dgain_ref[...] = jnp.zeros_like(dgain_ref)

    for g, ref in enumerate(dkv_refs):

        @pl.when(i // half == g)
        def _(ref=ref):
            dkv[...] = ref[...]

    ones = ones_ref[...]
    x = jnp.concatenate([x_ref[0, c, 0] for c in range(2)], axis=0)
    raw = mxu(x, w_ref[...])
    key_grad = jnp.concatenate([dkv[c, :tokens, :GROUP_WIDTH] for c in range(2)], axis=0)
    value_grad = jnp.concatenate([dkv[c, :tokens, GROUP_WIDTH:] for c in range(2)], axis=0)
    query_grad = jnp.concatenate([dq_ref[0, n] for n in range(2 * frames)], axis=0)
    turned = jnp.concatenate([query_grad, key_grad], axis=1).astype(F32)
    done = []
    for t, (x_t, dy) in enumerate(zip(tiles_of(raw), tiles_of(turned))):
        dy = turn(dy, cos_ref[0, 0], -sin_ref[0, 0])
        inv = lax.rsqrt(head_means(x_t * x_t, ones) + EPSILON)
        unit = x_t * inv
        lanes = slice(128 * t, 128 * (t + 1))
        dgain_ref[0:1, lanes] += jnp.sum(dy * unit, axis=0, keepdims=True)
        dn = dy * gain_ref[0:1, lanes]
        done.append((inv * (dn - unit * head_means(dn * unit, ones))).astype(BF16))
    grads = jnp.concatenate(done + [value_grad], axis=1)
    total[...] += mxu(grads, x, ((0,), (0,)))

    def put(ref):
        for c in range(2):
            ref[c, :FRAME_TOK, :] = packed_frames(grads[tokens * c : tokens * (c + 1)], frames)
            rows = slice(tokens, tokens + chunk_text)
            text = dkv[c, rows, :]
            lower = chunk_text // 2
            ref[c, FRAME_TOK:, : 4 * GROUP_WIDTH] = jnp.concatenate(
                [text[:lower], text[lower:]], axis=1
            )
            ref[c, FRAME_TOK:, 4 * GROUP_WIDTH :] = jnp.zeros(
                (lower, ref.shape[2] - 4 * GROUP_WIDTH), BF16
            )

    for g, ref in enumerate(out_refs):

        @pl.when(i // half == g)
        def _(ref=ref):
            put(ref)

    @pl.when(i == pl.num_programs(0) - 1)
    def _():
        for b in range(total.shape[1] // 256):
            lanes = slice(256 * b, 256 * (b + 1))
            dw_ref[lanes, :] = jnp.transpose(total[:, lanes]).astype(BF16)


def proj_back(group, x, w_tri, dq, dkv, cosine, sine, gains):
    groups = len(dkv)
    half = x.shape[2]
    tokens, width = x.shape[3:]
    frames = tokens // FRAME_TOK
    chunk_text = dkv[0].shape[2] - tokens
    lanes = frames * 3 * GROUP_WIDTH
    rows = FRAME_TOK + chunk_text // 2
    got = call(
        functools.partial(
            proj_back_kernel, groups=groups, frames=frames, half=half, chunk_text=chunk_text
        ),
        "proj_back",
        (groups * half,),
        1,
        [
            pl.BlockSpec(
                (1, 2, 1, tokens, width), lambda i, g: (g[0] ^ (i // half), 0, i % half, 0, 0)
            ),
            whole_spec(w_tri.shape),
            pl.BlockSpec(
                (1, 2 * frames, FRAME_TOK, GROUP_WIDTH), lambda i, g: (i % half, i // half, 0, 0)
            ),
        ]
        + [
            pl.BlockSpec((2, None) + dkv[0].shape[2:], lambda i, g: (0, i % half, 0, 0))
        ]
        * groups
        + [
            pl.BlockSpec((1, 1, 2 * tokens, 128), lambda i, g: (i // half, i % half, 0, 0)),
            pl.BlockSpec((1, 1, 2 * tokens, 128), lambda i, g: (i // half, i % half, 0, 0)),
            whole_spec(gains.shape),
            whole_spec((256, 128)),
        ],
        [
            pl.BlockSpec(
                (2, None, rows, lanes),
                lambda i, g, n=n: (0, jnp.clip(i - n * half, 0, half - 1), 0, 0),
            )
            for n in range(groups)
        ]
        + [whole_spec((width, 3 * GROUP_WIDTH)), whole_spec((8, 2 * GROUP_WIDTH))],
        [jax.ShapeDtypeStruct((2, half, rows, lanes), BF16)] * groups
        + [
            jax.ShapeDtypeStruct((width, 3 * GROUP_WIDTH), BF16),
            jax.ShapeDtypeStruct((8, 2 * GROUP_WIDTH), F32),
        ],
        [
            pltpu.VMEM(dkv[0].shape[:1] + dkv[0].shape[2:], BF16),
            pltpu.VMEM((3 * GROUP_WIDTH, width), F32),
        ],
        48 * MIB,
        2 * x.size * GROUP_WIDTH * 5,
        x.size * 4 + w_tri.size * 2,
        (group, x, w_tri, dq, *dkv, cosine, sine, gains, head_ones()),
    )
    return got[:groups], got[groups], got[groups + 1]


def in_back_kernel(info_ref, *refs, half, groups, frames, own_width, chunk_text):
    own_refs, refs = refs[:groups], refs[groups:]
    other_ref, w_ref, raw_ref, gain_ref, ones_ref = refs[:5]
    first_ref, rest_ref, text_ref, dgain_ref, grads, texts = refs[5:]
    k = pl.program_id(0)
    here = (k // half) == info_ref[0]
    wide = lane_tiles(own_width)
    lower = chunk_text // 2

    @pl.when(k == 0)
    def _():
        dgain_ref[...] = jnp.zeros_like(dgain_ref)
        texts[...] = jnp.zeros_like(texts)

    def fill(v, take):
        for s in range(groups):
            piece = take(s)
            at = GROUP_WIDTH * (v ^ s)
            for f in range(frames):
                for p in range(3):
                    from_lane = GROUP_WIDTH * (3 * f + p)
                    grads[
                        FRAME_TOK * f : FRAME_TOK * (f + 1),
                        own_width * p + at : own_width * p + at + GROUP_WIDTH,
                    ] = piece[:FRAME_TOK, from_lane : from_lane + GROUP_WIDTH]
            for f in range(2):
                for p in range(2):
                    from_lane = GROUP_WIDTH * (2 * f + p)
                    texts[lower * f : lower * (f + 1), wide * p + at : wide * p + at + GROUP_WIDTH] = piece[
                        FRAME_TOK:, from_lane : from_lane + GROUP_WIDTH
                    ].astype(F32)

    @pl.when(here)
    def _():
        for_group(info_ref[1], groups, lambda v: fill(v, lambda s: own_refs[s][0, 0]))

    @pl.when(jnp.logical_not(here))
    def _():
        for_group(info_ref[1], groups, lambda v: fill(v, lambda s: other_ref[s, 0]))

    part = mxu(grads[...], w_ref[...], ((1,), (1,)))

    @pl.when(k == 0)
    def _():
        first_ref[...] = part

    @pl.when(k > 0)
    def _():
        rest_ref[0] = part.astype(BF16)

    ones = ones_ref[...]
    for t in range(wide // 128):
        lanes = slice(128 * t, 128 * (t + 1))
        x = raw_ref[0, :, lanes]
        dy = texts[:, lanes]
        inv = lax.rsqrt(head_means(x * x, ones) + EPSILON)
        unit = x * inv
        dgain_ref[0:1, :] += jnp.sum(dy * unit, axis=0, keepdims=True)
        dn = dy * gain_ref[2:3, :]
        text_ref[0, :, lanes] = (inv * (dn - unit * head_means(dn * unit, ones))).astype(BF16)
    text_ref[0, :, wide:] = texts[:, wide:].astype(BF16)


def in_back(info, own, other, w_cols, text_raw, gains, tokens):
    streams, chunk_text, text_lanes = text_raw.shape
    groups = len(own)
    half = streams // 2
    frames = tokens // FRAME_TOK
    width = w_cols.shape[0]
    own_width = w_cols.shape[1] // 3
    rows, lanes = own[0].shape[2:]
    return call(
        functools.partial(
            in_back_kernel,
            half=half,
            groups=groups,
            frames=frames,
            own_width=own_width,
            chunk_text=chunk_text,
        ),
        "in_back",
        (streams,),
        1,
        [pl.BlockSpec((1, 1, rows, lanes), lambda k, _: (0, k % half, 0, 0))] * groups
        + [
            pl.BlockSpec((groups, 1, rows, lanes), lambda k, _: (0, k % half, 0, 0)),
            whole_spec(w_cols.shape),
            pl.BlockSpec((1, chunk_text, text_lanes), lambda k, _: (k, 0, 0)),
            whole_spec((8, 128)),
            whole_spec((256, 128)),
        ],
        [
            whole_spec((tokens, width)),
            pl.BlockSpec((1, tokens, width), lambda k, _: (jnp.maximum(k - 1, 0), 0, 0)),
            pl.BlockSpec((1, chunk_text, text_lanes), lambda k, _: (k, 0, 0)),
            whole_spec((8, 128)),
        ],
        [
            jax.ShapeDtypeStruct((tokens, width), F32),
            jax.ShapeDtypeStruct((streams - 1, tokens, width), BF16),
            jax.ShapeDtypeStruct(text_raw.shape, BF16),
            jax.ShapeDtypeStruct((8, 128), F32),
        ],
        [
            pltpu.VMEM((tokens, 3 * own_width), BF16),
            pltpu.VMEM((chunk_text, text_lanes), F32),
        ],
        48 * MIB,
        2 * streams * tokens * w_cols.size,
        streams * tokens * width * 6 + w_cols.size * 2,
        (info, *own, other, w_cols, text_raw, gains, head_ones()),
    )


def weights_kernel(*refs, tiles, streams):
    cut = [refs[streams * n : streams * (n + 1)] for n in range(5)]
    x_refs, g_refs, gate_refs, up_refs, hidden_refs = cut
    out_ref, x_flip, g_flip = refs[5 * streams :]
    i = pl.program_id(0)
    rows = x_refs[0].shape[0]

    @pl.when(i == 0)
    def _():
        for k in range(streams):
            x_flip[:, rows * k : rows * (k + 1)] = jnp.transpose(x_refs[k][...])
            g_flip[:, rows * k : rows * (k + 1)] = jnp.transpose(g_refs[k][...])

    def total(flip, refs):
        right = joined([ref[...] for ref in refs], 0)
        out_ref[...] = mxu(flip[...], right).astype(BF16)

    @pl.when(i < tiles)
    def _():
        total(x_flip, gate_refs)

    @pl.when(jnp.logical_and(i >= tiles, i < 2 * tiles))
    def _():
        total(x_flip, up_refs)

    @pl.when(i >= 2 * tiles)
    def _():
        total(g_flip, hidden_refs)


def ffn_weights(x, g, gate, up, hidden):
    streams = len(x)
    rows, width = x[0].shape
    inner = hidden[0].shape[1]
    tile = min(512, inner)
    tiles = inner // tile
    at = lambda first: pl.BlockSpec(
        (rows, tile), lambda i: (0, jnp.clip(i - first * tiles, 0, tiles - 1))
    )
    return call(
        functools.partial(weights_kernel, tiles=tiles, streams=streams),
        "ffn_weights",
        (3 * tiles,),
        0,
        [whole_spec((rows, width))] * (2 * streams)
        + [at(0)] * streams
        + [at(1)] * streams
        + [at(2)] * streams,
        pl.BlockSpec((width, tile), lambda i: (0, i)),
        jax.ShapeDtypeStruct((width, 3 * inner), BF16),
        [pltpu.VMEM((width, streams * rows), BF16)] * 2,
        56 * MIB,
        6 * streams * rows * width * inner,
        6 * width * inner + 10 * streams * rows * width,
        (*x, *g, *gate, *up, *hidden),
    )


def unit_rms(values):
    inv = lax.rsqrt(jnp.mean(values * values, axis=-1, keepdims=True) + EPSILON)
    return values * inv, inv


def unit_back(grad_unit, unit, inv):
    return inv * (grad_unit - unit * jnp.mean(grad_unit * unit, axis=-1, keepdims=True))


def rope_lanes(frames):
    half = HD // 2
    frame_pairs = HD // 8
    row_pairs = (half - frame_pairs) // 2
    col_pairs = half - frame_pairs - row_pairs
    pair = (np.arange(128) % HD) // 2

    def lanes(first, count):
        freq = 10000.0 ** (-(np.arange(count, dtype=np.float32)) / np.float32(count))
        out = np.zeros((128,), np.float32)
        inside = (pair >= first) & (pair < first + count)
        out[inside] = freq.astype(np.float32)[pair[inside] - first]
        return jnp.asarray(out)[None, :]

    rows = frames.shape[0]
    inner = jnp.arange(rows) % FRAME_TOK
    row_pos = (inner // PW).astype(F32)
    col_pos = (inner % PW).astype(F32)
    angle = (
        frames[:, None] * lanes(0, frame_pairs)
        + row_pos[:, None] * lanes(frame_pairs, row_pairs)
        + col_pos[:, None] * lanes(frame_pairs + row_pairs, col_pairs)
    )
    sign = jnp.asarray(np.where(np.arange(128) % 2 == 0, -1.0, 1.0).astype(np.float32))[None, :]
    return jnp.cos(angle), jnp.sin(angle) * sign


def gain_rows(*gains):
    rows = [jnp.concatenate([g, g]) for g in gains]
    rows += [jnp.zeros((128,), F32)] * (8 - len(rows))
    return jnp.stack(rows)


def pad_parts(values, parts):
    width = values.shape[-1] // parts
    wide = lane_tiles(width)
    if wide == width:
        return values
    cut = values.reshape(values.shape[:-1] + (parts, width))
    cut = jnp.pad(cut, [(0, 0)] * (cut.ndim - 1) + [(0, wide - width)])
    return cut.reshape(values.shape[:-1] + (parts * wide,))


def pick(values, index, axis=0):
    return lax.dynamic_index_in_dim(values, index, axis, keepdims=False)


def beside(value, *others):
    return lax.optimization_barrier((value,) + others)


def held(value, *others):
    return lax.optimization_barrier((value,) + others)[0]


def per_device(
    fsdp,
    dps,
    states,
    cotangent,
    segment_ids,
    frame_ids,
    condition,
    context,
    w_modulate,
    w_qkv,
    w_text_kv,
    w_out,
    w_gate_up,
    w_down,
    gain_attn_in,
    gain_attn_out,
    gain_ffn_in,
    gain_ffn_out,
    gain_query,
    gain_key,
    gain_text_key,
    cross_gate,
):
    xs = Moves("fsdp", fsdp)
    ds = Moves("dp", dps)
    rows_in = states[0]
    tokens, width = rows_in.shape
    frames = tokens // FRAME_TOK
    heads = cross_gate.shape[0]
    own_heads = heads // fsdp
    own_width = own_heads * HD
    groups = own_heads // GROUP_HEADS
    ranks = dps // groups
    rank_bits = ranks.bit_length() - 1
    clips = condition.shape[1]
    text_local = context[0]
    text_own = text_local.shape[0]
    half = fsdp // 2
    group_me = ds.me // ranks
    rank_me = ds.me % ranks
    core = ds.me % 2

    def frame_view(values):
        return values.reshape(frames, FRAME_TOK, values.shape[-1])

    def group_swap(pieces):
        return [pieces[0]] + [ds.swap(pieces[s], s * ranks) for s in range(1, groups)]

    def group_exchange(keep, send, *first):
        other = ds.swap(send, 1)
        pieces = [
            jnp.stack([pick(keep, group_me ^ s, 1), pick(other, group_me ^ s, 1)])
            for s in range(groups)
        ]
        return group_swap([held(piece, *first) for piece in pieces])

    def group_return(pieces):
        own = group_swap(pieces)
        return own, ds.swap(jnp.stack([piece[1] for piece in own]), 1)

    own_frames = segment_ids[0][::FRAME_TOK].astype(F32)
    own_frame_ids = frame_ids[0].reshape(frames, FRAME_TOK)[:, 0].astype(F32)
    met = jnp.stack(xs.gather(jnp.concatenate([own_frames, own_frame_ids])))
    core_info = core.astype(jnp.int32)[None]
    group_info = group_me.astype(jnp.int32)[None]
    both_info = jnp.concatenate([core_info, group_info])

    silu_cond = jax.nn.silu(condition[0]).astype(BF16)
    cond_rel = jnp.concatenate(xs.gather(silu_cond))
    rows = w_qkv.shape[0]
    quarter = rows // 4

    def columns_of(weight, first, count, s):
        return jnp.concatenate(
            [
                lax.dynamic_slice(
                    weight, (first, p * width + (xs.me ^ s) * own_width), (count, own_width)
                )
                for p in range(3)
            ],
            axis=1,
        )

    fetched = []
    for s in range(1, fsdp):
        wanted = columns_of(w_qkv, (ds.me % 4) * quarter, quarter, s)
        wanted, cond_rel = beside(wanted, cond_rel)
        quarters = [(0, xs.swap(wanted, s))]
        for mask in (2, 1):
            quarters += [(m ^ mask, ds.swap(v, mask)) for m, v in quarters]
        fetched += [(s, m, v) for m, v in quarters]
    cond_own = xs.own_block(cond_rel, 1)
    mod_part = mxu(cond_own, w_modulate).reshape(fsdp, clips, -1)
    modulation = mod_part[0]
    for s in range(1, fsdp):
        modulation = modulation + xs.swap(mod_part[s], s)

    own_seg = lax.dynamic_slice_in_dim(own_frames, ds.me * frames, frames)
    onehot = (own_seg[:, None] == jnp.arange(clips, dtype=F32)[None, :]).astype(F32)
    per_frame = jnp.dot(onehot, modulation, precision=HIGHEST)[:, None, :]
    scale_attn, gate_attn, scale_ffn, gate_ffn = jnp.split(per_frame, 4, axis=2)

    states_f = frame_view(rows_in)
    unit_in, inv_in = unit_rms(states_f)
    normed = (unit_in * gain_attn_in * (1.0 + scale_attn)).astype(BF16).reshape(tokens, width)
    normed, met, w_there = beside(normed, met, w_qkv)
    normed_all = jnp.stack(xs.gather(normed))
    w_cols = lax.dynamic_update_slice_in_dim(
        jnp.zeros((width, 3 * own_width), BF16), columns_of(w_there, 0, rows, 0), xs.me * rows, 0
    )
    for s, m, v in fetched:
        at = (xs.me ^ s) * rows + ((ds.me % 4) ^ m) * quarter
        w_cols = lax.dynamic_update_slice_in_dim(w_cols, v, at, 0)

    stream_seg = met[:, : own_frames.shape[0]].astype(jnp.int32)
    rel_frame_ids = met[:, own_frames.shape[0] :]
    core_seg = lax.dynamic_slice_in_dim(stream_seg, core * half, half, 0)
    masks = [s * ranks for s in range(groups)]
    for b in reversed(range(1, rank_bits)):
        masks = masks + [m ^ (1 << b) for m in masks]
    place_dev = jnp.stack([ds.me ^ (m ^ c) for m in masks for c in range(2)])
    q_dev = jnp.stack([ds.me ^ (s * ranks ^ c) for s in range(groups) for c in range(2)])
    in_frames = lambda dev: (dev[:, None] * frames + jnp.arange(frames)[None, :]).reshape(-1)
    kv_seg = jnp.take(core_seg, in_frames(place_dev), axis=1)
    q_seg = jnp.take(core_seg, in_frames(q_dev), axis=1)
    order = jnp.arange(kv_seg.shape[1])
    less = kv_seg[:, None, :] < kv_seg[:, :, None]
    tie = (kv_seg[:, None, :] == kv_seg[:, :, None]) & (order[None, None, :] < order[None, :, None])
    kv_rank = jnp.sum((less | tie).astype(jnp.int32), axis=2)
    q_start = jnp.sum((kv_seg[:, None, :] < q_seg[:, :, None]).astype(jnp.int32), axis=2)
    q_count = jnp.sum((kv_seg[:, None, :] == q_seg[:, :, None]).astype(jnp.int32), axis=2)
    tables = (kv_rank, q_start, q_count, jnp.maximum(q_seg, 0), place_dev.astype(jnp.int32))
    cosine, sine = rope_lanes(jnp.repeat(rel_frame_ids, FRAME_TOK, axis=1).reshape(-1))
    cosine = cosine.reshape(fsdp, tokens, 128)
    sine = sine.reshape(fsdp, tokens, 128)

    text_rel = jnp.concatenate(
        [xs.own_block(text_local, 1)]
        + [xs.swap(xs.own_block(text_local, 1, s), s) for s in range(1, fsdp)]
    )
    text_part = mxu(text_rel, w_text_kv).reshape(fsdp, text_own, 2, fsdp, own_width)
    text_raw = pick(text_part, xs.me, 3)
    for s in range(1, fsdp):
        piece = pick(text_part, xs.me ^ s, 3)
        piece = jnp.stack([piece[s ^ k] for k in range(fsdp)])
        text_raw = text_raw + xs.swap(piece.astype(BF16), s).astype(F32)
    text_raw = pad_parts(text_raw.reshape(fsdp, text_own, 2 * own_width), 2)

    gains = gain_rows(gain_query, gain_key, gain_text_key)
    send_q, send_kv, keep_q, keep_kv = make_heads(
        core_info, normed_all, w_cols, text_raw, cosine, sine, gains, groups
    )

    kv = group_exchange(keep_kv, send_kv)
    kv_first = kv[1:]
    for b in reversed(range(1, rank_bits)):
        kv = kv + [ds.swap(v, 1 << b) for v in kv]
    query = group_exchange(keep_q, send_q, *kv_first)
    tanh_gate = jnp.tanh(cross_gate)
    first_head = xs.me * own_heads + group_me * GROUP_HEADS
    gate_row = jnp.repeat(lax.dynamic_slice_in_dim(tanh_gate, first_head, GROUP_HEADS), HD)[None, :]

    mixed, kept = attn_fwd(tables, kv, query, gate_row)
    mixed_own, mixed_other = group_return(mixed)
    mixed_low, mix_first, mix_rest = out_project(
        both_info, mixed_own, mixed_other, w_out, fsdp, tokens
    )

    def swapped_sum(first, rest):
        for s in range(1, fsdp):
            first = first + xs.swap(rest[s - 1], s).astype(F32)
        return first

    late_ids = held(rel_frame_ids, mix_first)
    set_of = lambda values, which: lax.dynamic_slice_in_dim(values, which * half, half, 0)
    near_ids = jnp.stack(
        [set_of(late_ids, core), ds.swap(set_of(late_ids, 1 - core), 1)], axis=1
    )
    far_ids = jnp.stack([near_ids] + [ds.swap(near_ids, s * ranks) for s in range(1, groups)])
    normed_two = jnp.stack(
        [set_of(normed_all, core), ds.swap(set_of(normed_all, 1 - core), 1)]
    )
    late_normed = held(normed_two, *mixed_own)
    text_every = lax.all_gather(held(text_rel, *mixed_own), "dp", axis=0, tiled=True)
    if groups > 1:
        members = [[g * ranks + r for g in range(groups)] for r in range(ranks)]
        normed_group = lax.all_gather(late_normed, "dp", axis_index_groups=members)
    else:
        normed_group = late_normed[None]
    mix_got = [xs.swap(mix_rest[s - 1], s) for s in range(1, fsdp)]
    mix_got = [held(v, far_ids) for v in mix_got]
    for v in mix_got:
        mix_first = mix_first + v.astype(F32)
    mixed_out = frame_view(mix_first)
    unit_mix, inv_mix = unit_rms(mixed_out)
    tanh_attn = jnp.tanh(gate_attn)
    after = states_f + tanh_attn * unit_mix * gain_attn_out
    unit_ffn, inv_ffn = unit_rms(after)
    ffn_low = (unit_ffn * gain_ffn_in * (1.0 + scale_ffn)).astype(BF16).reshape(tokens, width)
    ffn_all = xs.gather(ffn_low)
    gate_part = [mxu(x, w_gate_up[0]) for x in ffn_all]
    up_part = [mxu(x, w_gate_up[1]) for x in ffn_all]
    hidden = [(jax.nn.silu(g) * u).astype(BF16) for g, u in zip(gate_part, up_part)]
    far_ids = held(far_ids, hidden[-1])
    far_cos, far_sin = rope_lanes(jnp.repeat(far_ids.reshape(-1), FRAME_TOK))
    far_shape = (groups, half, 2 * tokens, 128)
    far_cos = far_cos.reshape(far_shape)
    far_sin = far_sin.reshape(far_shape)
    ffn_got = [xs.swap(mxu(h, w_down).astype(BF16), s + 1) for s, h in enumerate(hidden[1:])]
    ffn_out = mxu(hidden[0], w_down)
    for v in ffn_got:
        ffn_out = ffn_out + held(v, far_cos, far_sin).astype(F32)
    ffn_out = frame_view(ffn_out)
    unit_out, inv_out = unit_rms(ffn_out)
    tanh_ffn = jnp.tanh(gate_ffn)
    output = after + tanh_ffn * unit_out * gain_ffn_out

    def frame_sum(values):
        return jnp.sum(values, axis=1)

    cot = frame_view(cotangent[0])
    cot_unit = frame_sum(cot * unit_out)
    grad_gate_ffn = cot_unit * gain_ffn_out * (1.0 - tanh_ffn[:, 0] ** 2)
    grad_gain_ffn_out = jnp.sum(cot_unit * tanh_ffn[:, 0], axis=0)
    grad_ffn_low = (
        unit_back(cot * (tanh_ffn * gain_ffn_out), unit_out, inv_out)
        .astype(BF16)
        .reshape(tokens, width)
    )
    grad_ffn_all = xs.gather(grad_ffn_low)
    grad_gate = []
    grad_up = []
    for g, u, d in zip(gate_part, up_part, grad_ffn_all):
        grad_hidden = mxu(d, w_down, ((1,), (1,)))
        sig = jax.nn.sigmoid(g)
        grad_gate.append((grad_hidden * u * (sig * (1.0 + g * (1.0 - sig)))).astype(BF16))
        grad_up.append((grad_hidden * (g * sig)).astype(BF16))

    def ffn_in_part(s):
        return mxu(grad_gate[s], w_gate_up[0], ((1,), (1,))) + mxu(
            grad_up[s], w_gate_up[1], ((1,), (1,))
        )

    def reduce_rows(term):
        return lax.psum_scatter(term, "dp", scatter_dimension=0, tiled=True).astype(F32)

    ffn_rest = [xs.swap(ffn_in_part(s).astype(BF16), s) for s in range(1, fsdp)]
    ffn_grads = ffn_weights(ffn_all, grad_ffn_all, grad_gate, grad_up, hidden)
    ffn_grads, grad_ffn_in, *ffn_rest = beside(ffn_grads, ffn_in_part(0), *ffn_rest)
    for v in ffn_rest:
        grad_ffn_in = grad_ffn_in + v.astype(F32)
    grad_ffn_in = frame_view(grad_ffn_in)
    inner = w_down.shape[0]
    ffn_sums = reduce_rows(ffn_grads)
    grad_unit = frame_sum(grad_ffn_in * unit_ffn)
    grad_scale_ffn = grad_unit * gain_ffn_in
    grad_gain_ffn_in = jnp.sum(grad_unit * (1.0 + scale_ffn[:, 0]), axis=0)
    grad_after = cot + unit_back(
        grad_ffn_in * (gain_ffn_in * (1.0 + scale_ffn)), unit_ffn, inv_ffn
    )
    after_unit = frame_sum(grad_after * unit_mix)
    grad_gate_attn = after_unit * gain_attn_out * (1.0 - tanh_attn[:, 0] ** 2)
    grad_gain_attn_out = jnp.sum(after_unit * tanh_attn[:, 0], axis=0)
    grad_mix_low = (
        unit_back(grad_after * (tanh_attn * gain_attn_out), unit_mix, inv_mix)
        .astype(BF16)
        .reshape(tokens, width)
    )
    grad_mix_all = held(jnp.stack(xs.gather(grad_mix_low)), normed_group, text_every)

    send_grad, keep_grad = out_back(core_info, grad_mix_all, w_out, groups)
    grad_group = group_exchange(keep_grad, send_grad)
    out_grad = mxu(
        grad_mix_all.reshape(fsdp * tokens, width),
        mixed_low.reshape(fsdp * tokens, own_width),
        ((0,), (0,)),
    ).astype(BF16)
    out_grad, *grad_group = beside(out_grad, *grad_group)
    dquery, dkv, dgate = attn_bwd(tables, kv, query, grad_group, kept, gate_row)
    for b in range(1, rank_bits):
        count = len(dkv) // 2
        dkv = [
            (dkv[i].astype(F32) + ds.swap(dkv[count + i], 1 << b).astype(F32)).astype(BF16)
            for i in range(count)
        ]

    w_tri = jnp.concatenate(
        [
            lax.dynamic_slice_in_dim(
                w_cols, p * own_width + group_me * GROUP_WIDTH, GROUP_WIDTH, 1
            )
            for p in range(2)
        ],
        axis=1,
    )
    tri_gain = jnp.concatenate([jnp.tile(gain_query, GROUP_HEADS), jnp.tile(gain_key, GROUP_HEADS)])
    tri_gain = jnp.pad(tri_gain[None, :], ((0, 7), (0, 0)))
    proj_pieces, qkv_grad, gain_qk = proj_back(
        group_info,
        normed_group,
        w_tri,
        dquery,
        dkv,
        far_cos,
        far_sin,
        tri_gain,
    )
    per = width // (fsdp * ranks)
    part = qkv_grad.reshape(fsdp, ranks, per, 3 * GROUP_WIDTH)
    parts = []
    for b in range(rank_bits):
        part = part.reshape(fsdp, part.shape[1] // 2, 2, per, 3 * GROUP_WIDTH)
        mine = (rank_me >> b) & 1
        got = ds.swap(pick(part, 1 - mine, 2), 1 << b)
        part = (pick(part, mine, 2).astype(F32) + got.astype(F32)).astype(BF16)
        parts.append(part)
    proj_own = [held(piece, parts[0]) for piece in group_swap(proj_pieces)]
    proj_other = ds.swap(jnp.stack([piece[1] for piece in proj_own]), 1)
    part = part[:, 0]
    part_own = pick(part, xs.me)
    part_sent = [pick(part, xs.me ^ s) for s in range(1, fsdp)]
    proj_other = held(proj_other, part_own, ffn_sums, *part_sent)
    in_first, in_rest, grad_text, gain_text = in_back(
        both_info, proj_own, proj_other, w_cols, text_raw, gains, tokens
    )
    part_got = [held(xs.swap(v, s + 1), in_first) for s, v in enumerate(part_sent)]
    part = jnp.stack([part_own] + part_got)
    part = jnp.stack([pick(part, xs.me ^ k) for k in range(fsdp)])
    blocks = jnp.transpose(part.reshape(fsdp, per, 3, GROUP_WIDTH), (2, 0, 1, 3))
    blocks = blocks.reshape(3 * fsdp, per, GROUP_WIDTH)
    in_got = [xs.swap(in_rest[s - 1], s) for s in range(1, fsdp)]
    if groups > 1:
        window = 3 * heads // GROUP_HEADS // groups
        slots = -(-window // groups)
        first_of = lambda target, source: (window * target - source + groups - 1) // groups
        sent = []
        for s in range(groups):
            first = first_of(group_me ^ s, group_me)
            sent.append(
                jnp.stack(
                    [pick(blocks, jnp.clip(first + t, 0, 3 * fsdp - 1)) for t in range(slots)]
                )
            )
        in_got = [held(v, *sent) for v in in_got]
    for v in in_got:
        in_first = in_first + v.astype(F32)
    grad_normed = frame_view(in_first)
    in_unit = frame_sum(grad_normed * unit_in)
    grad_scale_attn = in_unit * gain_attn_in
    grad_gain_attn_in = jnp.sum(in_unit * (1.0 + scale_attn[:, 0]), axis=0)
    grad_input = grad_after + unit_back(
        grad_normed * (gain_attn_in * (1.0 + scale_attn)), unit_in, inv_in
    )
    if groups > 1:
        got = held(jnp.stack(group_swap(sent)), grad_gain_attn_in, grad_scale_attn)
        got = got.reshape(groups * slots, per, GROUP_WIDTH)
        ordered = []
        for k in range(window):
            block = window * group_me + k
            source = block % groups
            slot = block // groups - first_of(group_me, source)
            ordered.append(pick(got, (source ^ group_me) * slots + slot))
        blocks = jnp.stack(ordered)
    columns = jnp.swapaxes(blocks, 0, 1).reshape(per, ranks, 3 * width // dps)
    columns = jnp.swapaxes(columns, 0, 1)
    if ranks <= 4:
        got = jnp.stack(
            [pick(columns, rank_me)]
            + [ds.swap(pick(columns, rank_me ^ m), m) for m in range(1, ranks)]
        )
        got = jnp.stack([pick(got, rank_me ^ r) for r in range(ranks)])
    else:
        got = lax.all_to_all(columns, "dp", 0, 0, tiled=True)
    grad_w_qkv = got.reshape(rows, 3 * width // dps).astype(F32)

    grad_w_gate_up = jnp.stack([ffn_sums[:, :inner], ffn_sums[:, inner : 2 * inner]])
    grad_w_down = jnp.transpose(ffn_sums[:, 2 * inner :])

    out_grad, ffn_sums = beside(out_grad, ffn_sums)
    grad_w_out = jnp.transpose(reduce_rows(out_grad))
    def gather_columns(values, parts):
        wide = values.shape[2] // parts
        cut = values.reshape(fsdp, values.shape[1], parts, wide)[..., :own_width]
        got = [cut]
        for s in range(1, fsdp):
            other = xs.swap(cut, s)
            got.append(jnp.stack([other[s ^ k] for k in range(fsdp)]))
        got = jnp.stack(got)
        whole = jnp.stack([pick(got, xs.me ^ k) for k in range(fsdp)], axis=3)
        return whole.reshape(fsdp * values.shape[1], parts * fsdp * own_width)

    grad_text_all = gather_columns(grad_text, 2)
    text_cols = grad_text_all.shape[1] // dps
    grad_text_cols = jnp.swapaxes(grad_text_all.reshape(fsdp * text_own, dps, text_cols), 0, 1)
    grad_text_cols = lax.all_to_all(grad_text_cols, "dp", 0, 0, tiled=True)
    grad_w_text_kv = mxu(text_every, grad_text_cols.reshape(-1, text_cols), ((0,), (0,)))

    frame_grads = jnp.concatenate(
        [grad_scale_attn, grad_gate_attn, grad_scale_ffn, grad_gate_ffn], axis=1
    )
    clip_grads = jnp.dot(jnp.transpose(onehot), frame_grads, precision=HIGHEST)
    mod_cols = clip_grads.shape[1] // dps
    clip_grads = jnp.swapaxes(clip_grads.reshape(clips, dps, mod_cols), 0, 1)
    clip_grads = jnp.sum(lax.all_to_all(clip_grads, "dp", 0, 0, tiled=True), axis=0)
    clip_rel = jnp.concatenate(xs.gather(clip_grads))
    grad_w_modulate = jnp.dot(jnp.transpose(cond_own.astype(F32)), clip_rel, precision=HIGHEST)
    head_term = jnp.sum(dgate.reshape(GROUP_HEADS, HD), axis=1)
    gate_term = lax.dynamic_update_slice_in_dim(jnp.zeros((heads,), F32), head_term, first_head, 0)
    gate_term = gate_term * (1.0 - tanh_gate * tanh_gate)
    qk_sums = jnp.sum(gain_qk[0].reshape(2, GROUP_HEADS, HD), axis=1)
    small = [
        grad_gain_attn_in,
        grad_gain_attn_out,
        grad_gain_ffn_in,
        grad_gain_ffn_out,
        qk_sums[0],
        qk_sums[1],
        gain_text[0, :HD] + gain_text[0, HD:],
        gate_term,
    ]
    sizes = [v.shape[0] for v in small]
    packed = jnp.concatenate(small)
    packed = jnp.pad(packed, (0, -packed.shape[0] % 1024)).reshape(-1, 128)
    for moves in (ds, xs):
        for b in range(moves.size.bit_length() - 1):
            packed = packed + moves.swap(packed, 1 << b)
    packed = packed.reshape(-1)
    sums = []
    at = 0
    for size in sizes:
        sums.append(packed[at : at + size])
        at += size
    return (
        output.reshape(1, tokens, width),
        grad_input.reshape(1, tokens, width),
        grad_w_modulate,
        grad_w_qkv,
        grad_w_text_kv,
        grad_w_out,
        grad_w_gate_up,
        grad_w_down,
        *sums,
    )


def solution(mesh):
    rows = P("fsdp", "dp", None)
    first = P("fsdp", None)
    split = P("fsdp", "dp")
    return jax.shard_map(
        functools.partial(per_device, mesh.shape["fsdp"], mesh.shape["dp"]),
        mesh=mesh,
        in_specs=(
            rows,
            rows,
            first,
            split,
            P("fsdp", None, None),
            rows,
            first,
            first,
            first,
            first,
            P(None, None, "fsdp"),
            first,
        )
        + (P(),) * 8,
        out_specs=(
            rows,
            rows,
            split,
            split,
            split,
            split,
            P(None, "dp", "fsdp"),
            split,
        )
        + (P(),) * 8,
        check_vma=False,
    )
```
